256 devices in a mesh: rows: 32 (over y, z), protos: 8 (over x, core).
Axes of the slice: x: 4, y: 4, z: 8, core: 2. Of those that a mesh axis runs over, the one named last changes fastest.
Arguments:
- teacher_patches: bfloat16 [128, 256, 256], P('rows'), may hold values from -7 to 7
- student_patches: bfloat16 [128, 256, 256], P('rows'), may hold values from -0.0625 to 0.0625
- mask_order: int32 [128, 256], P('rows'), may hold values from 0 to 255, each once within a row
- teacher_protos: bfloat16 [65536, 256], P('protos'), may hold values from -1 to 1
- student_protos: bfloat16 [65536, 256], P('protos'), may hold values from -0.0234375 to 0.0234375
Outputs:
- grad_student: float32 [128, 128, 256], P('rows')
- grad_protos: float32 [65536, 256], P(('protos', 'rows'))
The draws below stay inside these ranges and needn't reach their ends.
Inputs may be any that keep to these rules, and one draw needn't show every extreme that they name: `mask_order`: each row is an order of the 256 patch positions of its image, each once; its first 128 entries are the masked patches.
All inputs are finite; a program needn't handle non-finite values.
Results may differ from the reference program's by a relative error of at most 0.007.
The reference program's roundings to bfloat16 on the way (of `logit_grad`) count: a program that leaves them out, or rounds other values in their place, can miss the bound.
Values sent between devices are 32-bit elements; how exact they have to be, the bound alone decides.
No kernel may reach another device: no remote copies, remote signals or barrier semaphores. Data moves between devices by JAX's collectives and lax.ppermute only.
A program may use at most 128 MiB of HBM per device.

```python
import jax
import jax.numpy as jnp
from jax import lax

D = 256
K = 65536
PATCHES = 256
MASKED = 128
ITERS = 3
IMAGES = 128


center_count = 16


def shared_centers(key):
    return jnp.clip(jax.random.normal(key, (center_count, D), jnp.float32), -3.0, 3.0)


def rough_noise(key, shape, spread):
    return spread * jnp.clip(jax.random.normal(key, shape, jnp.float32), -4.0, 4.0)


def draw_teacher_patches(key, part):
    centers = shared_centers(key)
    key = jax.random.fold_in(key, 11)
    pick_key, other_key, noise_key = jax.random.split(key, 3)
    first = jax.random.randint(pick_key, (IMAGES, PATCHES), 0, center_count)
    second = jax.random.randint(other_key, (IMAGES, PATCHES), 0, center_count)
    member = jnp.minimum(first, second).astype(jnp.int32)
    base = jnp.take(centers, member, axis=0)
    noise = rough_noise(noise_key, (IMAGES, PATCHES, D), 0.8)
    return (base + noise).astype(jnp.bfloat16)


def draw_teacher_protos(key, part):
    centers = shared_centers(key)
    key = jax.random.fold_in(key, 23)
    pick_key, noise_key = jax.random.split(key, 2)
    member = jax.random.randint(pick_key, (K,), 0, center_count).astype(jnp.int32)
    base = jnp.take(centers, member, axis=0)
    noise = rough_noise(noise_key, (K, D), 0.8)
    return (0.1 * (base + noise)).astype(jnp.bfloat16)


def block_scale(key, dims, cuts, low, top_value):
    level, own = 1.0, jax.random.fold_in(key, 6)
    for axis_at, shards_of in cuts:
        steps = jnp.exp(jax.random.uniform(jax.random.fold_in(own, axis_at), (shards_of,), jnp.float32, low / len(cuts), top_value / len(cuts)))
        level = level * jnp.repeat(steps, dims[axis_at] // shards_of).reshape([-1 if axis == axis_at else 1 for axis in range(len(dims))])
    return level


def gaussian(own_key, extent, scale, limit, cuts=(), dtype=jnp.bfloat16):
    entries = jax.random.normal(own_key, extent, jnp.float32) * scale
    if len(cuts) > 0:
        entries = block_scale(own_key, extent, cuts, -0.22, 0.18) * entries
    return jnp.clip(entries, min=-limit, max=limit).astype(dtype)


def setup_inputs(seed: int = 0) -> dict:
    key_of = jax.random.split(jax.random.key(seed), 6)
    return {
        "teacher_patches": draw_teacher_patches(jax.random.fold_in(key_of[5], 71), 0),
        "student_patches": gaussian(key_of[1], (IMAGES, PATCHES, D), 0.01, 0.0625, ((0, 32),)),
        "mask_order": jax.vmap(lambda own: jax.random.permutation(own, PATCHES))(jax.random.split(key_of[2], IMAGES)).reshape((IMAGES, PATCHES)).astype(jnp.int32),
        "teacher_protos": draw_teacher_protos(jax.random.fold_in(key_of[5], 71), 0),
        "student_protos": gaussian(key_of[4], (K, D), 0.004, 0.0234375, ((0, 8),)),
    }


teacher_temp = 0.07
student_temp = 0.1
epsilon = 1e-06

def unit_rows(values):
    length = jnp.sqrt(lax.optimization_barrier(jnp.sum(values * values, axis=-1, keepdims=True)) + epsilon)
    return (values / length, length)

def reference(teacher_patches, student_patches, mask_order, teacher_protos, student_protos):
    chosen = mask_order[:, :MASKED].astype(jnp.int32)
    teacher_sel = jnp.take_along_axis(teacher_patches, chosen[:, :, None], axis=1).reshape(-1, D).astype(jnp.float32)
    student_sel = jnp.take_along_axis(student_patches, chosen[:, :, None], axis=1).reshape(-1, D).astype(jnp.float32)
    teacher_unit, teacher_length = unit_rows(teacher_sel)
    student_unit, student_length = unit_rows(student_sel)
    teacher_dir, teacher_plen = unit_rows(teacher_protos.astype(jnp.float32))
    student_dir, proto_length = unit_rows(student_protos.astype(jnp.float32))
    teacher_cast = teacher_unit.astype(jnp.bfloat16)
    student_cast = student_unit.astype(jnp.bfloat16)
    teacher_wcast = teacher_dir.astype(jnp.bfloat16)
    student_wcast = student_dir.astype(jnp.bfloat16)
    token_count = teacher_cast.shape[0]
    block_size = min(4096, K)
    block_count = K // block_size
    teacher_blocks = teacher_wcast.reshape(block_count, block_size, D)
    student_blocks = student_wcast.reshape(block_count, block_size, D)

    def energy_of(proto_block):
        return jnp.exp(jnp.dot(teacher_cast, proto_block.T, preferred_element_type=jnp.float32) / teacher_temp)

    def student_of(proto_block):
        return jnp.exp(jnp.dot(student_cast, proto_block.T, preferred_element_type=jnp.float32) / student_temp)
    row_scale = jnp.ones((token_count,), jnp.float32)
    col_scale = None
    for sweep in range(ITERS):

        def visit(accumulated, proto_block):
            energy_block = energy_of(proto_block)
            col_block = 1.0 / lax.optimization_barrier(jnp.sum(energy_block * row_scale[:, None], axis=0))
            accumulated = accumulated + lax.optimization_barrier(jnp.sum(energy_block * col_block[None, :], axis=1))
            return (accumulated, col_block)
        row_total, col_scale = lax.scan(visit, jnp.zeros((token_count,), jnp.float32), teacher_blocks)
        row_scale = 1.0 / row_total

    def norm_visit(accumulated, proto_block):
        return (accumulated + lax.optimization_barrier(jnp.sum(student_of(proto_block), axis=1)), None)
    normalizer, unused = lax.scan(norm_visit, jnp.zeros((token_count,), jnp.float32), student_blocks)

    def grad_visit(accumulated, inputs):
        teacher_block, student_block, col_block = inputs
        targets = energy_of(teacher_block) * row_scale[:, None] * col_block[None, :]
        logit_grad = ((student_of(student_block) / normalizer[:, None] - targets) / student_temp).astype(jnp.bfloat16)
        accumulated = accumulated + jnp.dot(logit_grad, student_block, preferred_element_type=jnp.float32)
        proto_term = lax.dot_general(logit_grad, student_cast, (((0,), (0,)), ((), ())), preferred_element_type=jnp.float32)
        return (accumulated, proto_term)
    feature_grad, proto_terms = lax.scan(grad_visit, jnp.zeros((token_count, D), jnp.float32), (teacher_blocks, student_blocks, col_scale))
    grad_student = (feature_grad - student_unit * lax.optimization_barrier(jnp.sum(student_unit * feature_grad, axis=-1, keepdims=True))) / student_length
    proto_term = proto_terms.reshape(K, D)
    grad_protos = (proto_term - student_dir * lax.optimization_barrier(jnp.sum(student_dir * proto_term, axis=-1, keepdims=True))) / proto_length
    return (grad_student.reshape(-1, MASKED, D), grad_protos)
```

```python
import math

import jax
import jax.numpy as jnp
from jax import lax
from jax.experimental import pallas as pl
from jax.experimental.pallas import tpu as pltpu
from jax.sharding import Mesh, PartitionSpec as P

D = 256
MASKED = 128
ITERS = 3
LANES = 128

teacher_temp = 0.07
student_temp = 0.1
epsilon = 1e-06

teacher_power = math.log2(math.e) / teacher_temp
student_power = math.log2(math.e) / student_temp

ROWS = ("y", "z")
PROTOS = ("x", "core")

f32 = jnp.float32
bf16 = jnp.bfloat16


def params(mib):
    return pltpu.CompilerParams(vmem_limit_bytes=mib * 2**20)


def spread(value, axes):
    return lax.all_to_all(value, axes, 0, 0, tiled=True)


def work(flops, moved, powers=0):
    return pl.CostEstimate(flops=int(flops), bytes_accessed=int(moved), transcendentals=int(powers))


def in_hbm(value):
    return pltpu.with_memory_space_constraint(value, pltpu.HBM)


def nt_dot(a, b):
    return lax.dot_general(a, b, (((1,), (1,)), ((), ())), preferred_element_type=f32)


def unit_rows(values):
    length = jnp.sqrt(jnp.sum(values * values, axis=-1, keepdims=True) + epsilon)
    return (values / length, length)


def directions(values):
    values = values.astype(f32)
    return (values * lax.rsqrt(jnp.sum(values * values, axis=-1, keepdims=True) + epsilon)).astype(bf16)


def to_column(row):
    return jnp.broadcast_to(row, (LANES, LANES)).T


def fill_columns(rows, tile_ref):
    for k in range(rows.shape[0]):
        tile_ref[k * LANES : (k + 1) * LANES, :] = to_column(rows[k : k + 1, :])


def lane_totals(tile):
    parts = [
        jnp.sum(tile[k * LANES : (k + 1) * LANES, :].T, axis=0, keepdims=True)
        for k in range(tile.shape[0] // LANES)
    ]
    return jnp.concatenate(parts, axis=0)


def select_body(place_ref, teacher_ref, student_ref, order_ref, units_ref, length_ref, mine_ref):
    images, patches, _ = teacher_ref.shape
    for image in range(images):
        chosen = order_ref[image : image + 1, :MASKED]
        place = lax.broadcasted_iota(jnp.int32, (patches, MASKED), 0)
        onehot = jnp.where(place == chosen, 1.0, 0.0).astype(bf16)

        def pick(ref):
            return lax.dot_general(
                onehot, ref[image], (((0,), (0,)), ((), ())), preferred_element_type=f32
            )

        rows = slice(image * MASKED, (image + 1) * MASKED)
        teacher = unit_rows(pick(teacher_ref))[0]
        student, length_ref[rows, :] = unit_rows(pick(student_ref))
        units_ref[rows, :D] = teacher
        units_ref[rows, D:] = student
        mine_ref[rows, :] = jnp.where(place_ref[3] == 0, teacher, student)


def select_tokens(place, teacher_patches, student_patches, mask_order):
    tokens = teacher_patches.shape[0] * MASKED
    return pl.pallas_call(
        select_body,
        in_specs=[pl.BlockSpec(memory_space=pltpu.SMEM)]
        + [pl.BlockSpec(memory_space=pltpu.VMEM)] * 3,
        out_specs=[pl.BlockSpec(memory_space=pltpu.VMEM)] * 3,
        out_shape=[
            pltpu.HBM((tokens, 2 * D), f32),
            pltpu.HBM((tokens, 1), f32),
            pltpu.HBM((tokens, D), f32),
        ],
        compiler_params=params(8),
        name="select",
    )(place, in_hbm(teacher_patches), in_hbm(student_patches), in_hbm(mask_order))


def lane_rows(row):
    parts = [row[:, j * LANES : (j + 1) * LANES] for j in range(row.shape[1] // LANES)]
    return jnp.concatenate(parts, axis=0)


def chunks(tokens):
    return [slice(c, c + LANES) for c in range(0, tokens, LANES)]


FETCHES = 8
WIDE = 256


def fetch(protos_ref, buffer_ref, sems, i):
    size = buffer_ref.shape[0] // FETCHES
    rows = pl.ds(pl.multiple_of(i * size, size), size)
    return pltpu.make_async_copy(protos_ref.at[rows, :], buffer_ref.at[rows, :], sems.at[i])


def fetch_all(units_ref, column, unit_ref, protos_ref, buffer_ref, sems):
    units = pltpu.make_async_copy(
        units_ref.at[:, pl.ds(column, D)], unit_ref, sems.at[FETCHES]
    )
    units.start()
    for i in range(FETCHES):
        fetch(protos_ref, buffer_ref, sems, i).start()
    units.wait()


def energy_body(units_ref, protos_ref, energy_ref, sums_ref, unit_ref, cast_ref, buffer_ref, sems):
    size = buffer_ref.shape[0] // FETCHES
    tiles = size // LANES
    fetch_all(units_ref, 0, unit_ref, protos_ref, buffer_ref, sems)
    cast_ref[...] = unit_ref[...].astype(bf16)

    def step(i, carry):
        fetch(protos_ref, buffer_ref, sems, i).wait()
        totals = []

        def logits_of(part):
            rows = pl.ds(pl.multiple_of(i * size + part * WIDE, WIDE), WIDE)
            return nt_dot(cast_ref[...], directions(buffer_ref[rows, :]))

        parts = size // WIDE
        logits = logits_of(0)
        for part in range(parts):
            following = logits_of(part + 1) if part + 1 < parts else None
            energy = jnp.exp2(logits * teacher_power)
            logits = following
            totals.append(lane_rows(jnp.sum(energy, axis=0, keepdims=True)))
            for j in range(WIDE // LANES):
                tile = i * tiles + part * (WIDE // LANES) + j
                energy_ref[tile] = energy[:, j * LANES : (j + 1) * LANES].astype(bf16)
        sums_ref[pl.ds(pl.multiple_of(i * tiles, tiles), tiles), :] = jnp.concatenate(totals, axis=0)
        return carry

    lax.fori_loop(0, FETCHES, step, 0)


def fixed(*shape):
    return pl.BlockSpec(shape, lambda i: (0,) * len(shape))


def left(tokens):
    return pl.BlockSpec((tokens, D), lambda *i: (0, 0))


def right(tokens):
    return pl.BlockSpec((tokens, D), lambda *i: (0, 1))


def energy_of(units, protos):
    tokens, count = units.shape[0], protos.shape[0]
    tiles = count // LANES
    whole = pl.BlockSpec(memory_space=pltpu.VMEM)
    return pl.pallas_call(
        energy_body,
        in_specs=[pl.BlockSpec(memory_space=pl.ANY)] * 2,
        out_specs=[whole] * 2,
        out_shape=[
            pltpu.VMEM((tiles, tokens, LANES), bf16),
            jax.ShapeDtypeStruct((tiles, LANES), f32),
        ],
        scratch_shapes=[
            pltpu.VMEM((tokens, D), f32),
            pltpu.VMEM((tokens, D), bf16),
            pltpu.VMEM((count, D), bf16),
            pltpu.SemaphoreType.DMA((FETCHES + 1,)),
        ],
        compiler_params=params(16),
        cost_estimate=work(4 * tokens * count * D, 8 * 2**20, tokens * count),
        name="energy",
    )(in_hbm(units), in_hbm(protos))


def student_body(units_ref, protos_ref, sums_ref, unit_ref, cast_ref, total_ref, buffer_ref, sems):
    size = buffer_ref.shape[0] // FETCHES
    fetch_all(units_ref, D, unit_ref, protos_ref, buffer_ref, sems)
    cast_ref[...] = unit_ref[...].astype(bf16)
    total_ref[...] = jnp.zeros_like(total_ref)

    def step(i, carry):
        fetch(protos_ref, buffer_ref, sems, i).wait()
        total = total_ref[...]

        def logits_of(part):
            rows = pl.ds(pl.multiple_of(i * size + part * WIDE, WIDE), WIDE)
            return nt_dot(cast_ref[...], directions(buffer_ref[rows, :]))

        parts = size // WIDE
        logits = logits_of(0)
        for part in range(parts):
            following = logits_of(part + 1) if part + 1 < parts else None
            values = jnp.exp2(logits * student_power)
            logits = following
            for j in range(WIDE // LANES):
                total = total + values[:, j * LANES : (j + 1) * LANES]
        total_ref[...] = total
        return carry

    lax.fori_loop(0, FETCHES, step, 0)
    sums_ref[...] = lane_totals(total_ref[...])


def student_sums(units, protos):
    tokens, count = units.shape[0], protos.shape[0]
    return pl.pallas_call(
        student_body,
        in_specs=[pl.BlockSpec(memory_space=pl.ANY)] * 2,
        out_specs=pl.BlockSpec(memory_space=pltpu.VMEM),
        out_shape=jax.ShapeDtypeStruct((tokens // LANES, LANES), f32),
        scratch_shapes=[
            pltpu.VMEM((tokens, D), f32),
            pltpu.VMEM((tokens, D), bf16),
            pltpu.VMEM((tokens, LANES), f32),
            pltpu.VMEM((count, D), bf16),
            pltpu.SemaphoreType.DMA((FETCHES + 1,)),
        ],
        compiler_params=params(16),
        cost_estimate=work(4 * tokens * count * D, 8 * 2**20, tokens * count),
        name="student",
    )(in_hbm(units), in_hbm(protos))


def right(tokens):
    return pl.BlockSpec((tokens, D), lambda *i: (0, 1))


def row_body(energy_ref, pieces_ref, scale_ref, sums_ref):
    tiles, tokens, _ = energy_ref.shape
    scale_ref[...] = 1.0 / jnp.sum(pieces_ref[...], axis=0)
    for k, rows in enumerate(chunks(tokens)):

        def step(j, total):
            return total + energy_ref[j, rows, :].astype(f32) * scale_ref[pl.ds(j, 1), :]

        total = lax.fori_loop(0, tiles, step, jnp.zeros((LANES, LANES), f32), unroll=8)
        totals = lane_totals(total)
        for copy in range(sums_ref.shape[0]):
            sums_ref[copy, k : k + 1, :] = totals


def row_sums(energy, pieces, copies):
    tiles, tokens, _ = energy.shape
    whole = pl.BlockSpec(memory_space=pltpu.VMEM)
    return pl.pallas_call(
        row_body,
        in_specs=[whole] * 2,
        out_specs=[whole] * 2,
        out_shape=[
            jax.ShapeDtypeStruct((tiles, LANES), f32),
            jax.ShapeDtypeStruct((copies, tokens // LANES, LANES), f32),
        ],
        compiler_params=params(12),
        cost_estimate=work(2 * energy.size, 0),
        name="row_sums",
    )(energy, pieces)


def column_body(energy_ref, pieces_ref, sums_ref, tile_ref):
    tiles = energy_ref.shape[0]
    fill_columns(1.0 / jnp.sum(pieces_ref[...], axis=0), tile_ref)

    def step(j, carry):
        total = jnp.sum(energy_ref[j].astype(f32) * tile_ref[...], axis=0, keepdims=True)
        sums_ref[pl.ds(j, 1), :] = total
        return carry

    lax.fori_loop(0, tiles, step, 0, unroll=4)


def column_sums(energy, pieces):
    tiles, tokens, _ = energy.shape
    whole = pl.BlockSpec(memory_space=pltpu.VMEM)
    return pl.pallas_call(
        column_body,
        in_specs=[whole] * 2,
        out_specs=whole,
        out_shape=jax.ShapeDtypeStruct((tiles, LANES), f32),
        scratch_shapes=[pltpu.VMEM((tokens, LANES), f32)],
        compiler_params=params(12),
        cost_estimate=work(2 * energy.size, 0),
        name="column_sums",
    )(energy, pieces)


LEFT_PLACE = [4, 5, 6, 7, 3, 2, 1, 0]
RIGHT_PLACE = [4, 0, 1, 2, 3, 7, 6, 5]


def collect(send, keep, offset):
    n = lax.axis_size("z")
    way = [1 if (z + offset) % 2 else -1 for z in range(n)]
    got = lax.ppermute(send, "z", [(z, (z - way[z]) % n) for z in range(n)])
    return [keep[k] + got[k] for k in range(4)]


def deliver(parts, offset):
    n = lax.axis_size("z")
    way = [1 if (z + offset) % 2 else -1 for z in range(n)]
    return [parts[0]] + [
        lax.ppermute(parts[k], "z", [(z, (z + way[z] * k) % n) for z in range(n)]) for k in (1, 2, 3)
    ]


def cast_body(place_ref, units_ref, *refs):
    *got_refs, out_ref = refs
    tokens = units_ref.shape[0]
    half = len(got_refs) // 2
    out_ref[:tokens, :] = units_ref[...].astype(bf16)
    for core in range(2):

        @pl.when(place_ref[3] == core)
        def _(core=core):
            for i in range(half):
                rows = slice((i + 1) * tokens, (i + 2) * tokens)
                mine, other = slice(core * D, (core + 1) * D), slice((1 - core) * D, (2 - core) * D)
                out_ref[rows, mine] = got_refs[i][...].astype(bf16)
                out_ref[rows, other] = got_refs[half + i][...].astype(bf16)


def cast_units(place, units, got, other):
    tokens, width = units.shape
    whole = pl.BlockSpec(memory_space=pltpu.VMEM)
    return pl.pallas_call(
        cast_body,
        in_specs=[pl.BlockSpec(memory_space=pltpu.SMEM)] + [whole] * (1 + len(got) + len(other)),
        out_specs=whole,
        out_shape=pltpu.HBM((tokens * (1 + len(got)), width), bf16),
        compiler_params=params(12),
        cost_estimate=work(0, 24 * units.size),
        name="cast",
    )(place, in_hbm(units), *got, *other)


def proto_body(
    table_ref,
    units_ref,
    pieces_ref,
    tw_first_ref,
    tw_second_ref,
    sw_first_ref,
    sw_second_ref,
    first_scale_ref,
    second_scale_ref,
    send_left_ref,
    send_right_ref,
    keep_left_ref,
    keep_right_ref,
    r_ref,
    n_ref,
    total_ref,
):
    groups, _, double, _ = pieces_ref.shape
    rows = double // 2
    step = pl.program_id(0)

    @pl.when(step == 0)
    def _():
        for group in range(groups):
            inverse = (1.0 / student_temp) / jnp.sum(pieces_ref[table_ref[3, group]], axis=0)
            for k in range(rows):
                lanes = slice((group * rows + k) * LANES, (group * rows + k + 1) * LANES)
                r_ref[:, lanes] = inverse[k : k + 1, :]
                n_ref[:, lanes] = inverse[rows + k : rows + k + 1, :]

    both = lambda first, second: jnp.concatenate([first, second], axis=0)
    tw = both(directions(tw_first_ref[...]), directions(tw_second_ref[...]))
    sw = both(directions(sw_first_ref[...]), directions(sw_second_ref[...]))
    scale = both(first_scale_ref[0], second_scale_ref[0])
    columns = [to_column(scale[k : k + 1, :]) for k in range(scale.shape[0])]
    col_scale = jnp.concatenate(columns, axis=0)[:, 0:1]

    def logits_of(part):
        return nt_dot(tw, units_ref[part, :D]), nt_dot(sw, units_ref[part, D:])

    parts = [slice(c, c + WIDE) for c in range(0, units_ref.shape[0], WIDE)]
    logits = logits_of(parts[0])
    for i, part in enumerate(parts):
        following = logits_of(parts[i + 1]) if i + 1 < len(parts) else None
        targets = jnp.exp2(logits[0] * teacher_power) * (r_ref[:, part] * col_scale)
        probs = jnp.exp2(logits[1] * student_power) * n_ref[:, part]
        added = jnp.dot(
            (probs - targets).astype(bf16), units_ref[part, D:], preferred_element_type=f32
        )
        total_ref[...] = added if i == 0 else total_ref[...] + added
        logits = following

    block = tw_first_ref.shape[0]
    for which in range(2):
        rows_here = slice(which * block, (which + 1) * block)
        for row, columns_here, sent_ref, kept_ref in (
            (1, slice(0, D // 2), send_left_ref, keep_left_ref),
            (2, slice(D // 2, D), send_right_ref, keep_right_ref),
        ):
            place = table_ref[row, 2 * step + which]

            @pl.when(place < 4)
            def _():
                sent_ref[jnp.minimum(place, 3)] = total_ref[rows_here, columns_here]

            @pl.when(place >= 4)
            def _():
                kept_ref[jnp.maximum(place - 4, 0)] = total_ref[rows_here, columns_here]


def proto_gradient(y, z, units_all, pieces, teacher_protos, student_protos, scale, share):
    tokens = units_all.shape[0]
    block = 256
    blocks = share // block
    way = jnp.where(z % 2 == 1, 1, -1)
    source = y * blocks + (z + way * jnp.arange(blocks) + blocks) % blocks
    owners = (y - jnp.arange(blocks) + blocks) % pieces.shape[0]
    table = jnp.stack([source, jnp.array(LEFT_PLACE), jnp.array(RIGHT_PLACE), owners])
    table = table.astype(jnp.int32)
    whole = lambda *shape: pl.BlockSpec(shape, lambda i, p: (0,) * len(shape))
    first = pl.BlockSpec((block, D), lambda i, p: (p[0, 2 * i], 0))
    second = pl.BlockSpec((block, D), lambda i, p: (p[0, 2 * i + 1], 0))
    direct = pl.BlockSpec(memory_space=pltpu.VMEM)
    scale = scale.reshape(-1, block // LANES, LANES)
    return pl.pallas_call(
        proto_body,
        grid_spec=pltpu.PrefetchScalarGridSpec(
            num_scalar_prefetch=1,
            grid=(blocks // 2,),
            in_specs=[
                whole(tokens, 2 * D),
                whole(*pieces.shape),
                first,
                second,
                first,
                second,
                pl.BlockSpec((1, block // LANES, LANES), lambda i, p: (p[0, 2 * i], 0, 0)),
                pl.BlockSpec((1, block // LANES, LANES), lambda i, p: (p[0, 2 * i + 1], 0, 0)),
            ],
            out_specs=[direct] * 4,
            scratch_shapes=[
                pltpu.VMEM((1, tokens), f32),
                pltpu.VMEM((1, tokens), f32),
                pltpu.VMEM((2 * block, D), f32),
            ],
        ),
        out_shape=[pltpu.VMEM((blocks // 2, block, D // 2), f32)] * 4,
        compiler_params=params(24),
        cost_estimate=work(8 * tokens * share * D, 8 * 2**20, 2 * tokens * share),
        name="proto_gradient",
    )(
        table,
        in_hbm(units_all),
        pieces,
        in_hbm(teacher_protos),
        in_hbm(teacher_protos),
        in_hbm(student_protos),
        in_hbm(student_protos),
        scale,
        scale,
    )


def feature_body(
    place_ref, energy_ref, student_ref, pieces_ref, sw_ref, scale_ref, out_ref, s_ref, r_ref, n_ref, total_ref
):
    step = pl.program_id(0)

    @pl.when(step == 0)
    def _():
        s_ref[...] = student_ref[...].astype(bf16)
        inverse = (1.0 / student_temp) / jnp.sum(pieces_ref[0], axis=0)
        rows = inverse.shape[0] // 2
        fill_columns(inverse[:rows], r_ref)
        fill_columns(inverse[rows:], n_ref)
        total_ref[...] = jnp.zeros_like(total_ref)

    weights = directions(sw_ref[...])
    part_of = lambda part: weights[part * WIDE : (part + 1) * WIDE, :]
    parts = weights.shape[0] // WIDE
    logits = nt_dot(s_ref[...], part_of(0))
    grads = []
    for part in range(parts):
        following = nt_dot(s_ref[...], part_of(part + 1)) if part + 1 < parts else None
        for j in range(WIDE // LANES):
            tile = part * (WIDE // LANES) + j
            probs = jnp.exp2(logits[:, j * LANES : (j + 1) * LANES] * student_power) * n_ref[...]
            targets = energy_ref[tile].astype(f32) * r_ref[...] * scale_ref[tile : tile + 1, :]
            grads.append((probs - targets).astype(bf16))
        logits = following
    logit_grad = jnp.concatenate(grads, axis=1)
    total_ref[...] += jnp.dot(logit_grad, weights, preferred_element_type=f32)

    @pl.when(step == pl.num_programs(0) - 1)
    def _():
        out_ref[...] = total_ref[...].reshape(out_ref.shape)


def feature_gradient(place, energy, units, pieces, protos, scale, copies):
    tiles, tokens, _ = energy.shape
    block = 1024
    steps = block // LANES
    whole = lambda *shape: pl.BlockSpec(shape, lambda i, p: (0,) * len(shape))
    return pl.pallas_call(
        feature_body,
        grid_spec=pltpu.PrefetchScalarGridSpec(
            num_scalar_prefetch=1,
            grid=(tiles // steps,),
            in_specs=[
                pl.BlockSpec((steps, tokens, LANES), lambda i, p: (i, 0, 0)),
                right(tokens),
                pl.BlockSpec((1,) + pieces.shape[1:], lambda i, p: (p[0], 0, 0, 0)),
                pl.BlockSpec((block, D), lambda i, p: (i, 0)),
                pl.BlockSpec((steps, LANES), lambda i, p: (i, 0)),
            ],
            out_specs=whole(copies, tokens // copies, D),
            scratch_shapes=[
                pltpu.VMEM((tokens, D), bf16),
                pltpu.VMEM((tokens, LANES), f32),
                pltpu.VMEM((tokens, LANES), f32),
                pltpu.VMEM((tokens, D), f32),
            ],
        ),
        out_shape=jax.ShapeDtypeStruct((copies, tokens // copies, D), f32),
        compiler_params=params(32),
        cost_estimate=work(8 * energy.size * D, 16 * 2**20, energy.size),
        name="feature_gradient",
    )(place, in_hbm(energy), in_hbm(units), pieces, in_hbm(protos), scale)


def project(total, unit, length):
    return (total - unit * jnp.sum(unit * total, axis=-1, keepdims=True)) / length


def student_end_body(place_ref, pieces_ref, unit_ref, length_ref, out_ref):
    result = project(jnp.sum(pieces_ref[...], axis=0), unit_ref[...], length_ref[...])
    for copy in range(out_ref.shape[0]):
        out_ref[copy] = result


def student_end(place, pieces, units, length):
    copies, rows, _ = pieces.shape
    return pl.pallas_call(
        student_end_body,
        grid_spec=pltpu.PrefetchScalarGridSpec(
            num_scalar_prefetch=1,
            grid=(1,),
            in_specs=[
                pl.BlockSpec(pieces.shape, lambda i, p: (0, 0, 0)),
                pl.BlockSpec((rows, D), lambda i, p: (p[2], 1)),
                pl.BlockSpec((rows, 1), lambda i, p: (p[2], 0)),
            ],
            out_specs=pl.BlockSpec(pieces.shape, lambda i, p: (0, 0, 0)),
        ),
        out_shape=jax.ShapeDtypeStruct(pieces.shape, f32),
        compiler_params=params(8),
        name="student_end",
    )(place, pieces, in_hbm(units), in_hbm(length))


def proto_end_body(place_ref, *refs):
    piece_refs, (protos_ref, out_ref) = refs[:-2], refs[-2:]
    unit, length = unit_rows(protos_ref[...].astype(f32))
    half = len(piece_refs) // 2
    sums = []
    for group in (piece_refs[:half], piece_refs[half:]):
        total = group[0][...]
        for ref in group[1:]:
            total = total + ref[...]
        sums.append(total)
    out_ref[...] = project(jnp.concatenate(sums, axis=1), unit, length)


def proto_end(place, pieces, protos):
    rows, width = pieces[0].shape
    return pl.pallas_call(
        proto_end_body,
        grid_spec=pltpu.PrefetchScalarGridSpec(
            num_scalar_prefetch=1,
            grid=(1,),
            in_specs=[pl.BlockSpec((rows, width), lambda i, p: (0, 0))] * len(pieces)
            + [pl.BlockSpec((rows, D), lambda i, p: (p[1], 0))],
            out_specs=pl.BlockSpec((rows, D), lambda i, p: (0, 0)),
        ),
        out_shape=jax.ShapeDtypeStruct((rows, D), f32),
        compiler_params=params(8),
        name="proto_end",
    )(place, *pieces, in_hbm(protos))


def direct_sum(value, axis):
    n = lax.axis_size(axis)
    total = value
    for step in range(1, n):
        total = total + lax.ppermute(value, axis, [(i, (i + step) % n) for i in range(n)])
    return total


def on_device(teacher_patches, student_patches, mask_order, teacher_protos, student_protos):
    y_size, z_size = lax.axis_size("y"), lax.axis_size("z")
    proto_size = lax.axis_size("x") * lax.axis_size("core")
    y, z = lax.axis_index("y"), lax.axis_index("z")
    core = lax.axis_index("core")
    place = jnp.stack([y, y * z_size + z, lax.axis_index(PROTOS), core]).astype(jnp.int32)

    units, student_length, mine = select_tokens(
        place, teacher_patches, student_patches, mask_order
    )
    from_y = lambda value, step: lax.ppermute(
        value, "y", [(i, (i + step) % y_size) for i in range(y_size)]
    )
    from_core = lambda value: lax.ppermute(value, "core", [(0, 1), (1, 0)])

    energy, sums = energy_of(units, teacher_protos)
    norm_part = student_sums(units, student_protos)
    for sweep in range(ITERS):
        last = sweep == ITERS - 1
        if sweep > 0:
            sums = column_sums(energy, pieces)
        sums = direct_sum(sums, "y")
        if sweep == 0:
            sums, mine = lax.optimization_barrier((sums, mine))
            got_first, got_third = from_y(mine, 1), from_y(mine, 3)
        elif sweep == 1:
            sums, mine, got_first, got_third = lax.optimization_barrier(
                (sums, mine, got_first, got_third)
            )
            got_second = from_y(mine, 2)
            other_first, other_third = from_core(got_first), from_core(got_third)
        else:
            sums, got_second = lax.optimization_barrier((sums, got_second))
            other_second = from_core(got_second)
        sums = spread(jnp.broadcast_to(sums, (z_size,) + sums.shape), "z")
        col_scale, row_part = row_sums(energy, sums, 1 if last else proto_size)
        if not last:
            pieces = spread(row_part, PROTOS)
        if sweep == 0:
            pieces, got_first, got_third = lax.optimization_barrier((pieces, got_first, got_third))
        elif sweep == 1:
            pieces, got_second, other_first, other_third = lax.optimization_barrier(
                (pieces, got_second, other_first, other_third)
            )
    row_part, other_second = lax.optimization_barrier((row_part, other_second))
    units_cast = cast_units(
        place, units, [got_first, got_second, got_third], [other_first, other_second, other_third]
    )
    both = jnp.concatenate([row_part[0], norm_part], axis=0)
    peers = y_size * proto_size
    both = jnp.broadcast_to(both, (peers,) + both.shape)
    pieces = spread(both, ("y",) + PROTOS).reshape((y_size, proto_size) + both.shape[1:])

    share = teacher_protos.shape[0] // y_size
    send_left, send_right, keep_left, keep_right = proto_gradient(
        y, z, units_cast, pieces, teacher_protos, student_protos, col_scale, share
    )
    keep_left, col_scale = lax.optimization_barrier((keep_left, col_scale))
    left = collect(send_left, keep_left, 0)
    right_half = collect(send_right, keep_right, 1)
    feature_part = feature_gradient(
        place, energy, units, pieces, student_protos, col_scale, proto_size
    )
    feature_part, left, right_half = lax.optimization_barrier((feature_part, left, right_half))
    left, right_half = deliver(left, 0), deliver(right_half, 1)
    feature_pieces = spread(feature_part, PROTOS)
    feature_pieces, left, right_half = lax.optimization_barrier((feature_pieces, left, right_half))
    result = spread(student_end(place, feature_pieces, units, student_length), PROTOS)
    grad_protos = proto_end(place, left + right_half, student_protos)
    return (result.reshape(-1, MASKED, D), grad_protos)


def solution(mesh):
    fine = Mesh(mesh.devices.reshape(4, 8, 4, 2), ("y", "z", "x", "core"))
    return jax.shard_map(
        on_device,
        mesh=fine,
        in_specs=(
            P(ROWS, None, None),
            P(ROWS, None, None),
            P(ROWS, None),
            P(PROTOS, None),
            P(PROTOS, None),
        ),
        out_specs=(P(ROWS, None, None), P(PROTOS + ROWS, None)),
        check_vma=False,
    )
```

```python
import math

import jax
import jax.numpy as jnp
from jax import lax
from jax.experimental import pallas as pl
from jax.experimental.pallas import tpu as pltpu
from jax.sharding import Mesh, PartitionSpec as P

D = 256
MASKED = 128
ITERS = 3
LANES = 128

teacher_temp = 0.07
student_temp = 0.1
epsilon = 1e-06

teacher_power = math.log2(math.e) / teacher_temp
student_power = math.log2(math.e) / student_temp

ROWS = ("y", "z")
PROTOS = ("x", "core")

f32 = jnp.float32
bf16 = jnp.bfloat16


def params(mib):
    return pltpu.CompilerParams(vmem_limit_bytes=mib * 2**20)


def spread(value, axes):
    return lax.all_to_all(value, axes, 0, 0, tiled=True)


def work(flops, moved, powers=0):
    return pl.CostEstimate(flops=int(flops), bytes_accessed=int(moved), transcendentals=int(powers))


def in_hbm(value):
    return pltpu.with_memory_space_constraint(value, pltpu.HBM)


def nt_dot(a, b):
    return lax.dot_general(a, b, (((1,), (1,)), ((), ())), preferred_element_type=f32)


def unit_rows(values):
    length = jnp.sqrt(jnp.sum(values * values, axis=-1, keepdims=True) + epsilon)
    return (values / length, length)


def directions(values):
    values = values.astype(f32)
    return (values * lax.rsqrt(jnp.sum(values * values, axis=-1, keepdims=True) + epsilon)).astype(bf16)


def to_column(row):
    return jnp.broadcast_to(row, (LANES, LANES)).T


def fill_columns(rows, tile_ref):
    for k in range(rows.shape[0]):
        tile_ref[k * LANES : (k + 1) * LANES, :] = to_column(rows[k : k + 1, :])


def lane_totals(tile):
    parts = [
        jnp.sum(tile[k * LANES : (k + 1) * LANES, :].T, axis=0, keepdims=True)
        for k in range(tile.shape[0] // LANES)
    ]
    return jnp.concatenate(parts, axis=0)


def select_body(place_ref, teacher_ref, student_ref, order_ref, units_ref, length_ref, mine_ref):
    images, patches, _ = teacher_ref.shape
    for image in range(images):
        chosen = order_ref[image : image + 1, :MASKED]
        place = lax.broadcasted_iota(jnp.int32, (patches, MASKED), 0)
        onehot = jnp.where(place == chosen, 1.0, 0.0).astype(bf16)

        def pick(ref):
            return lax.dot_general(
                onehot, ref[image], (((0,), (0,)), ((), ())), preferred_element_type=f32
            )

        rows = slice(image * MASKED, (image + 1) * MASKED)
        teacher = unit_rows(pick(teacher_ref))[0]
        student, length_ref[rows, :] = unit_rows(pick(student_ref))
        units_ref[rows, :D] = teacher
        units_ref[rows, D:] = student
        mine_ref[rows, :] = jnp.where(place_ref[3] == 0, teacher, student)


def select_tokens(place, teacher_patches, student_patches, mask_order):
    tokens = teacher_patches.shape[0] * MASKED
    return pl.pallas_call(
        select_body,
        in_specs=[pl.BlockSpec(memory_space=pltpu.SMEM)]
        + [pl.BlockSpec(memory_space=pltpu.VMEM)] * 3,
        out_specs=[pl.BlockSpec(memory_space=pltpu.VMEM)] * 3,
        out_shape=[
            pltpu.HBM((tokens, 2 * D), f32),
            pltpu.HBM((tokens, 1), f32),
            pltpu.HBM((tokens, D), f32),
        ],
        compiler_params=params(8),
        name="select",
    )(place, in_hbm(teacher_patches), in_hbm(student_patches), in_hbm(mask_order))


def lane_rows(row):
    parts = [row[:, j * LANES : (j + 1) * LANES] for j in range(row.shape[1] // LANES)]
    return jnp.concatenate(parts, axis=0)


def chunks(tokens):
    return [slice(c, c + LANES) for c in range(0, tokens, LANES)]


FETCHES = 8
WIDE = 256


def fetch(protos_ref, buffer_ref, sems, i):
    size = buffer_ref.shape[0] // FETCHES
    rows = pl.ds(pl.multiple_of(i * size, size), size)
    return pltpu.make_async_copy(protos_ref.at[rows, :], buffer_ref.at[rows, :], sems.at[i])


def fetch_all(units_ref, column, unit_ref, protos_ref, buffer_ref, sems):
    units = pltpu.make_async_copy(
        units_ref.at[:, pl.ds(column, D)], unit_ref, sems.at[FETCHES]
    )
    units.start()
    for i in range(FETCHES):
        fetch(protos_ref, buffer_ref, sems, i).start()
    units.wait()


def energy_body(units_ref, protos_ref, energy_ref, sums_ref, unit_ref, cast_ref, buffer_ref, sems):
    size = buffer_ref.shape[0] // FETCHES
    tiles = size // LANES
    fetch_all(units_ref, 0, unit_ref, protos_ref, buffer_ref, sems)
    cast_ref[...] = unit_ref[...].astype(bf16)

    def step(i, carry):
        fetch(protos_ref, buffer_ref, sems, i).wait()
        totals = []

        def logits_of(part):
            rows = pl.ds(pl.multiple_of(i * size + part * WIDE, WIDE), WIDE)
            return nt_dot(cast_ref[...], directions(buffer_ref[rows, :]))

        parts = size // WIDE
        logits = logits_of(0)
        for part in range(parts):
            following = logits_of(part + 1) if part + 1 < parts else None
            energy = jnp.exp2(logits * teacher_power)
            logits = following
            totals.append(lane_rows(jnp.sum(energy, axis=0, keepdims=True)))
            for j in range(WIDE // LANES):
                tile = i * tiles + part * (WIDE // LANES) + j
                energy_ref[tile] = energy[:, j * LANES : (j + 1) * LANES].astype(bf16)
        sums_ref[pl.ds(pl.multiple_of(i * tiles, tiles), tiles), :] = jnp.concatenate(totals, axis=0)
        return carry

    lax.fori_loop(0, FETCHES, step, 0)


def fixed(*shape):
    return pl.BlockSpec(shape, lambda i: (0,) * len(shape))


def left(tokens):
    return pl.BlockSpec((tokens, D), lambda *i: (0, 0))


def right(tokens):
    return pl.BlockSpec((tokens, D), lambda *i: (0, 1))


def energy_of(units, protos):
    tokens, count = units.shape[0], protos.shape[0]
    tiles = count // LANES
    whole = pl.BlockSpec(memory_space=pltpu.VMEM)
    return pl.pallas_call(
        energy_body,
        in_specs=[pl.BlockSpec(memory_space=pl.ANY)] * 2,
        out_specs=[whole] * 2,
        out_shape=[
            pltpu.VMEM((tiles, tokens, LANES), bf16),
            jax.ShapeDtypeStruct((tiles, LANES), f32),
        ],
        scratch_shapes=[
            pltpu.VMEM((tokens, D), f32),
            pltpu.VMEM((tokens, D), bf16),
            pltpu.VMEM((count, D), bf16),
            pltpu.SemaphoreType.DMA((FETCHES + 1,)),
        ],
        compiler_params=params(16),
        cost_estimate=work(4 * tokens * count * D, 8 * 2**20, tokens * count),
        name="energy",
    )(in_hbm(units), in_hbm(protos))


def student_body(units_ref, protos_ref, sums_ref, unit_ref, cast_ref, total_ref, buffer_ref, sems):
    size = buffer_ref.shape[0] // FETCHES
    fetch_all(units_ref, D, unit_ref, protos_ref, buffer_ref, sems)
    cast_ref[...] = unit_ref[...].astype(bf16)
    total_ref[...] = jnp.zeros_like(total_ref)

    def step(i, carry):
        fetch(protos_ref, buffer_ref, sems, i).wait()
        total = total_ref[...]

        def logits_of(part):
            rows = pl.ds(pl.multiple_of(i * size + part * WIDE, WIDE), WIDE)
            return nt_dot(cast_ref[...], directions(buffer_ref[rows, :]))

        parts = size // WIDE
        logits = logits_of(0)
        for part in range(parts):
            following = logits_of(part + 1) if part + 1 < parts else None
            values = jnp.exp2(logits * student_power)
            logits = following
            for j in range(WIDE // LANES):
                total = total + values[:, j * LANES : (j + 1) * LANES]
        total_ref[...] = total
        return carry

    lax.fori_loop(0, FETCHES, step, 0)
    sums_ref[...] = lane_totals(total_ref[...])


def student_sums(units, protos):
    tokens, count = units.shape[0], protos.shape[0]
    return pl.pallas_call(
        student_body,
        in_specs=[pl.BlockSpec(memory_space=pl.ANY)] * 2,
        out_specs=pl.BlockSpec(memory_space=pltpu.VMEM),
        out_shape=jax.ShapeDtypeStruct((tokens // LANES, LANES), f32),
        scratch_shapes=[
            pltpu.VMEM((tokens, D), f32),
            pltpu.VMEM((tokens, D), bf16),
            pltpu.VMEM((tokens, LANES), f32),
            pltpu.VMEM((count, D), bf16),
            pltpu.SemaphoreType.DMA((FETCHES + 1,)),
        ],
        compiler_params=params(16),
        cost_estimate=work(4 * tokens * count * D, 8 * 2**20, tokens * count),
        name="student",
    )(in_hbm(units), in_hbm(protos))


def right(tokens):
    return pl.BlockSpec((tokens, D), lambda *i: (0, 1))


def row_body(energy_ref, pieces_ref, scale_ref, sums_ref):
    tiles, tokens, _ = energy_ref.shape
    scale_ref[...] = 1.0 / jnp.sum(pieces_ref[...], axis=0)
    for k, rows in enumerate(chunks(tokens)):

        def step(j, total):
            return total + energy_ref[j, rows, :].astype(f32) * scale_ref[pl.ds(j, 1), :]

        total = lax.fori_loop(0, tiles, step, jnp.zeros((LANES, LANES), f32), unroll=8)
        totals = lane_totals(total)
        for copy in range(sums_ref.shape[0]):
            sums_ref[copy, k : k + 1, :] = totals


def row_sums(energy, pieces, copies):
    tiles, tokens, _ = energy.shape
    whole = pl.BlockSpec(memory_space=pltpu.VMEM)
    return pl.pallas_call(
        row_body,
        in_specs=[whole] * 2,
        out_specs=[whole] * 2,
        out_shape=[
            jax.ShapeDtypeStruct((tiles, LANES), f32),
            jax.ShapeDtypeStruct((copies, tokens // LANES, LANES), f32),
        ],
        compiler_params=params(12),
        cost_estimate=work(2 * energy.size, 0),
        name="row_sums",
    )(energy, pieces)


def column_body(energy_ref, pieces_ref, sums_ref, tile_ref):
    tiles = energy_ref.shape[0]
    fill_columns(1.0 / jnp.sum(pieces_ref[...], axis=0), tile_ref)

    def step(j, carry):
        total = jnp.sum(energy_ref[j].astype(f32) * tile_ref[...], axis=0, keepdims=True)
        sums_ref[pl.ds(j, 1), :] = total
        return carry

    lax.fori_loop(0, tiles, step, 0, unroll=4)


def column_sums(energy, pieces):
    tiles, tokens, _ = energy.shape
    whole = pl.BlockSpec(memory_space=pltpu.VMEM)
    return pl.pallas_call(
        column_body,
        in_specs=[whole] * 2,
        out_specs=whole,
        out_shape=jax.ShapeDtypeStruct((tiles, LANES), f32),
        scratch_shapes=[pltpu.VMEM((tokens, LANES), f32)],
        compiler_params=params(12),
        cost_estimate=work(2 * energy.size, 0),
        name="column_sums",
    )(energy, pieces)


LEFT_PLACE = [4, 5, 6, 7, 3, 2, 1, 0]
RIGHT_PLACE = [4, 0, 1, 2, 3, 7, 6, 5]


def collect(send, keep, offset):
    n = lax.axis_size("z")
    way = [1 if (z + offset) % 2 else -1 for z in range(n)]
    got = lax.ppermute(send, "z", [(z, (z - way[z]) % n) for z in range(n)])
    return keep[0] + got[0], keep[1] + got[1], keep[2:] + got[2:]


def pass_on(sums, offset):
    n = lax.axis_size("z")
    way = [1 if (z + offset) % 2 else -1 for z in range(n)]
    own, following, far = sums
    got = lax.ppermute(far, "z", [(z, (z + 2 * way[z]) % n) for z in range(n)])
    return own + got[0], following + got[1]


def deliver(sums, offset):
    n = lax.axis_size("z")
    way = [1 if (z + offset) % 2 else -1 for z in range(n)]
    own, following = sums
    return [own, lax.ppermute(following, "z", [(z, (z + way[z]) % n) for z in range(n)])]


def cast_body(place_ref, units_ref, *refs):
    *got_refs, out_ref = refs
    tokens = units_ref.shape[0]
    half = len(got_refs) // 2
    out_ref[:tokens, :] = units_ref[...].astype(bf16)
    for core in range(2):

        @pl.when(place_ref[3] == core)
        def _(core=core):
            for i in range(half):
                rows = slice((i + 1) * tokens, (i + 2) * tokens)
                mine, other = slice(core * D, (core + 1) * D), slice((1 - core) * D, (2 - core) * D)
                out_ref[rows, mine] = got_refs[i][...].astype(bf16)
                out_ref[rows, other] = got_refs[half + i][...].astype(bf16)


def cast_units(place, units, got, other):
    tokens, width = units.shape
    whole = pl.BlockSpec(memory_space=pltpu.VMEM)
    return pl.pallas_call(
        cast_body,
        in_specs=[pl.BlockSpec(memory_space=pltpu.SMEM)] + [whole] * (1 + len(got) + len(other)),
        out_specs=whole,
        out_shape=pltpu.HBM((tokens * (1 + len(got)), width), bf16),
        compiler_params=params(12),
        cost_estimate=work(0, 24 * units.size),
        name="cast",
    )(place, in_hbm(units), *got, *other)


def proto_body(
    table_ref,
    units_ref,
    pieces_ref,
    tw_first_ref,
    tw_second_ref,
    sw_first_ref,
    sw_second_ref,
    first_scale_ref,
    second_scale_ref,
    send_left_ref,
    send_right_ref,
    keep_left_ref,
    keep_right_ref,
    r_ref,
    n_ref,
    total_ref,
):
    groups, _, double, _ = pieces_ref.shape
    rows = double // 2
    step = pl.program_id(0)

    @pl.when(step == 0)
    def _():
        for group in range(groups):
            inverse = (1.0 / student_temp) / jnp.sum(pieces_ref[table_ref[3, group]], axis=0)
            for k in range(rows):
                lanes = slice((group * rows + k) * LANES, (group * rows + k + 1) * LANES)
                r_ref[:, lanes] = inverse[k : k + 1, :]
                n_ref[:, lanes] = inverse[rows + k : rows + k + 1, :]

    both = lambda first, second: jnp.concatenate([first, second], axis=0)
    tw = both(directions(tw_first_ref[...]), directions(tw_second_ref[...]))
    sw = both(directions(sw_first_ref[...]), directions(sw_second_ref[...]))
    scale = both(first_scale_ref[0], second_scale_ref[0])
    columns = [to_column(scale[k : k + 1, :]) for k in range(scale.shape[0])]
    col_scale = jnp.concatenate(columns, axis=0)[:, 0:1]

    def logits_of(part):
        return nt_dot(tw, units_ref[part, :D]), nt_dot(sw, units_ref[part, D:])

    parts = [slice(c, c + WIDE) for c in range(0, units_ref.shape[0], WIDE)]
    logits = logits_of(parts[0])
    for i, part in enumerate(parts):
        following = logits_of(parts[i + 1]) if i + 1 < len(parts) else None
        targets = jnp.exp2(logits[0] * teacher_power) * (r_ref[:, part] * col_scale)
        probs = jnp.exp2(logits[1] * student_power) * n_ref[:, part]
        added = jnp.dot(
            (probs - targets).astype(bf16), units_ref[part, D:], preferred_element_type=f32
        )
        total_ref[...] = added if i == 0 else total_ref[...] + added
        logits = following

    block = tw_first_ref.shape[0]
    for which in range(2):
        rows_here = slice(which * block, (which + 1) * block)
        for row, columns_here, sent_ref, kept_ref in (
            (1, slice(0, D // 2), send_left_ref, keep_left_ref),
            (2, slice(D // 2, D), send_right_ref, keep_right_ref),
        ):
            place = table_ref[row, 2 * step + which]

            @pl.when(place < 4)
            def _():
                sent_ref[jnp.minimum(place, 3)] = total_ref[rows_here, columns_here]

            @pl.when(place >= 4)
            def _():
                kept_ref[jnp.maximum(place - 4, 0)] = total_ref[rows_here, columns_here]


def proto_gradient(y, z, units_all, pieces, teacher_protos, student_protos, scale, share):
    tokens = units_all.shape[0]
    block = 256
    blocks = share // block
    way = jnp.where(z % 2 == 1, 1, -1)
    source = y * blocks + (z + way * jnp.arange(blocks) + blocks) % blocks
    owners = (y - jnp.arange(blocks) + blocks) % pieces.shape[0]
    table = jnp.stack([source, jnp.array(LEFT_PLACE), jnp.array(RIGHT_PLACE), owners])
    table = table.astype(jnp.int32)
    whole = lambda *shape: pl.BlockSpec(shape, lambda i, p: (0,) * len(shape))
    first = pl.BlockSpec((block, D), lambda i, p: (p[0, 2 * i], 0))
    second = pl.BlockSpec((block, D), lambda i, p: (p[0, 2 * i + 1], 0))
    direct = pl.BlockSpec(memory_space=pltpu.VMEM)
    scale = scale.reshape(-1, block // LANES, LANES)
    return pl.pallas_call(
        proto_body,
        grid_spec=pltpu.PrefetchScalarGridSpec(
            num_scalar_prefetch=1,
            grid=(blocks // 2,),
            in_specs=[
                whole(tokens, 2 * D),
                whole(*pieces.shape),
                first,
                second,
                first,
                second,
                pl.BlockSpec((1, block // LANES, LANES), lambda i, p: (p[0, 2 * i], 0, 0)),
                pl.BlockSpec((1, block // LANES, LANES), lambda i, p: (p[0, 2 * i + 1], 0, 0)),
            ],
            out_specs=[direct] * 4,
            scratch_shapes=[
                pltpu.VMEM((1, tokens), f32),
                pltpu.VMEM((1, tokens), f32),
                pltpu.VMEM((2 * block, D), f32),
            ],
        ),
        out_shape=[pltpu.VMEM((blocks // 2, block, D // 2), f32)] * 4,
        compiler_params=params(24),
        cost_estimate=work(8 * tokens * share * D, 8 * 2**20, 2 * tokens * share),
        name="proto_gradient",
    )(
        table,
        in_hbm(units_all),
        pieces,
        in_hbm(teacher_protos),
        in_hbm(teacher_protos),
        in_hbm(student_protos),
        in_hbm(student_protos),
        scale,
        scale,
    )


def feature_body(
    place_ref, energy_ref, student_ref, pieces_ref, sw_ref, scale_ref, out_ref, s_ref, r_ref, n_ref, total_ref
):
    step = pl.program_id(0)

    @pl.when(step == 0)
    def _():
        s_ref[...] = student_ref[...].astype(bf16)
        inverse = (1.0 / student_temp) / jnp.sum(pieces_ref[0], axis=0)
        rows = inverse.shape[0] // 2
        fill_columns(inverse[:rows], r_ref)
        fill_columns(inverse[rows:], n_ref)
        total_ref[...] = jnp.zeros_like(total_ref)

    weights = directions(sw_ref[...])
    part_of = lambda part: weights[part * WIDE : (part + 1) * WIDE, :]
    parts = weights.shape[0] // WIDE
    logits = nt_dot(s_ref[...], part_of(0))
    grads = []
    for part in range(parts):
        following = nt_dot(s_ref[...], part_of(part + 1)) if part + 1 < parts else None
        for j in range(WIDE // LANES):
            tile = part * (WIDE // LANES) + j
            probs = jnp.exp2(logits[:, j * LANES : (j + 1) * LANES] * student_power) * n_ref[...]
            targets = energy_ref[tile].astype(f32) * r_ref[...] * scale_ref[tile : tile + 1, :]
            grads.append((probs - targets).astype(bf16))
        logits = following
    logit_grad = jnp.concatenate(grads, axis=1)
    total_ref[...] += jnp.dot(logit_grad, weights, preferred_element_type=f32)

    @pl.when(step == pl.num_programs(0) - 1)
    def _():
        out_ref[...] = total_ref[...].reshape(out_ref.shape)


def feature_gradient(place, energy, units, pieces, protos, scale, copies):
    tiles, tokens, _ = energy.shape
    block = 1024
    steps = block // LANES
    whole = lambda *shape: pl.BlockSpec(shape, lambda i, p: (0,) * len(shape))
    return pl.pallas_call(
        feature_body,
        grid_spec=pltpu.PrefetchScalarGridSpec(
            num_scalar_prefetch=1,
            grid=(tiles // steps,),
            in_specs=[
                pl.BlockSpec((steps, tokens, LANES), lambda i, p: (i, 0, 0)),
                right(tokens),
                pl.BlockSpec((1,) + pieces.shape[1:], lambda i, p: (p[0], 0, 0, 0)),
                pl.BlockSpec((block, D), lambda i, p: (i, 0)),
                pl.BlockSpec((steps, LANES), lambda i, p: (i, 0)),
            ],
            out_specs=whole(copies, tokens // copies, D),
            scratch_shapes=[
                pltpu.VMEM((tokens, D), bf16),
                pltpu.VMEM((tokens, LANES), f32),
                pltpu.VMEM((tokens, LANES), f32),
                pltpu.VMEM((tokens, D), f32),
            ],
        ),
        out_shape=jax.ShapeDtypeStruct((copies, tokens // copies, D), f32),
        compiler_params=params(32),
        cost_estimate=work(8 * energy.size * D, 16 * 2**20, energy.size),
        name="feature_gradient",
    )(place, in_hbm(energy), in_hbm(units), pieces, in_hbm(protos), scale)


def project(total, unit, length):
    return (total - unit * jnp.sum(unit * total, axis=-1, keepdims=True)) / length


def student_end_body(place_ref, pieces_ref, unit_ref, length_ref, out_ref):
    result = project(jnp.sum(pieces_ref[...], axis=0), unit_ref[...], length_ref[...])
    for copy in range(out_ref.shape[0]):
        out_ref[copy] = result


def student_end(place, pieces, units, length):
    copies, rows, _ = pieces.shape
    return pl.pallas_call(
        student_end_body,
        grid_spec=pltpu.PrefetchScalarGridSpec(
            num_scalar_prefetch=1,
            grid=(1,),
            in_specs=[
                pl.BlockSpec(pieces.shape, lambda i, p: (0, 0, 0)),
                pl.BlockSpec((rows, D), lambda i, p: (p[2], 1)),
                pl.BlockSpec((rows, 1), lambda i, p: (p[2], 0)),
            ],
            out_specs=pl.BlockSpec(pieces.shape, lambda i, p: (0, 0, 0)),
        ),
        out_shape=jax.ShapeDtypeStruct(pieces.shape, f32),
        compiler_params=params(8),
        name="student_end",
    )(place, pieces, in_hbm(units), in_hbm(length))


def proto_end_body(place_ref, *refs):
    piece_refs, (protos_ref, out_ref) = refs[:-2], refs[-2:]
    unit, length = unit_rows(protos_ref[...].astype(f32))
    half = len(piece_refs) // 2
    sums = []
    for group in (piece_refs[:half], piece_refs[half:]):
        total = group[0][...]
        for ref in group[1:]:
            total = total + ref[...]
        sums.append(total)
    out_ref[...] = project(jnp.concatenate(sums, axis=1), unit, length)


def proto_end(place, pieces, protos):
    rows, width = pieces[0].shape
    return pl.pallas_call(
        proto_end_body,
        grid_spec=pltpu.PrefetchScalarGridSpec(
            num_scalar_prefetch=1,
            grid=(1,),
            in_specs=[pl.BlockSpec((rows, width), lambda i, p: (0, 0))] * len(pieces)
            + [pl.BlockSpec((rows, D), lambda i, p: (p[1], 0))],
            out_specs=pl.BlockSpec((rows, D), lambda i, p: (0, 0)),
        ),
        out_shape=jax.ShapeDtypeStruct((rows, D), f32),
        compiler_params=params(8),
        name="proto_end",
    )(place, *pieces, in_hbm(protos))


def direct_sum(value, axis):
    n = lax.axis_size(axis)
    total = value
    for step in range(1, n):
        total = total + lax.ppermute(value, axis, [(i, (i + step) % n) for i in range(n)])
    return total


def on_device(teacher_patches, student_patches, mask_order, teacher_protos, student_protos):
    y_size, z_size = lax.axis_size("y"), lax.axis_size("z")
    proto_size = lax.axis_size("x") * lax.axis_size("core")
    y, z = lax.axis_index("y"), lax.axis_index("z")
    core = lax.axis_index("core")
    place = jnp.stack([y, y * z_size + z, lax.axis_index(PROTOS), core]).astype(jnp.int32)

    units, student_length, mine = select_tokens(
        place, teacher_patches, student_patches, mask_order
    )
    from_y = lambda value, step: lax.ppermute(
        value, "y", [(i, (i + step) % y_size) for i in range(y_size)]
    )
    from_core = lambda value: lax.ppermute(value, "core", [(0, 1), (1, 0)])

    energy, sums = energy_of(units, teacher_protos)
    norm_part = student_sums(units, student_protos)
    for sweep in range(ITERS):
        last = sweep == ITERS - 1
        if sweep > 0:
            sums = column_sums(energy, pieces)
        sums = direct_sum(sums, "y")
        if sweep == 0:
            sums, mine = lax.optimization_barrier((sums, mine))
            got_first, got_third = from_y(mine, 1), from_y(mine, 3)
        elif sweep == 1:
            sums, mine, got_first, got_third = lax.optimization_barrier(
                (sums, mine, got_first, got_third)
            )
            got_second = from_y(mine, 2)
            other_first, other_third = from_core(got_first), from_core(got_third)
        else:
            sums, got_second = lax.optimization_barrier((sums, got_second))
            other_second = from_core(got_second)
        sums = spread(jnp.broadcast_to(sums, (z_size,) + sums.shape), "z")
        col_scale, row_part = row_sums(energy, sums, 1 if last else proto_size)
        if not last:
            pieces = spread(row_part, PROTOS)
        if sweep == 0:
            pieces, got_first, got_third = lax.optimization_barrier((pieces, got_first, got_third))
        elif sweep == 1:
            pieces, got_second, other_first, other_third = lax.optimization_barrier(
                (pieces, got_second, other_first, other_third)
            )
    row_part, other_second = lax.optimization_barrier((row_part, other_second))
    units_cast = cast_units(
        place, units, [got_first, got_second, got_third], [other_first, other_second, other_third]
    )
    both = jnp.concatenate([row_part[0], norm_part], axis=0)
    peers = y_size * proto_size
    both = jnp.broadcast_to(both, (peers,) + both.shape)
    pieces = spread(both, ("y",) + PROTOS).reshape((y_size, proto_size) + both.shape[1:])

    share = teacher_protos.shape[0] // y_size
    send_left, send_right, keep_left, keep_right = proto_gradient(
        y, z, units_cast, pieces, teacher_protos, student_protos, col_scale, share
    )
    keep_left, col_scale = lax.optimization_barrier((keep_left, col_scale))
    left = collect(send_left, keep_left, 0)
    right_half = collect(send_right, keep_right, 1)
    feature_part = feature_gradient(
        place, energy, units, pieces, student_protos, col_scale, proto_size
    )
    feature_part, left, right_half = lax.optimization_barrier((feature_part, left, right_half))
    left, right_half = pass_on(left, 0), pass_on(right_half, 1)
    feature_pieces = spread(feature_part, PROTOS)
    feature_pieces, left, right_half = lax.optimization_barrier((feature_pieces, left, right_half))
    left, right_half = deliver(left, 0), deliver(right_half, 1)
    result = spread(student_end(place, feature_pieces, units, student_length), PROTOS)
    grad_protos = proto_end(place, left + right_half, student_protos)
    return (result.reshape(-1, MASKED, D), grad_protos)


def solution(mesh):
    fine = Mesh(mesh.devices.reshape(4, 8, 4, 2), ("y", "z", "x", "core"))
    return jax.shard_map(
        on_device,
        mesh=fine,
        in_specs=(
            P(ROWS, None, None),
            P(ROWS, None, None),
            P(ROWS, None),
            P(PROTOS, None),
            P(PROTOS, None),
        ),
        out_specs=(P(ROWS, None, None), P(PROTOS + ROWS, None)),
        check_vma=False,
    )
```

```python
import math

import jax
import jax.numpy as jnp
from jax import lax
from jax.experimental import pallas as pl
from jax.experimental.pallas import tpu as pltpu
from jax.sharding import Mesh, PartitionSpec as P

D = 256
MASKED = 128
ITERS = 3
LANES = 128

teacher_temp = 0.07
student_temp = 0.1
epsilon = 1e-06

teacher_power = math.log2(math.e) / teacher_temp
student_power = math.log2(math.e) / student_temp

ROWS = ("y", "z")
PROTOS = ("x", "core")

f32 = jnp.float32
bf16 = jnp.bfloat16


def params(mib):
    return pltpu.CompilerParams(vmem_limit_bytes=mib * 2**20)


def spread(value, axes):
    return lax.all_to_all(value, axes, 0, 0, tiled=True)


def work(flops, moved, powers=0):
    return pl.CostEstimate(flops=int(flops), bytes_accessed=int(moved), transcendentals=int(powers))


def in_hbm(value):
    return pltpu.with_memory_space_constraint(value, pltpu.HBM)


def nt_dot(a, b):
    return lax.dot_general(a, b, (((1,), (1,)), ((), ())), preferred_element_type=f32)


def unit_rows(values):
    length = jnp.sqrt(jnp.sum(values * values, axis=-1, keepdims=True) + epsilon)
    return (values / length, length)


def directions(values):
    values = values.astype(f32)
    return (values * lax.rsqrt(jnp.sum(values * values, axis=-1, keepdims=True) + epsilon)).astype(bf16)


def to_column(row):
    return jnp.broadcast_to(row, (LANES, LANES)).T


def fill_columns(rows, tile_ref):
    for k in range(rows.shape[0]):
        tile_ref[k * LANES : (k + 1) * LANES, :] = to_column(rows[k : k + 1, :])


def lane_totals(tile):
    parts = [
        jnp.sum(tile[k * LANES : (k + 1) * LANES, :].T, axis=0, keepdims=True)
        for k in range(tile.shape[0] // LANES)
    ]
    return jnp.concatenate(parts, axis=0)


def select_body(place_ref, teacher_ref, student_ref, order_ref, units_ref, length_ref, mine_ref):
    images, patches, _ = teacher_ref.shape
    for image in range(images):
        chosen = order_ref[image : image + 1, :MASKED]
        place = lax.broadcasted_iota(jnp.int32, (patches, MASKED), 0)
        onehot = jnp.where(place == chosen, 1.0, 0.0).astype(bf16)

        def pick(ref):
            return lax.dot_general(
                onehot, ref[image], (((0,), (0,)), ((), ())), preferred_element_type=f32
            )

        rows = slice(image * MASKED, (image + 1) * MASKED)
        teacher = unit_rows(pick(teacher_ref))[0]
        student, length_ref[rows, :] = unit_rows(pick(student_ref))
        units_ref[rows, :D] = teacher
        units_ref[rows, D:] = student
        mine_ref[rows, :] = jnp.where(place_ref[3] == 0, teacher, student)


def select_tokens(place, teacher_patches, student_patches, mask_order):
    tokens = teacher_patches.shape[0] * MASKED
    return pl.pallas_call(
        select_body,
        in_specs=[pl.BlockSpec(memory_space=pltpu.SMEM)]
        + [pl.BlockSpec(memory_space=pltpu.VMEM)] * 3,
        out_specs=[pl.BlockSpec(memory_space=pltpu.VMEM)] * 3,
        out_shape=[
            pltpu.HBM((tokens, 2 * D), f32),
            pltpu.HBM((tokens, 1), f32),
            pltpu.HBM((tokens, D), f32),
        ],
        compiler_params=params(8),
        name="select",
    )(place, in_hbm(teacher_patches), in_hbm(student_patches), in_hbm(mask_order))


def lane_rows(row):
    parts = [row[:, j * LANES : (j + 1) * LANES] for j in range(row.shape[1] // LANES)]
    return jnp.concatenate(parts, axis=0)


def chunks(tokens):
    return [slice(c, c + LANES) for c in range(0, tokens, LANES)]


FETCHES = 8
WIDE = 256


def fetch(protos_ref, buffer_ref, sems, i):
    size = buffer_ref.shape[0] // FETCHES
    rows = pl.ds(pl.multiple_of(i * size, size), size)
    return pltpu.make_async_copy(protos_ref.at[rows, :], buffer_ref.at[rows, :], sems.at[i])


def fetch_all(units_ref, column, unit_ref, protos_ref, buffer_ref, sems):
    units = pltpu.make_async_copy(
        units_ref.at[:, pl.ds(column, D)], unit_ref, sems.at[FETCHES]
    )
    units.start()
    for i in range(FETCHES):
        fetch(protos_ref, buffer_ref, sems, i).start()
    units.wait()


def energy_body(
    place_ref, units_ref, *refs
):
    piece_refs, (protos_ref, energy_ref, sums_ref, cast_ref, weights_ref, total_ref) = refs[:8], refs[8:]
    own = units_ref.shape[0]
    tokens = cast_ref.shape[0]

    def rows_of(slot, start, size):
        return pl.ds(pl.multiple_of(place_ref[4 + slot] * own + start, size), size)

    cast_ref[rows_of(0, 0, own), :] = units_ref[...].astype(bf16)
    places = [(1, 0, own), (3, 0, own), (2, 0, own // 2), (2, own // 2, own // 2)]
    for core in range(2):

        @pl.when(place_ref[3] == core)
        def _(core=core):
            for i, ref in enumerate(piece_refs):
                kind = core if i < 4 else 1 - core
                cast_ref[rows_of(*places[i % 4]), kind * D : (kind + 1) * D] = ref[...].astype(bf16)

    weights_ref[...] = directions(protos_ref[...])
    total_ref[...] = jnp.zeros_like(total_ref)
    size = 512
    parts = [slice(c, c + size) for c in range(0, weights_ref.shape[0], size)]

    def step(i, carry):
        chunk = cast_ref[pl.ds(pl.multiple_of(i * WIDE, WIDE), WIDE), :][:, :D]
        logits = nt_dot(weights_ref[parts[0], :], chunk)
        for k, part in enumerate(parts):
            following = nt_dot(weights_ref[parts[k + 1], :], chunk) if k + 1 < len(parts) else None
            energy = jnp.exp2(logits * teacher_power)
            total = total_ref[part, :]
            for j in range(WIDE // LANES):
                tile = energy[:, j * LANES : (j + 1) * LANES]
                energy_ref[i * (WIDE // LANES) + j, part, :] = tile.astype(bf16)
                total = total + tile
            total_ref[part, :] = total
            logits = following
        return carry

    lax.fori_loop(0, tokens // WIDE, step, 0)
    totals = lane_totals(total_ref[...])
    for copy in range(sums_ref.shape[0]):
        sums_ref[copy] = totals


def fixed(*shape):
    return pl.BlockSpec(shape, lambda i: (0,) * len(shape))


def left(tokens):
    return pl.BlockSpec((tokens, D), lambda *i: (0, 0))


def right(tokens):
    return pl.BlockSpec((tokens, D), lambda *i: (0, 1))


def energy_of(place, units, pieces, protos, share, copies):
    own = units.shape[0]
    tokens = own * 4
    direct = pl.BlockSpec(memory_space=pltpu.VMEM)
    return pl.pallas_call(
        energy_body,
        grid_spec=pltpu.PrefetchScalarGridSpec(
            num_scalar_prefetch=1,
            grid=(1,),
            in_specs=[pl.BlockSpec(units.shape, lambda i, p: (0, 0))]
            + [pl.BlockSpec(piece.shape, lambda i, p: (0, 0)) for piece in pieces]
            + [pl.BlockSpec((share, D), lambda i, p: (p[0], 0))],
            out_specs=[
                direct,
                pl.BlockSpec((copies, share // LANES, LANES), lambda i, p: (0, 0, 0)),
                pl.BlockSpec((tokens, 2 * D), lambda i, p: (0, 0)),
            ],
            scratch_shapes=[pltpu.VMEM((share, D), bf16), pltpu.VMEM((share, LANES), f32)],
        ),
        out_shape=[
            pltpu.VMEM((tokens // LANES, share, LANES), bf16),
            jax.ShapeDtypeStruct((copies, share // LANES, LANES), f32),
            pltpu.HBM((tokens, 2 * D), bf16),
        ],
        compiler_params=params(24),
        cost_estimate=work(4 * tokens * share * D, 8 * 2**20, tokens * share),
        name="energy",
    )(place, in_hbm(units), *pieces, in_hbm(protos))


def student_body(units_ref, protos_ref, sums_ref, unit_ref, cast_ref, total_ref, buffer_ref, sems):
    size = buffer_ref.shape[0] // FETCHES
    fetch_all(units_ref, D, unit_ref, protos_ref, buffer_ref, sems)
    cast_ref[...] = unit_ref[...].astype(bf16)
    total_ref[...] = jnp.zeros_like(total_ref)

    def step(i, carry):
        fetch(protos_ref, buffer_ref, sems, i).wait()
        total = total_ref[...]

        def logits_of(part):
            rows = pl.ds(pl.multiple_of(i * size + part * WIDE, WIDE), WIDE)
            return nt_dot(cast_ref[...], directions(buffer_ref[rows, :]))

        parts = size // WIDE
        logits = logits_of(0)
        for part in range(parts):
            following = logits_of(part + 1) if part + 1 < parts else None
            values = jnp.exp2(logits * student_power)
            logits = following
            for j in range(WIDE // LANES):
                total = total + values[:, j * LANES : (j + 1) * LANES]
        total_ref[...] = total
        return carry

    lax.fori_loop(0, FETCHES, step, 0)
    sums_ref[...] = lane_totals(total_ref[...])


def student_sums(units, protos):
    tokens, count = units.shape[0], protos.shape[0]
    return pl.pallas_call(
        student_body,
        in_specs=[pl.BlockSpec(memory_space=pl.ANY)] * 2,
        out_specs=pl.BlockSpec(memory_space=pltpu.VMEM),
        out_shape=jax.ShapeDtypeStruct((tokens // LANES, LANES), f32),
        scratch_shapes=[
            pltpu.VMEM((tokens, D), f32),
            pltpu.VMEM((tokens, D), bf16),
            pltpu.VMEM((tokens, LANES), f32),
            pltpu.VMEM((count, D), bf16),
            pltpu.SemaphoreType.DMA((FETCHES + 1,)),
        ],
        compiler_params=params(16),
        cost_estimate=work(4 * tokens * count * D, 8 * 2**20, tokens * count),
        name="student",
    )(in_hbm(units), in_hbm(protos))


def right(tokens):
    return pl.BlockSpec((tokens, D), lambda *i: (0, 1))


def row_body(energy_ref, pieces_ref, *refs):
    norm_refs, (scale_ref, sums_ref, tile_ref) = refs[:-3], refs[-3:]
    scale_ref[...] = 1.0 / jnp.sum(pieces_ref[...], axis=0)
    fill_columns(scale_ref[...], tile_ref)
    tiles, protos, _ = energy_ref.shape
    size = 512
    totals = []
    for j in range(tiles):
        total = jnp.zeros((1, LANES), f32)
        for start in range(0, protos, size):
            part = slice(start, start + size)
            energy = energy_ref[j, part, :].astype(f32)
            total = total + jnp.sum(energy * tile_ref[part, :], axis=0, keepdims=True)
        totals.append(total)
    for ref in norm_refs:
        totals += [ref[...], jnp.zeros_like(ref)]
    totals = jnp.concatenate(totals, axis=0)
    for copy in range(sums_ref.shape[0]):
        sums_ref[copy] = totals


def row_sums(energy, pieces, copies, norm_part=()):
    tiles, protos, _ = energy.shape
    whole = pl.BlockSpec(memory_space=pltpu.VMEM)
    rows = tiles + 2 * sum(part.shape[0] for part in norm_part)
    return pl.pallas_call(
        row_body,
        in_specs=[whole] * (2 + len(norm_part)),
        out_specs=[whole] * 2,
        out_shape=[
            jax.ShapeDtypeStruct((protos // LANES, LANES), f32),
            jax.ShapeDtypeStruct((copies, rows, LANES), f32),
        ],
        scratch_shapes=[pltpu.VMEM((protos, LANES), f32)],
        compiler_params=params(12),
        cost_estimate=work(2 * energy.size, 0),
        name="row_sums",
    )(energy, pieces, *norm_part)


def column_body(energy_ref, pieces_ref, sums_ref, scale_ref):
    tiles, protos, _ = energy_ref.shape
    scale_ref[...] = 1.0 / jnp.sum(pieces_ref[...], axis=0)

    def step(k, carry):
        rows = pl.ds(pl.multiple_of(k * LANES, LANES), LANES)
        total = jnp.zeros((LANES, LANES), f32)
        for j in range(tiles):
            total = total + energy_ref[j, rows, :].astype(f32) * scale_ref[j : j + 1, :]
        sums_ref[0, pl.ds(k, 1), :] = lane_totals(total)
        return carry

    lax.fori_loop(0, protos // LANES, step, 0, unroll=4)
    for copy in range(1, sums_ref.shape[0]):
        sums_ref[copy] = sums_ref[0]


def column_sums(energy, pieces, copies):
    tiles, protos, _ = energy.shape
    whole = pl.BlockSpec(memory_space=pltpu.VMEM)
    return pl.pallas_call(
        column_body,
        in_specs=[whole] * 2,
        out_specs=whole,
        out_shape=jax.ShapeDtypeStruct((copies, protos // LANES, LANES), f32),
        scratch_shapes=[pltpu.VMEM((tiles, LANES), f32)],
        compiler_params=params(12),
        cost_estimate=work(2 * energy.size, 0),
        name="column_sums",
    )(energy, pieces)


LEFT_PLACE = [4, 5, 6, 7, 3, 2, 1, 0]
RIGHT_PLACE = [4, 0, 1, 2, 3, 7, 6, 5]


def collect(send, keep, offset):
    n = lax.axis_size("z")
    way = [1 if (z + offset) % 2 else -1 for z in range(n)]
    got = lax.ppermute(send, "z", [(z, (z - way[z]) % n) for z in range(n)])
    return keep[0] + got[0], keep[1] + got[1], keep[2:] + got[2:]


def pass_on(sums, offset):
    n = lax.axis_size("z")
    way = [1 if (z + offset) % 2 else -1 for z in range(n)]
    own, following, far = sums
    got = lax.ppermute(far, "z", [(z, (z + 2 * way[z]) % n) for z in range(n)])
    return own + got[0], following + got[1]


def deliver(sums, offset):
    n = lax.axis_size("z")
    way = [1 if (z + offset) % 2 else -1 for z in range(n)]
    own, following = sums
    return [own, lax.ppermute(following, "z", [(z, (z + way[z]) % n) for z in range(n)])]


def gradient_body(
    table_ref,
    units_ref,
    energy_ref,
    pieces_ref,
    sw_first_ref,
    sw_second_ref,
    scale_ref,
    send_left_ref,
    send_right_ref,
    keep_left_ref,
    keep_right_ref,
    feature_ref,
    r_ref,
    n_ref,
    total_ref,
):
    step = pl.program_id(0)
    tiles = energy_ref.shape[0]
    groups = pieces_ref.shape[0]
    own = tiles // groups

    @pl.when(step == 0)
    def _():
        scale = (1.0 / student_temp) / jnp.sum(pieces_ref[:, :, :tiles, :], axis=(0, 1))
        for k in range(tiles):
            r_ref[:, k * LANES : (k + 1) * LANES] = scale[k : k + 1, :]
        for group in range(groups):
            total = jnp.sum(pieces_ref[group, :, tiles : tiles + own, :], axis=0)
            inverse = (1.0 / student_temp) / total
            for k in range(own):
                lanes = slice((group * own + k) * LANES, (group * own + k + 1) * LANES)
                n_ref[:, lanes] = inverse[k : k + 1, :]
        feature_ref[...] = jnp.zeros_like(feature_ref)

    both = lambda first, second: jnp.concatenate([first, second], axis=0)
    block = sw_first_ref.shape[0]
    sw = both(directions(sw_first_ref[...]), directions(sw_second_ref[...]))
    local = [table_ref[3, 2 * step], table_ref[3, 2 * step + 1]]
    here = [pl.ds(pl.multiple_of(place * block, block), block) for place in local]
    columns = []
    for place in local:
        for k in range(block // LANES):
            row = scale_ref[pl.ds(place * (block // LANES) + k, 1), :]
            columns.append(to_column(row))
    col_scale = jnp.concatenate(columns, axis=0)

    def logits_of(part):
        return nt_dot(sw, units_ref[part, D:])

    parts = [slice(c, c + WIDE) for c in range(0, units_ref.shape[0], WIDE)]
    logits = logits_of(parts[0])
    for i, part in enumerate(parts):
        following = logits_of(parts[i + 1]) if i + 1 < len(parts) else None
        grads = []
        for j in range(WIDE // LANES):
            tile = i * (WIDE // LANES) + j
            lanes = slice(tile * LANES, (tile + 1) * LANES)
            energy = both(energy_ref[tile, here[0], :], energy_ref[tile, here[1], :]).astype(f32)
            probs = jnp.exp2(logits[:, j * LANES : (j + 1) * LANES] * student_power) * n_ref[:, lanes]
            grads.append((probs - energy * r_ref[:, lanes] * col_scale).astype(bf16))
        logit_grad = jnp.concatenate(grads, axis=1)
        added = jnp.dot(logit_grad, units_ref[part, D:], preferred_element_type=f32)
        total_ref[...] = added if i == 0 else total_ref[...] + added
        feature_ref[part, :] += lax.dot_general(
            logit_grad, sw, (((0,), (0,)), ((), ())), preferred_element_type=f32
        )
        logits = following

    for which in range(2):
        rows_here = slice(which * block, (which + 1) * block)
        for row, columns_here, sent_ref, kept_ref in (
            (1, slice(0, D // 2), send_left_ref, keep_left_ref),
            (2, slice(D // 2, D), send_right_ref, keep_right_ref),
        ):
            place = table_ref[row, 2 * step + which]

            @pl.when(place < 4)
            def _():
                sent_ref[jnp.minimum(place, 3)] = total_ref[rows_here, columns_here]

            @pl.when(place >= 4)
            def _():
                kept_ref[jnp.maximum(place - 4, 0)] = total_ref[rows_here, columns_here]


def gradients(y, z, units_all, energy, pieces, student_protos, scale):
    tiles, share, _ = energy.shape
    tokens = units_all.shape[0]
    block = 256
    blocks = share // block
    way = jnp.where(z % 2 == 1, 1, -1)
    local = (z + way * jnp.arange(blocks) + blocks) % blocks
    table = jnp.stack(
        [y * blocks + local, jnp.array(LEFT_PLACE), jnp.array(RIGHT_PLACE), local]
    ).astype(jnp.int32)
    whole = lambda *shape: pl.BlockSpec(shape, lambda i, p: (0,) * len(shape))
    first = pl.BlockSpec((block, D), lambda i, p: (p[0, 2 * i], 0))
    second = pl.BlockSpec((block, D), lambda i, p: (p[0, 2 * i + 1], 0))
    direct = pl.BlockSpec(memory_space=pltpu.VMEM)
    half = pltpu.VMEM((blocks // 2, block, D // 2), f32)
    return pl.pallas_call(
        gradient_body,
        grid_spec=pltpu.PrefetchScalarGridSpec(
            num_scalar_prefetch=1,
            grid=(blocks // 2,),
            in_specs=[
                whole(tokens, 2 * D),
                direct,
                whole(*pieces.shape),
                first,
                second,
                whole(*scale.shape),
            ],
            out_specs=[direct] * 5,
            scratch_shapes=[
                pltpu.VMEM((1, tokens), f32),
                pltpu.VMEM((1, tokens), f32),
                pltpu.VMEM((2 * block, D), f32),
            ],
        ),
        out_shape=[half, half, half, half, pltpu.VMEM((tokens, D), f32)],
        compiler_params=params(24),
        cost_estimate=work(8 * tokens * share * D, 8 * 2**20, tokens * share),
        name="gradients",
    )(
        table,
        in_hbm(units_all),
        energy,
        pieces,
        in_hbm(student_protos),
        in_hbm(student_protos),
        scale,
    )


def project(total, unit, length):
    return (total - unit * jnp.sum(unit * total, axis=-1, keepdims=True)) / length


def student_end_body(place_ref, pieces_ref, unit_ref, length_ref, out_ref):
    result = project(jnp.sum(pieces_ref[...], axis=0), unit_ref[...], length_ref[...])
    for copy in range(out_ref.shape[0]):
        out_ref[copy] = result


def student_end(place, pieces, units, length, copies):
    _, rows, _ = pieces.shape
    return pl.pallas_call(
        student_end_body,
        grid_spec=pltpu.PrefetchScalarGridSpec(
            num_scalar_prefetch=1,
            grid=(1,),
            in_specs=[
                pl.BlockSpec(pieces.shape, lambda i, p: (0, 0, 0)),
                pl.BlockSpec((rows, D), lambda i, p: (p[2], 1)),
                pl.BlockSpec((rows, 1), lambda i, p: (p[2], 0)),
            ],
            out_specs=pl.BlockSpec((copies, rows, D), lambda i, p: (0, 0, 0)),
        ),
        out_shape=jax.ShapeDtypeStruct((copies, rows, D), f32),
        compiler_params=params(8),
        name="student_end",
    )(place, pieces, in_hbm(units), in_hbm(length))


def proto_end_body(place_ref, *refs):
    piece_refs, (protos_ref, out_ref) = refs[:-2], refs[-2:]
    unit, length = unit_rows(protos_ref[...].astype(f32))
    half = len(piece_refs) // 2
    sums = []
    for group in (piece_refs[:half], piece_refs[half:]):
        total = group[0][...]
        for ref in group[1:]:
            total = total + ref[...]
        sums.append(total)
    out_ref[...] = project(jnp.concatenate(sums, axis=1), unit, length)


def proto_end(place, pieces, protos):
    rows, width = pieces[0].shape
    return pl.pallas_call(
        proto_end_body,
        grid_spec=pltpu.PrefetchScalarGridSpec(
            num_scalar_prefetch=1,
            grid=(1,),
            in_specs=[pl.BlockSpec((rows, width), lambda i, p: (0, 0))] * len(pieces)
            + [pl.BlockSpec((rows, D), lambda i, p: (p[1], 0))],
            out_specs=pl.BlockSpec((rows, D), lambda i, p: (0, 0)),
        ),
        out_shape=jax.ShapeDtypeStruct((rows, D), f32),
        compiler_params=params(8),
        name="proto_end",
    )(place, *pieces, in_hbm(protos))


def on_device(teacher_patches, student_patches, mask_order, teacher_protos, student_protos):
    y_size, z_size = lax.axis_size("y"), lax.axis_size("z")
    proto_size = lax.axis_size("x") * lax.axis_size("core")
    y, z = lax.axis_index("y"), lax.axis_index("z")
    others = [(y - step + y_size) % y_size for step in range(y_size)]
    place = [y, y * z_size + z, lax.axis_index(PROTOS), lax.axis_index("core")] + others
    place = jnp.stack(place).astype(jnp.int32)
    share = teacher_protos.shape[0] // y_size

    units, student_length, mine = select_tokens(
        place, teacher_patches, student_patches, mask_order
    )
    from_y = lambda value, step: lax.ppermute(
        value, "y", [(i, (i + step) % y_size) for i in range(y_size)]
    )
    from_core = lambda value: lax.ppermute(value, "core", [(0, 1), (1, 0)])
    half = mine.shape[0] // 2
    first, third = from_y(mine, 1), from_y(mine, 3)
    got = [first, third, from_y(first[:half], 1), from_y(third[half:], 3)]
    got = got + [from_core(piece) for piece in got]
    norm_part = student_sums(units, student_protos)
    norm_part, got = lax.optimization_barrier((norm_part, got))

    rows = ("y",) + PROTOS
    peers = y_size * proto_size
    energy, sums, units_all = energy_of(place, units, got, teacher_protos, share, z_size)
    for sweep in range(ITERS):
        if sweep > 0:
            sums = column_sums(energy, pieces, z_size)
        norms = (norm_part,) if sweep == ITERS - 1 else ()
        col_scale, row_part = row_sums(energy, spread(sums, "z"), peers, norms)
        pieces = spread(row_part, rows)
    pieces = pieces.reshape((y_size, proto_size) + pieces.shape[1:])

    send_left, send_right, keep_left, keep_right, feature_part = gradients(
        y, z, units_all, energy, pieces, student_protos, col_scale
    )
    left = pass_on(collect(send_left, keep_left, 0), 0)
    right_half = pass_on(collect(send_right, keep_right, 1), 1)
    feature_pieces = spread(feature_part.reshape(peers, -1, D), rows)
    feature_pieces, left, right_half = lax.optimization_barrier((feature_pieces, left, right_half))
    left, right_half = deliver(left, 0), deliver(right_half, 1)
    result = student_end(place, feature_pieces, units, student_length, proto_size)
    result = spread(result, PROTOS)
    grad_protos = proto_end(place, left + right_half, student_protos)
    return (result.reshape(-1, MASKED, D), grad_protos)


def solution(mesh):
    fine = Mesh(mesh.devices.reshape(4, 8, 4, 2), ("y", "z", "x", "core"))
    return jax.shard_map(
        on_device,
        mesh=fine,
        in_specs=(
            P(ROWS, None, None),
            P(ROWS, None, None),
            P(ROWS, None),
            P(PROTOS, None),
            P(PROTOS, None),
        ),
        out_specs=(P(ROWS, None, None), P(PROTOS + ROWS, None)),
        check_vma=False,
    )
```

```python
import math

import jax
import jax.numpy as jnp
from jax import lax
from jax.experimental import pallas as pl
from jax.experimental.pallas import tpu as pltpu
from jax.sharding import Mesh, PartitionSpec as P

D = 256
MASKED = 128
ITERS = 3
LANES = 128

teacher_temp = 0.07
student_temp = 0.1
epsilon = 1e-06

teacher_power = math.log2(math.e) / teacher_temp
student_power = math.log2(math.e) / student_temp

ROWS = ("y", "z")
PROTOS = ("x", "core")

f32 = jnp.float32
bf16 = jnp.bfloat16


def params(mib):
    return pltpu.CompilerParams(vmem_limit_bytes=mib * 2**20)


def spread(value, axes):
    return lax.all_to_all(value, axes, 0, 0, tiled=True)


def work(flops, moved, powers=0):
    return pl.CostEstimate(flops=int(flops), bytes_accessed=int(moved), transcendentals=int(powers))


def in_hbm(value):
    return pltpu.with_memory_space_constraint(value, pltpu.HBM)


def nt_dot(a, b):
    return lax.dot_general(a, b, (((1,), (1,)), ((), ())), preferred_element_type=f32)


def unit_rows(values):
    length = jnp.sqrt(jnp.sum(values * values, axis=-1, keepdims=True) + epsilon)
    return (values / length, length)


def directions(values):
    values = values.astype(f32)
    return (values * lax.rsqrt(jnp.sum(values * values, axis=-1, keepdims=True) + epsilon)).astype(bf16)


def to_column(row):
    return jnp.broadcast_to(row, (LANES, LANES)).T


def fill_columns(rows, tile_ref):
    for k in range(rows.shape[0]):
        tile_ref[k * LANES : (k + 1) * LANES, :] = to_column(rows[k : k + 1, :])


def lane_totals(tile):
    parts = [
        jnp.sum(tile[k * LANES : (k + 1) * LANES, :].T, axis=0, keepdims=True)
        for k in range(tile.shape[0] // LANES)
    ]
    return jnp.concatenate(parts, axis=0)


def select_body(place_ref, teacher_ref, student_ref, order_ref, units_ref, length_ref, mine_ref):
    images, patches, _ = teacher_ref.shape
    for image in range(images):
        chosen = order_ref[image : image + 1, :MASKED]
        place = lax.broadcasted_iota(jnp.int32, (patches, MASKED), 0)
        onehot = jnp.where(place == chosen, 1.0, 0.0).astype(bf16)

        def pick(ref):
            return lax.dot_general(
                onehot, ref[image], (((0,), (0,)), ((), ())), preferred_element_type=f32
            )

        rows = slice(image * MASKED, (image + 1) * MASKED)
        teacher = unit_rows(pick(teacher_ref))[0]
        student, length_ref[rows, :] = unit_rows(pick(student_ref))
        units_ref[rows, :D] = teacher
        units_ref[rows, D:] = student
        mine_ref[rows, :] = jnp.where(place_ref[3] == 0, teacher, student)


def select_tokens(place, teacher_patches, student_patches, mask_order):
    tokens = teacher_patches.shape[0] * MASKED
    return pl.pallas_call(
        select_body,
        in_specs=[pl.BlockSpec(memory_space=pltpu.SMEM)]
        + [pl.BlockSpec(memory_space=pltpu.VMEM)] * 3,
        out_specs=[pl.BlockSpec(memory_space=pltpu.VMEM)] * 3,
        out_shape=[
            pltpu.HBM((tokens, 2 * D), f32),
            pltpu.HBM((tokens, 1), f32),
            pltpu.HBM((tokens, D), f32),
        ],
        compiler_params=params(8),
        name="select",
    )(place, in_hbm(teacher_patches), in_hbm(student_patches), in_hbm(mask_order))


def lane_rows(row):
    parts = [row[:, j * LANES : (j + 1) * LANES] for j in range(row.shape[1] // LANES)]
    return jnp.concatenate(parts, axis=0)


def chunks(tokens):
    return [slice(c, c + LANES) for c in range(0, tokens, LANES)]


FETCHES = 8
WIDE = 256


def fetch(protos_ref, buffer_ref, sems, i):
    size = buffer_ref.shape[0] // FETCHES
    rows = pl.ds(pl.multiple_of(i * size, size), size)
    return pltpu.make_async_copy(protos_ref.at[rows, :], buffer_ref.at[rows, :], sems.at[i])


def fetch_all(units_ref, column, unit_ref, protos_ref, buffer_ref, sems):
    units = pltpu.make_async_copy(
        units_ref.at[:, pl.ds(column, D)], unit_ref, sems.at[FETCHES]
    )
    units.start()
    for i in range(FETCHES):
        fetch(protos_ref, buffer_ref, sems, i).start()
    units.wait()


def energy_body(
    place_ref, units_ref, *refs
):
    piece_refs, (protos_ref, energy_ref, sums_ref, cast_ref, weights_ref, total_ref) = refs[:8], refs[8:]
    own = units_ref.shape[0]
    tokens = cast_ref.shape[0]

    def rows_of(slot, start, size):
        return pl.ds(pl.multiple_of(place_ref[4 + slot] * own + start, size), size)

    cast_ref[rows_of(0, 0, own), :] = units_ref[...].astype(bf16)
    places = [(1, 0, own), (3, 0, own), (2, 0, own // 2), (2, own // 2, own // 2)]
    for core in range(2):

        @pl.when(place_ref[3] == core)
        def _(core=core):
            for i, ref in enumerate(piece_refs):
                kind = core if i < 4 else 1 - core
                cast_ref[rows_of(*places[i % 4]), kind * D : (kind + 1) * D] = ref[...].astype(bf16)

    weights_ref[...] = directions(protos_ref[...])
    total_ref[...] = jnp.zeros_like(total_ref)
    size = 512
    parts = [slice(c, c + size) for c in range(0, weights_ref.shape[0], size)]

    def step(i, carry):
        chunk = cast_ref[pl.ds(pl.multiple_of(i * WIDE, WIDE), WIDE), :][:, :D]
        logits = nt_dot(weights_ref[parts[0], :], chunk)
        for k, part in enumerate(parts):
            following = nt_dot(weights_ref[parts[k + 1], :], chunk) if k + 1 < len(parts) else None
            energy = jnp.exp2(logits * teacher_power)
            total = total_ref[part, :]
            for j in range(WIDE // LANES):
                tile = energy[:, j * LANES : (j + 1) * LANES]
                energy_ref[i * (WIDE // LANES) + j, part, :] = tile.astype(bf16)
                total = total + tile
            total_ref[part, :] = total
            logits = following
        return carry

    lax.fori_loop(0, tokens // WIDE, step, 0)
    totals = lane_totals(total_ref[...])
    for copy in range(sums_ref.shape[0]):
        sums_ref[copy] = totals


def fixed(*shape):
    return pl.BlockSpec(shape, lambda i: (0,) * len(shape))


def left(tokens):
    return pl.BlockSpec((tokens, D), lambda *i: (0, 0))


def right(tokens):
    return pl.BlockSpec((tokens, D), lambda *i: (0, 1))


def energy_of(place, units, pieces, protos, share, copies):
    own = units.shape[0]
    tokens = own * 4
    direct = pl.BlockSpec(memory_space=pltpu.VMEM)
    return pl.pallas_call(
        energy_body,
        grid_spec=pltpu.PrefetchScalarGridSpec(
            num_scalar_prefetch=1,
            grid=(1,),
            in_specs=[pl.BlockSpec(units.shape, lambda i, p: (0, 0))]
            + [pl.BlockSpec(piece.shape, lambda i, p: (0, 0)) for piece in pieces]
            + [pl.BlockSpec((share, D), lambda i, p: (p[0], 0))],
            out_specs=[
                direct,
                pl.BlockSpec((copies, share // LANES, LANES), lambda i, p: (0, 0, 0)),
                pl.BlockSpec((tokens, 2 * D), lambda i, p: (0, 0)),
            ],
            scratch_shapes=[pltpu.VMEM((share, D), bf16), pltpu.VMEM((share, LANES), f32)],
        ),
        out_shape=[
            pltpu.VMEM((tokens // LANES, share, LANES), bf16),
            jax.ShapeDtypeStruct((copies, share // LANES, LANES), f32),
            pltpu.HBM((tokens, 2 * D), bf16),
        ],
        compiler_params=params(24),
        cost_estimate=work(4 * tokens * share * D, 8 * 2**20, tokens * share),
        name="energy",
    )(place, in_hbm(units), *pieces, in_hbm(protos))


def student_body(units_ref, protos_ref, sums_ref, unit_ref, cast_ref, total_ref, buffer_ref, sems):
    size = buffer_ref.shape[0] // FETCHES
    fetch_all(units_ref, D, unit_ref, protos_ref, buffer_ref, sems)
    cast_ref[...] = unit_ref[...].astype(bf16)
    total_ref[...] = jnp.zeros_like(total_ref)

    def step(i, carry):
        fetch(protos_ref, buffer_ref, sems, i).wait()
        total = total_ref[...]

        def logits_of(part):
            rows = pl.ds(pl.multiple_of(i * size + part * WIDE, WIDE), WIDE)
            return nt_dot(cast_ref[...], directions(buffer_ref[rows, :]))

        parts = size // WIDE
        logits = logits_of(0)
        for part in range(parts):
            following = logits_of(part + 1) if part + 1 < parts else None
            values = jnp.exp2(logits * student_power)
            logits = following
            for j in range(WIDE // LANES):
                total = total + values[:, j * LANES : (j + 1) * LANES]
        total_ref[...] = total
        return carry

    lax.fori_loop(0, FETCHES, step, 0)
    sums_ref[...] = lane_totals(total_ref[...])


def student_sums(units, protos):
    tokens, count = units.shape[0], protos.shape[0]
    return pl.pallas_call(
        student_body,
        in_specs=[pl.BlockSpec(memory_space=pl.ANY)] * 2,
        out_specs=pl.BlockSpec(memory_space=pltpu.VMEM),
        out_shape=jax.ShapeDtypeStruct((tokens // LANES, LANES), f32),
        scratch_shapes=[
            pltpu.VMEM((tokens, D), f32),
            pltpu.VMEM((tokens, D), bf16),
            pltpu.VMEM((tokens, LANES), f32),
            pltpu.VMEM((count, D), bf16),
            pltpu.SemaphoreType.DMA((FETCHES + 1,)),
        ],
        compiler_params=params(16),
        cost_estimate=work(4 * tokens * count * D, 8 * 2**20, tokens * count),
        name="student",
    )(in_hbm(units), in_hbm(protos))


def right(tokens):
    return pl.BlockSpec((tokens, D), lambda *i: (0, 1))


def row_body(energy_ref, pieces_ref, *refs):
    norm_refs, (scale_ref, sums_ref, tile_ref) = refs[:-3], refs[-3:]
    scale_ref[...] = 1.0 / jnp.sum(pieces_ref[...], axis=0)
    fill_columns(scale_ref[...], tile_ref)
    tiles, protos, _ = energy_ref.shape
    size = 512
    totals = []
    for j in range(tiles):
        total = jnp.zeros((1, LANES), f32)
        for start in range(0, protos, size):
            part = slice(start, start + size)
            energy = energy_ref[j, part, :].astype(f32)
            total = total + jnp.sum(energy * tile_ref[part, :], axis=0, keepdims=True)
        totals.append(total)
    for ref in norm_refs:
        totals += [ref[...], jnp.zeros_like(ref)]
    totals = jnp.concatenate(totals, axis=0)
    for copy in range(sums_ref.shape[0]):
        sums_ref[copy] = totals


def row_sums(energy, pieces, copies, norm_part=()):
    tiles, protos, _ = energy.shape
    whole = pl.BlockSpec(memory_space=pltpu.VMEM)
    rows = tiles + 2 * sum(part.shape[0] for part in norm_part)
    return pl.pallas_call(
        row_body,
        in_specs=[whole] * (2 + len(norm_part)),
        out_specs=[whole] * 2,
        out_shape=[
            jax.ShapeDtypeStruct((protos // LANES, LANES), f32),
            jax.ShapeDtypeStruct((copies, rows, LANES), f32),
        ],
        scratch_shapes=[pltpu.VMEM((protos, LANES), f32)],
        compiler_params=params(12),
        cost_estimate=work(2 * energy.size, 0),
        name="row_sums",
    )(energy, pieces, *norm_part)


def column_body(energy_ref, pieces_ref, sums_ref, scale_ref):
    tiles, protos, _ = energy_ref.shape
    scale_ref[...] = 1.0 / jnp.sum(pieces_ref[...], axis=0)

    def step(k, carry):
        rows = pl.ds(pl.multiple_of(k * LANES, LANES), LANES)
        total = jnp.zeros((LANES, LANES), f32)
        for j in range(tiles):
            total = total + energy_ref[j, rows, :].astype(f32) * scale_ref[j : j + 1, :]
        sums_ref[0, pl.ds(k, 1), :] = lane_totals(total)
        return carry

    lax.fori_loop(0, protos // LANES, step, 0, unroll=4)
    for copy in range(1, sums_ref.shape[0]):
        sums_ref[copy] = sums_ref[0]


def column_sums(energy, pieces, copies):
    tiles, protos, _ = energy.shape
    whole = pl.BlockSpec(memory_space=pltpu.VMEM)
    return pl.pallas_call(
        column_body,
        in_specs=[whole] * 2,
        out_specs=whole,
        out_shape=jax.ShapeDtypeStruct((copies, protos // LANES, LANES), f32),
        scratch_shapes=[pltpu.VMEM((tiles, LANES), f32)],
        compiler_params=params(12),
        cost_estimate=work(2 * energy.size, 0),
        name="column_sums",
    )(energy, pieces)


LEFT_PLACE = [4, 5, 6, 7, 3, 2, 1, 0]
RIGHT_PLACE = [4, 0, 1, 2, 3, 7, 6, 5]


def collect(send, keep, offset):
    n = lax.axis_size("z")
    way = [1 if (z + offset) % 2 else -1 for z in range(n)]
    got = lax.ppermute(send, "z", [(z, (z - way[z]) % n) for z in range(n)])
    return keep[0] + got[0], keep[1] + got[1], keep[2:] + got[2:]


def pass_on(sums, offset):
    n = lax.axis_size("z")
    way = [1 if (z + offset) % 2 else -1 for z in range(n)]
    own, following, far = sums
    got = lax.ppermute(far, "z", [(z, (z + 2 * way[z]) % n) for z in range(n)])
    return own + got[0], following + got[1]


def deliver(sums, offset):
    n = lax.axis_size("z")
    way = [1 if (z + offset) % 2 else -1 for z in range(n)]
    own, following = sums
    return [own, lax.ppermute(following, "z", [(z, (z + way[z]) % n) for z in range(n)])]


def gradient_body(
    table_ref,
    units_ref,
    energy_ref,
    pieces_ref,
    sw_first_ref,
    sw_second_ref,
    scale_ref,
    send_left_ref,
    send_right_ref,
    keep_left_ref,
    keep_right_ref,
    feature_out_ref,
    r_ref,
    n_ref,
    total_ref,
    feature_ref,
    stage_ref,
    sems,
    feature_sems,
):
    step = pl.program_id(0)
    tiles = energy_ref.shape[0]
    groups = pieces_ref.shape[0]
    own = tiles // groups

    @pl.when(step == 0)
    def _():
        scale = (1.0 / student_temp) / jnp.sum(pieces_ref[:, :, :tiles, :], axis=(0, 1))
        for k in range(tiles):
            r_ref[:, k * LANES : (k + 1) * LANES] = scale[k : k + 1, :]
        for group in range(groups):
            total = jnp.sum(pieces_ref[group, :, tiles : tiles + own, :], axis=0)
            inverse = (1.0 / student_temp) / total
            for k in range(own):
                lanes = slice((group * own + k) * LANES, (group * own + k + 1) * LANES)
                n_ref[:, lanes] = inverse[k : k + 1, :]
        feature_ref[...] = jnp.zeros_like(feature_ref)

    both = lambda first, second: jnp.concatenate([first, second], axis=0)
    block = sw_first_ref.shape[0]
    sw = both(directions(sw_first_ref[...]), directions(sw_second_ref[...]))
    local = [table_ref[3, 2 * step], table_ref[3, 2 * step + 1]]
    here = [pl.ds(pl.multiple_of(place * block, block), block) for place in local]
    columns = []
    for place in local:
        for k in range(block // LANES):
            row = scale_ref[pl.ds(place * (block // LANES) + k, 1), :]
            columns.append(to_column(row))
    col_scale = jnp.concatenate(columns, axis=0)

    def logits_of(part):
        return nt_dot(sw, units_ref[part, D:])

    parts = [slice(c, c + WIDE) for c in range(0, units_ref.shape[0], WIDE)]

    def feature_copy(i):
        rows = pl.ds(i * WIDE, WIDE)
        return pltpu.make_async_copy(
            feature_ref.at[rows, :], feature_out_ref.at[rows, :], feature_sems.at[i]
        )

    logits = logits_of(parts[0])
    for i, part in enumerate(parts):
        following = logits_of(parts[i + 1]) if i + 1 < len(parts) else None
        grads = []
        for j in range(WIDE // LANES):
            tile = i * (WIDE // LANES) + j
            lanes = slice(tile * LANES, (tile + 1) * LANES)
            energy = both(energy_ref[tile, here[0], :], energy_ref[tile, here[1], :]).astype(f32)
            probs = jnp.exp2(logits[:, j * LANES : (j + 1) * LANES] * student_power) * n_ref[:, lanes]
            grads.append((probs - energy * r_ref[:, lanes] * col_scale).astype(bf16))
        logit_grad = jnp.concatenate(grads, axis=1)
        added = jnp.dot(logit_grad, units_ref[part, D:], preferred_element_type=f32)
        total_ref[...] = added if i == 0 else total_ref[...] + added
        feature_ref[part, :] += lax.dot_general(
            logit_grad, sw, (((0,), (0,)), ((), ())), preferred_element_type=f32
        )
        pl.when(step == pl.num_programs(0) - 1)(feature_copy(i).start)
        logits = following

    def copies(which, at):
        found = []
        for half, (sent_ref, kept_ref) in enumerate(
            ((send_left_ref, keep_left_ref), (send_right_ref, keep_right_ref))
        ):
            block_at = 2 * at + which
            place = table_ref[1 + half, block_at]
            source, sem = stage_ref.at[half, block_at], sems.at[half, block_at]
            sent = pltpu.make_async_copy(source, sent_ref.at[jnp.minimum(place, 3)], sem)
            kept = pltpu.make_async_copy(source, kept_ref.at[jnp.maximum(place - 4, 0)], sem)
            found += [(place < 4, sent), (place >= 4, kept)]
        return found

    for which in range(2):
        rows_here = slice(which * block, (which + 1) * block)
        for half in range(2):
            columns_here = slice(half * (D // 2), (half + 1) * (D // 2))
            stage_ref[half, 2 * step + which] = total_ref[rows_here, columns_here]
        for wanted, copy in copies(which, step):
            pl.when(wanted)(copy.start)

    @pl.when(step == pl.num_programs(0) - 1)
    def _():
        for i in range(len(parts)):
            feature_copy(i).wait()
        for at in range(stage_ref.shape[1] // 2):
            for which in range(2):
                for wanted, copy in copies(which, at):
                    pl.when(wanted)(copy.wait)


def block_table(y, z):
    blocks = len(LEFT_PLACE)
    way = jnp.where(z % 2 == 1, 1, -1)
    local = (z + way * jnp.arange(blocks) + blocks) % blocks
    table = [y * blocks + local, jnp.array(LEFT_PLACE), jnp.array(RIGHT_PLACE), local]
    return jnp.stack(table).astype(jnp.int32)


def gradients(table, units_all, energy, pieces, student_protos, scale):
    tiles, share, _ = energy.shape
    tokens = units_all.shape[0]
    block = 256
    blocks = share // block
    whole = lambda *shape: pl.BlockSpec(shape, lambda i, p: (0,) * len(shape))
    first = pl.BlockSpec((block, D), lambda i, p: (p[0, 2 * i], 0))
    second = pl.BlockSpec((block, D), lambda i, p: (p[0, 2 * i + 1], 0))
    direct = pl.BlockSpec(memory_space=pltpu.VMEM)
    half = pltpu.HBM((blocks // 2, block, D // 2), f32)
    return pl.pallas_call(
        gradient_body,
        grid_spec=pltpu.PrefetchScalarGridSpec(
            num_scalar_prefetch=1,
            grid=(blocks // 2,),
            in_specs=[
                whole(tokens, 2 * D),
                direct,
                whole(*pieces.shape),
                first,
                second,
                whole(*scale.shape),
            ],
            out_specs=[pl.BlockSpec(memory_space=pl.ANY)] * 5,
            scratch_shapes=[
                pltpu.VMEM((1, tokens), f32),
                pltpu.VMEM((1, tokens), f32),
                pltpu.VMEM((2 * block, D), f32),
                pltpu.VMEM((tokens, D), f32),
                pltpu.VMEM((2, blocks, block, D // 2), f32),
                pltpu.SemaphoreType.DMA((2, blocks)),
                pltpu.SemaphoreType.DMA((tokens // WIDE,)),
            ],
        ),
        out_shape=[half, half, half, half, pltpu.HBM((tokens, D), f32)],
        compiler_params=params(24),
        cost_estimate=work(8 * tokens * share * D, 8 * 2**20, tokens * share),
        name="gradients",
    )(
        table,
        in_hbm(units_all),
        energy,
        pieces,
        in_hbm(student_protos),
        in_hbm(student_protos),
        scale,
    )


def project(total, unit, length):
    return (total - unit * jnp.sum(unit * total, axis=-1, keepdims=True)) / length


def student_end_body(place_ref, pieces_ref, unit_ref, length_ref, out_ref):
    result = project(jnp.sum(pieces_ref[...], axis=0), unit_ref[...], length_ref[...])
    for copy in range(out_ref.shape[0]):
        out_ref[copy] = result


def student_end(place, pieces, units, length, copies):
    _, rows, _ = pieces.shape
    return pl.pallas_call(
        student_end_body,
        grid_spec=pltpu.PrefetchScalarGridSpec(
            num_scalar_prefetch=1,
            grid=(1,),
            in_specs=[
                pl.BlockSpec(pieces.shape, lambda i, p: (0, 0, 0)),
                pl.BlockSpec((rows, D), lambda i, p: (p[2], 1)),
                pl.BlockSpec((rows, 1), lambda i, p: (p[2], 0)),
            ],
            out_specs=pl.BlockSpec((copies, rows, D), lambda i, p: (0, 0, 0)),
        ),
        out_shape=jax.ShapeDtypeStruct((copies, rows, D), f32),
        compiler_params=params(8),
        name="student_end",
    )(place, pieces, in_hbm(units), in_hbm(length))


def proto_end_body(place_ref, *refs):
    piece_refs, (protos_ref, out_ref) = refs[:-2], refs[-2:]
    unit, length = unit_rows(protos_ref[...].astype(f32))
    half = len(piece_refs) // 2
    sums = []
    for group in (piece_refs[:half], piece_refs[half:]):
        total = group[0][...]
        for ref in group[1:]:
            total = total + ref[...]
        sums.append(total)
    out_ref[...] = project(jnp.concatenate(sums, axis=1), unit, length)


def proto_end(place, pieces, protos):
    rows, width = pieces[0].shape
    return pl.pallas_call(
        proto_end_body,
        grid_spec=pltpu.PrefetchScalarGridSpec(
            num_scalar_prefetch=1,
            grid=(1,),
            in_specs=[pl.BlockSpec((rows, width), lambda i, p: (0, 0))] * len(pieces)
            + [pl.BlockSpec((rows, D), lambda i, p: (p[1], 0))],
            out_specs=pl.BlockSpec((rows, D), lambda i, p: (0, 0)),
        ),
        out_shape=jax.ShapeDtypeStruct((rows, D), f32),
        compiler_params=params(8),
        name="proto_end",
    )(place, *pieces, in_hbm(protos))


def on_device(teacher_patches, student_patches, mask_order, teacher_protos, student_protos):
    y_size, z_size = lax.axis_size("y"), lax.axis_size("z")
    proto_size = lax.axis_size("x") * lax.axis_size("core")
    y, z = lax.axis_index("y"), lax.axis_index("z")
    others = [(y - step + y_size) % y_size for step in range(y_size)]
    place = [y, y * z_size + z, lax.axis_index(PROTOS), lax.axis_index("core")] + others
    place = jnp.stack(place).astype(jnp.int32)
    share = teacher_protos.shape[0] // y_size

    units, student_length, mine = select_tokens(
        place, teacher_patches, student_patches, mask_order
    )
    from_y = lambda value, step: lax.ppermute(
        value, "y", [(i, (i + step) % y_size) for i in range(y_size)]
    )
    from_core = lambda value: lax.ppermute(value, "core", [(0, 1), (1, 0)])
    half = mine.shape[0] // 2
    first, third = from_y(mine, 1), from_y(mine, 3)
    norm_part = student_sums(units, student_protos)
    norm_part, first, third = lax.optimization_barrier((norm_part, first, third))
    got = [first, third, from_y(first[:half], 1), from_y(third[half:], 3)]
    got = got + [from_core(piece) for piece in got]

    table = block_table(y, z)
    rows = ("y",) + PROTOS
    peers = y_size * proto_size
    energy, sums, units_all = energy_of(place, units, got, teacher_protos, share, z_size)
    for sweep in range(ITERS):
        if sweep > 0:
            sums = column_sums(energy, pieces, z_size)
        norms = (norm_part,) if sweep == ITERS - 1 else ()
        col_scale, row_part = row_sums(energy, spread(sums, "z"), peers, norms)
        row_part, place, table = lax.optimization_barrier((row_part, place, table))
        pieces = spread(row_part, rows)
    pieces = pieces.reshape((y_size, proto_size) + pieces.shape[1:])

    send_left, send_right, keep_left, keep_right, feature_part = gradients(
        table, units_all, energy, pieces, student_protos, col_scale
    )
    left = pass_on(collect(send_left, keep_left, 0), 0)
    right_half = pass_on(collect(send_right, keep_right, 1), 1)
    feature_pieces = spread(feature_part.reshape(peers, -1, D), rows)
    feature_pieces, left, right_half = lax.optimization_barrier((feature_pieces, left, right_half))
    left, right_half = deliver(left, 0), deliver(right_half, 1)
    result = student_end(place, feature_pieces, units, student_length, proto_size)
    result = spread(result, PROTOS)
    grad_protos = proto_end(place, left + right_half, student_protos)
    return (result.reshape(-1, MASKED, D), grad_protos)


def solution(mesh):
    fine = Mesh(mesh.devices.reshape(4, 8, 4, 2), ("y", "z", "x", "core"))
    return jax.shard_map(
        on_device,
        mesh=fine,
        in_specs=(
            P(ROWS, None, None),
            P(ROWS, None, None),
            P(ROWS, None),
            P(PROTOS, None),
            P(PROTOS, None),
        ),
        out_specs=(P(ROWS, None, None), P(PROTOS + ROWS, None)),
        check_vma=False,
    )
```

```python
import math

import jax
import jax.numpy as jnp
from jax import lax
from jax.experimental import pallas as pl
from jax.experimental.pallas import tpu as pltpu
from jax.sharding import Mesh, PartitionSpec as P

D = 256
MASKED = 128
ITERS = 3
LANES = 128

teacher_temp = 0.07
student_temp = 0.1
epsilon = 1e-06

teacher_power = math.log2(math.e) / teacher_temp
student_power = math.log2(math.e) / student_temp

ROWS = ("y", "z")
PROTOS = ("x", "core")

f32 = jnp.float32
bf16 = jnp.bfloat16


def params(mib):
    return pltpu.CompilerParams(vmem_limit_bytes=mib * 2**20)


def spread(value, axes):
    return lax.all_to_all(value, axes, 0, 0, tiled=True)


def work(flops, moved, powers=0):
    return pl.CostEstimate(flops=int(flops), bytes_accessed=int(moved), transcendentals=int(powers))


def in_hbm(value):
    return pltpu.with_memory_space_constraint(value, pltpu.HBM)


def nt_dot(a, b):
    return lax.dot_general(a, b, (((1,), (1,)), ((), ())), preferred_element_type=f32)


def unit_rows(values):
    length = jnp.sqrt(jnp.sum(values * values, axis=-1, keepdims=True) + epsilon)
    return (values / length, length)


def directions(values):
    values = values.astype(f32)
    return (values * lax.rsqrt(jnp.sum(values * values, axis=-1, keepdims=True) + epsilon)).astype(bf16)


def to_column(row):
    return jnp.broadcast_to(row, (LANES, LANES)).T


def fill_columns(rows, tile_ref):
    for k in range(rows.shape[0]):
        tile_ref[k * LANES : (k + 1) * LANES, :] = to_column(rows[k : k + 1, :])


def lane_totals(tile):
    parts = [
        jnp.sum(tile[k * LANES : (k + 1) * LANES, :].T, axis=0, keepdims=True)
        for k in range(tile.shape[0] // LANES)
    ]
    return jnp.concatenate(parts, axis=0)


def select_body(place_ref, teacher_ref, student_ref, order_ref, units_ref, length_ref, mine_ref):
    images, patches, _ = teacher_ref.shape
    for image in range(images):
        chosen = order_ref[image : image + 1, :MASKED]
        place = lax.broadcasted_iota(jnp.int32, (patches, MASKED), 0)
        onehot = jnp.where(place == chosen, 1.0, 0.0).astype(bf16)

        def pick(ref):
            return lax.dot_general(
                onehot, ref[image], (((0,), (0,)), ((), ())), preferred_element_type=f32
            )

        rows = slice(image * MASKED, (image + 1) * MASKED)
        teacher = unit_rows(pick(teacher_ref))[0]
        student, length_ref[rows, :] = unit_rows(pick(student_ref))
        units_ref[rows, :D] = teacher
        units_ref[rows, D:] = student
        mine_ref[rows, :] = jnp.where(place_ref[3] == 0, teacher, student)


def select_tokens(place, teacher_patches, student_patches, mask_order):
    tokens = teacher_patches.shape[0] * MASKED
    return pl.pallas_call(
        select_body,
        in_specs=[pl.BlockSpec(memory_space=pltpu.SMEM)]
        + [pl.BlockSpec(memory_space=pltpu.VMEM)] * 3,
        out_specs=[pl.BlockSpec(memory_space=pltpu.VMEM)] * 3,
        out_shape=[
            pltpu.HBM((tokens, 2 * D), f32),
            pltpu.HBM((tokens, 1), f32),
            pltpu.HBM((tokens, D), f32),
        ],
        compiler_params=params(8),
        name="select",
    )(place, in_hbm(teacher_patches), in_hbm(student_patches), in_hbm(mask_order))


def lane_rows(row):
    parts = [row[:, j * LANES : (j + 1) * LANES] for j in range(row.shape[1] // LANES)]
    return jnp.concatenate(parts, axis=0)


def chunks(tokens):
    return [slice(c, c + LANES) for c in range(0, tokens, LANES)]


FETCHES = 8
WIDE = 256


def fetch(protos_ref, buffer_ref, sems, i):
    size = buffer_ref.shape[0] // FETCHES
    rows = pl.ds(pl.multiple_of(i * size, size), size)
    return pltpu.make_async_copy(protos_ref.at[rows, :], buffer_ref.at[rows, :], sems.at[i])


def fetch_all(units_ref, column, unit_ref, protos_ref, buffer_ref, sems):
    units = pltpu.make_async_copy(
        units_ref.at[:, pl.ds(column, D)], unit_ref, sems.at[FETCHES]
    )
    units.start()
    for i in range(FETCHES):
        fetch(protos_ref, buffer_ref, sems, i).start()
    units.wait()


def energy_body(
    place_ref, units_ref, *refs
):
    piece_refs, (protos_ref, energy_ref, sums_ref, cast_ref, weights_ref, total_ref) = refs[:8], refs[8:]
    own = units_ref.shape[0]
    tokens = cast_ref.shape[0]

    def rows_of(slot, start, size):
        return pl.ds(pl.multiple_of(place_ref[4 + slot] * own + start, size), size)

    cast_ref[rows_of(0, 0, own), :] = units_ref[...].astype(bf16)
    places = [(1, 0, own), (3, 0, own), (2, 0, own // 2), (2, own // 2, own // 2)]
    for core in range(2):

        @pl.when(place_ref[3] == core)
        def _(core=core):
            for i, ref in enumerate(piece_refs):
                kind = core if i < 4 else 1 - core
                cast_ref[rows_of(*places[i % 4]), kind * D : (kind + 1) * D] = ref[...].astype(bf16)

    weights_ref[...] = directions(protos_ref[...])
    total_ref[...] = jnp.zeros_like(total_ref)
    size = 512
    parts = [slice(c, c + size) for c in range(0, weights_ref.shape[0], size)]

    def step(i, carry):
        chunk = cast_ref[pl.ds(pl.multiple_of(i * WIDE, WIDE), WIDE), :][:, :D]
        logits = nt_dot(weights_ref[parts[0], :], chunk)
        for k, part in enumerate(parts):
            following = nt_dot(weights_ref[parts[k + 1], :], chunk) if k + 1 < len(parts) else None
            energy = jnp.exp2(logits * teacher_power)
            total = total_ref[part, :]
            for j in range(WIDE // LANES):
                tile = energy[:, j * LANES : (j + 1) * LANES]
                energy_ref[i * (WIDE // LANES) + j, part, :] = tile.astype(bf16)
                total = total + tile
            total_ref[part, :] = total
            logits = following
        return carry

    lax.fori_loop(0, tokens // WIDE, step, 0)
    totals = lane_totals(total_ref[...])
    for copy in range(sums_ref.shape[0]):
        sums_ref[copy] = totals


def fixed(*shape):
    return pl.BlockSpec(shape, lambda i: (0,) * len(shape))


def left(tokens):
    return pl.BlockSpec((tokens, D), lambda *i: (0, 0))


def right(tokens):
    return pl.BlockSpec((tokens, D), lambda *i: (0, 1))


def energy_of(place, units, pieces, protos, share, copies):
    own = units.shape[0]
    tokens = own * 4
    direct = pl.BlockSpec(memory_space=pltpu.VMEM)
    return pl.pallas_call(
        energy_body,
        grid_spec=pltpu.PrefetchScalarGridSpec(
            num_scalar_prefetch=1,
            grid=(1,),
            in_specs=[pl.BlockSpec(units.shape, lambda i, p: (0, 0))]
            + [pl.BlockSpec(piece.shape, lambda i, p: (0, 0)) for piece in pieces]
            + [pl.BlockSpec((share, D), lambda i, p: (p[0], 0))],
            out_specs=[
                direct,
                pl.BlockSpec((copies, share // LANES, LANES), lambda i, p: (0, 0, 0)),
                pl.BlockSpec((tokens, 2 * D), lambda i, p: (0, 0)),
            ],
            scratch_shapes=[pltpu.VMEM((share, D), bf16), pltpu.VMEM((share, LANES), f32)],
        ),
        out_shape=[
            pltpu.VMEM((tokens // LANES, share, LANES), bf16),
            jax.ShapeDtypeStruct((copies, share // LANES, LANES), f32),
            pltpu.HBM((tokens, 2 * D), bf16),
        ],
        compiler_params=params(24),
        cost_estimate=work(4 * tokens * share * D, 8 * 2**20, tokens * share),
        name="energy",
    )(place, in_hbm(units), *pieces, in_hbm(protos))


def student_body(units_ref, protos_ref, sums_ref, unit_ref, cast_ref, total_ref, buffer_ref, sems):
    size = buffer_ref.shape[0] // FETCHES
    fetch_all(units_ref, D, unit_ref, protos_ref, buffer_ref, sems)
    cast_ref[...] = unit_ref[...].astype(bf16)
    total_ref[...] = jnp.zeros_like(total_ref)

    def step(i, carry):
        fetch(protos_ref, buffer_ref, sems, i).wait()
        total = total_ref[...]

        def logits_of(part):
            rows = pl.ds(pl.multiple_of(i * size + part * WIDE, WIDE), WIDE)
            return nt_dot(cast_ref[...], directions(buffer_ref[rows, :]))

        parts = size // WIDE
        logits = logits_of(0)
        for part in range(parts):
            following = logits_of(part + 1) if part + 1 < parts else None
            values = jnp.exp2(logits * student_power)
            logits = following
            for j in range(WIDE // LANES):
                total = total + values[:, j * LANES : (j + 1) * LANES]
        total_ref[...] = total
        return carry

    lax.fori_loop(0, FETCHES, step, 0)
    sums_ref[...] = lane_totals(total_ref[...])


def student_sums(units, protos):
    tokens, count = units.shape[0], protos.shape[0]
    return pl.pallas_call(
        student_body,
        in_specs=[pl.BlockSpec(memory_space=pl.ANY)] * 2,
        out_specs=pl.BlockSpec(memory_space=pltpu.VMEM),
        out_shape=jax.ShapeDtypeStruct((tokens // LANES, LANES), f32),
        scratch_shapes=[
            pltpu.VMEM((tokens, D), f32),
            pltpu.VMEM((tokens, D), bf16),
            pltpu.VMEM((tokens, LANES), f32),
            pltpu.VMEM((count, D), bf16),
            pltpu.SemaphoreType.DMA((FETCHES + 1,)),
        ],
        compiler_params=params(16),
        cost_estimate=work(4 * tokens * count * D, 8 * 2**20, tokens * count),
        name="student",
    )(in_hbm(units), in_hbm(protos))


def right(tokens):
    return pl.BlockSpec((tokens, D), lambda *i: (0, 1))


def row_body(energy_ref, pieces_ref, *refs):
    norm_refs, (scale_ref, sums_ref, tile_ref) = refs[:-3], refs[-3:]
    scale_ref[...] = 1.0 / jnp.sum(pieces_ref[...], axis=0)
    fill_columns(scale_ref[...], tile_ref)
    tiles, protos, _ = energy_ref.shape
    size = 512
    totals = []
    for j in range(tiles):
        total = jnp.zeros((1, LANES), f32)
        for start in range(0, protos, size):
            part = slice(start, start + size)
            energy = energy_ref[j, part, :].astype(f32)
            total = total + jnp.sum(energy * tile_ref[part, :], axis=0, keepdims=True)
        totals.append(total)
    for ref in norm_refs:
        totals += [ref[...], jnp.zeros_like(ref)]
    totals = jnp.concatenate(totals, axis=0)
    for copy in range(sums_ref.shape[0]):
        sums_ref[copy] = totals


def row_sums(energy, pieces, copies, norm_part=()):
    tiles, protos, _ = energy.shape
    whole = pl.BlockSpec(memory_space=pltpu.VMEM)
    rows = tiles + 2 * sum(part.shape[0] for part in norm_part)
    return pl.pallas_call(
        row_body,
        in_specs=[whole] * (2 + len(norm_part)),
        out_specs=[whole] * 2,
        out_shape=[
            jax.ShapeDtypeStruct((protos // LANES, LANES), f32),
            jax.ShapeDtypeStruct((copies, rows, LANES), f32),
        ],
        scratch_shapes=[pltpu.VMEM((protos, LANES), f32)],
        compiler_params=params(12),
        cost_estimate=work(2 * energy.size, 0),
        name="row_sums",
    )(energy, pieces, *norm_part)


def column_body(energy_ref, pieces_ref, sums_ref, scale_ref):
    tiles, protos, _ = energy_ref.shape
    scale_ref[...] = 1.0 / jnp.sum(pieces_ref[...], axis=0)

    def step(k, carry):
        rows = pl.ds(pl.multiple_of(k * LANES, LANES), LANES)
        total = jnp.zeros((LANES, LANES), f32)
        for j in range(tiles):
            total = total + energy_ref[j, rows, :].astype(f32) * scale_ref[j : j + 1, :]
        sums_ref[0, pl.ds(k, 1), :] = lane_totals(total)
        return carry

    lax.fori_loop(0, protos // LANES, step, 0, unroll=4)
    for copy in range(1, sums_ref.shape[0]):
        sums_ref[copy] = sums_ref[0]


def column_sums(energy, pieces, copies):
    tiles, protos, _ = energy.shape
    whole = pl.BlockSpec(memory_space=pltpu.VMEM)
    return pl.pallas_call(
        column_body,
        in_specs=[whole] * 2,
        out_specs=whole,
        out_shape=jax.ShapeDtypeStruct((copies, protos // LANES, LANES), f32),
        scratch_shapes=[pltpu.VMEM((tiles, LANES), f32)],
        compiler_params=params(12),
        cost_estimate=work(2 * energy.size, 0),
        name="column_sums",
    )(energy, pieces)


LEFT_PLACE = [4, 5, 6, 7, 3, 2, 1, 0]
RIGHT_PLACE = [4, 0, 1, 2, 3, 7, 6, 5]


def collect(send, keep, offset):
    n = lax.axis_size("z")
    way = [1 if (z + offset) % 2 else -1 for z in range(n)]
    got = lax.ppermute(send, "z", [(z, (z - way[z]) % n) for z in range(n)])
    return keep[0] + got[0], keep[1] + got[1], keep[2:] + got[2:]


def pass_on(sums, offset):
    n = lax.axis_size("z")
    way = [1 if (z + offset) % 2 else -1 for z in range(n)]
    own, following, far = sums
    got = lax.ppermute(far, "z", [(z, (z + 2 * way[z]) % n) for z in range(n)])
    return own + got[0], following + got[1]


def deliver(sums, offset):
    n = lax.axis_size("z")
    way = [1 if (z + offset) % 2 else -1 for z in range(n)]
    own, following = sums
    return [own, lax.ppermute(following, "z", [(z, (z + way[z]) % n) for z in range(n)])]


def gradient_body(
    table_ref,
    units_ref,
    energy_ref,
    pieces_ref,
    sw_first_ref,
    sw_second_ref,
    scale_ref,
    send_left_ref,
    send_right_ref,
    keep_left_ref,
    keep_right_ref,
    feature_send_ref,
    feature_keep_ref,
    r_ref,
    n_ref,
    total_ref,
    feature_ref,
    stage_ref,
    sems,
    feature_sems,
):
    step = pl.program_id(0)
    tiles = energy_ref.shape[0]
    groups = pieces_ref.shape[0]
    own = tiles // groups

    @pl.when(step == 0)
    def _():
        scale = (1.0 / student_temp) / jnp.sum(pieces_ref[:, :, :tiles, :], axis=(0, 1))
        for k in range(tiles):
            r_ref[:, k * LANES : (k + 1) * LANES] = scale[k : k + 1, :]
        for group in range(groups):
            total = jnp.sum(pieces_ref[group, :, tiles : tiles + own, :], axis=0)
            inverse = (1.0 / student_temp) / total
            for k in range(own):
                lanes = slice((group * own + k) * LANES, (group * own + k + 1) * LANES)
                n_ref[:, lanes] = inverse[k : k + 1, :]
        feature_ref[...] = jnp.zeros_like(feature_ref)

    both = lambda first, second: jnp.concatenate([first, second], axis=0)
    block = sw_first_ref.shape[0]
    sw = both(directions(sw_first_ref[...]), directions(sw_second_ref[...]))
    local = [table_ref[3, 2 * step], table_ref[3, 2 * step + 1]]
    here = [pl.ds(pl.multiple_of(place * block, block), block) for place in local]
    columns = []
    for place in local:
        for k in range(block // LANES):
            row = scale_ref[pl.ds(place * (block // LANES) + k, 1), :]
            columns.append(to_column(row))
    col_scale = jnp.concatenate(columns, axis=0)

    def logits_of(part):
        return nt_dot(sw, units_ref[part, D:])

    parts = [slice(c, c + WIDE) for c in range(0, units_ref.shape[0], WIDE)]

    def feature_copies(i):
        size = feature_send_ref.shape[1]
        found = []
        for at in range(i * WIDE // size, (i + 1) * WIDE // size):
            source, sem = feature_ref.at[pl.ds(at * size, size), :], feature_sems.at[at]
            kept = pltpu.make_async_copy(source, feature_keep_ref.at[at // 2], sem)
            sent = pltpu.make_async_copy(source, feature_send_ref.at[at // 2], sem)
            found += [(table_ref[4, 0] == at % 2, kept), (table_ref[4, 0] != at % 2, sent)]
        return found

    logits = logits_of(parts[0])
    for i, part in enumerate(parts):
        following = logits_of(parts[i + 1]) if i + 1 < len(parts) else None
        grads = []
        for j in range(WIDE // LANES):
            tile = i * (WIDE // LANES) + j
            lanes = slice(tile * LANES, (tile + 1) * LANES)
            energy = both(energy_ref[tile, here[0], :], energy_ref[tile, here[1], :]).astype(f32)
            probs = jnp.exp2(logits[:, j * LANES : (j + 1) * LANES] * student_power) * n_ref[:, lanes]
            grads.append((probs - energy * r_ref[:, lanes] * col_scale).astype(bf16))
        logit_grad = jnp.concatenate(grads, axis=1)
        added = jnp.dot(logit_grad, units_ref[part, D:], preferred_element_type=f32)
        total_ref[...] = added if i == 0 else total_ref[...] + added
        feature_ref[part, :] += lax.dot_general(
            logit_grad, sw, (((0,), (0,)), ((), ())), preferred_element_type=f32
        )
        for wanted, copy in feature_copies(i):
            pl.when(jnp.logical_and(step == pl.num_programs(0) - 1, wanted))(copy.start)
        logits = following

    def copies(which, at):
        found = []
        for half, (sent_ref, kept_ref) in enumerate(
            ((send_left_ref, keep_left_ref), (send_right_ref, keep_right_ref))
        ):
            block_at = 2 * at + which
            place = table_ref[1 + half, block_at]
            source, sem = stage_ref.at[half, block_at], sems.at[half, block_at]
            sent = pltpu.make_async_copy(source, sent_ref.at[jnp.minimum(place, 3)], sem)
            kept = pltpu.make_async_copy(source, kept_ref.at[jnp.maximum(place - 4, 0)], sem)
            found += [(place < 4, sent), (place >= 4, kept)]
        return found

    for which in range(2):
        rows_here = slice(which * block, (which + 1) * block)
        for half in range(2):
            columns_here = slice(half * (D // 2), (half + 1) * (D // 2))
            stage_ref[half, 2 * step + which] = total_ref[rows_here, columns_here]
        for wanted, copy in copies(which, step):
            pl.when(wanted)(copy.start)

    @pl.when(step == pl.num_programs(0) - 1)
    def _():
        for i in range(len(parts)):
            for wanted, copy in feature_copies(i):
                pl.when(wanted)(copy.wait)
        for at in range(stage_ref.shape[1] // 2):
            for which in range(2):
                for wanted, copy in copies(which, at):
                    pl.when(wanted)(copy.wait)


def block_table(y, z, core):
    blocks = len(LEFT_PLACE)
    way = jnp.where(z % 2 == 1, 1, -1)
    local = (z + way * jnp.arange(blocks) + blocks) % blocks
    cores = jnp.full((blocks,), core)
    table = [y * blocks + local, jnp.array(LEFT_PLACE), jnp.array(RIGHT_PLACE), local, cores]
    return jnp.stack(table).astype(jnp.int32)


def gradients(table, units_all, energy, pieces, student_protos, scale, shares):
    tiles, share, _ = energy.shape
    tokens = units_all.shape[0]
    block = 256
    blocks = share // block
    whole = lambda *shape: pl.BlockSpec(shape, lambda i, p: (0,) * len(shape))
    first = pl.BlockSpec((block, D), lambda i, p: (p[0, 2 * i], 0))
    second = pl.BlockSpec((block, D), lambda i, p: (p[0, 2 * i + 1], 0))
    direct = pl.BlockSpec(memory_space=pltpu.VMEM)
    half = pltpu.HBM((blocks // 2, block, D // 2), f32)
    return pl.pallas_call(
        gradient_body,
        grid_spec=pltpu.PrefetchScalarGridSpec(
            num_scalar_prefetch=1,
            grid=(blocks // 2,),
            in_specs=[
                whole(tokens, 2 * D),
                direct,
                whole(*pieces.shape),
                first,
                second,
                whole(*scale.shape),
            ],
            out_specs=[pl.BlockSpec(memory_space=pl.ANY)] * 6,
            scratch_shapes=[
                pltpu.VMEM((1, tokens), f32),
                pltpu.VMEM((1, tokens), f32),
                pltpu.VMEM((2 * block, D), f32),
                pltpu.VMEM((tokens, D), f32),
                pltpu.VMEM((2, blocks, block, D // 2), f32),
                pltpu.SemaphoreType.DMA((2, blocks)),
                pltpu.SemaphoreType.DMA((shares,)),
            ],
        ),
        out_shape=[half] * 4 + [pltpu.HBM((shares // 2, tokens // shares, D), f32)] * 2,
        compiler_params=params(24),
        cost_estimate=work(8 * tokens * share * D, 8 * 2**20, tokens * share),
        name="gradients",
    )(
        table,
        in_hbm(units_all),
        energy,
        pieces,
        in_hbm(student_protos),
        in_hbm(student_protos),
        scale,
    )


def project(total, unit, length):
    return (total - unit * jnp.sum(unit * total, axis=-1, keepdims=True)) / length


def student_end_body(place_ref, pieces_ref, unit_ref, length_ref, out_ref):
    result = project(jnp.sum(pieces_ref[...], axis=0), unit_ref[...], length_ref[...])
    for copy in range(out_ref.shape[0]):
        out_ref[copy] = result


def student_end(place, pieces, units, length, copies):
    _, rows, _ = pieces.shape
    return pl.pallas_call(
        student_end_body,
        grid_spec=pltpu.PrefetchScalarGridSpec(
            num_scalar_prefetch=1,
            grid=(1,),
            in_specs=[
                pl.BlockSpec(pieces.shape, lambda i, p: (0, 0, 0)),
                pl.BlockSpec((rows, D), lambda i, p: (p[2], 1)),
                pl.BlockSpec((rows, 1), lambda i, p: (p[2], 0)),
            ],
            out_specs=pl.BlockSpec((copies, rows, D), lambda i, p: (0, 0, 0)),
        ),
        out_shape=jax.ShapeDtypeStruct((copies, rows, D), f32),
        compiler_params=params(8),
        name="student_end",
    )(place, pieces, in_hbm(units), in_hbm(length))


def proto_end_body(place_ref, *refs):
    piece_refs, (protos_ref, out_ref) = refs[:-2], refs[-2:]
    unit, length = unit_rows(protos_ref[...].astype(f32))
    half = len(piece_refs) // 2
    sums = []
    for group in (piece_refs[:half], piece_refs[half:]):
        total = group[0][...]
        for ref in group[1:]:
            total = total + ref[...]
        sums.append(total)
    out_ref[...] = project(jnp.concatenate(sums, axis=1), unit, length)


def proto_end(place, pieces, protos):
    rows, width = pieces[0].shape
    return pl.pallas_call(
        proto_end_body,
        grid_spec=pltpu.PrefetchScalarGridSpec(
            num_scalar_prefetch=1,
            grid=(1,),
            in_specs=[pl.BlockSpec((rows, width), lambda i, p: (0, 0))] * len(pieces)
            + [pl.BlockSpec((rows, D), lambda i, p: (p[1], 0))],
            out_specs=pl.BlockSpec((rows, D), lambda i, p: (0, 0)),
        ),
        out_shape=jax.ShapeDtypeStruct((rows, D), f32),
        compiler_params=params(8),
        name="proto_end",
    )(place, *pieces, in_hbm(protos))


def on_device(teacher_patches, student_patches, mask_order, teacher_protos, student_protos):
    y_size, z_size = lax.axis_size("y"), lax.axis_size("z")
    proto_size = lax.axis_size("x") * lax.axis_size("core")
    y, z = lax.axis_index("y"), lax.axis_index("z")
    others = [(y - step + y_size) % y_size for step in range(y_size)]
    place = [y, y * z_size + z, lax.axis_index(PROTOS), lax.axis_index("core")] + others
    place, table = lax.optimization_barrier(
        (jnp.stack(place).astype(jnp.int32), block_table(y, z, lax.axis_index("core")))
    )
    share = teacher_protos.shape[0] // y_size

    units, student_length, mine = select_tokens(
        place, teacher_patches, student_patches, mask_order
    )
    from_y = lambda value, step: lax.ppermute(
        value, "y", [(i, (i + step) % y_size) for i in range(y_size)]
    )
    from_core = lambda value: lax.ppermute(value, "core", [(0, 1), (1, 0)])
    half = mine.shape[0] // 2
    first, third = from_y(mine, 1), from_y(mine, 3)
    norm_part = student_sums(units, student_protos)
    norm_part, first, third = lax.optimization_barrier((norm_part, first, third))
    got = [first, third, from_y(first[:half], 1), from_y(third[half:], 3)]
    got = got + [from_core(piece) for piece in got]

    rows = ("y",) + PROTOS
    peers = y_size * proto_size
    energy, sums, units_all = energy_of(place, units, got, teacher_protos, share, z_size)
    for sweep in range(ITERS):
        if sweep > 0:
            sums = column_sums(energy, pieces, z_size)
        norms = (norm_part,) if sweep == ITERS - 1 else ()
        col_scale, row_part = row_sums(energy, spread(sums, "z"), peers, norms)
        pieces = spread(row_part, rows)
    pieces = pieces.reshape((y_size, proto_size) + pieces.shape[1:])

    send_left, send_right, keep_left, keep_right, feature_send, feature_keep = gradients(
        table, units_all, energy, pieces, student_protos, col_scale, peers
    )
    feature_part = feature_keep + from_core(feature_send)
    feature_part, keep_left, keep_right = lax.optimization_barrier(
        (feature_part, keep_left, keep_right)
    )
    left = pass_on(collect(send_left, keep_left, 0), 0)
    right_half = pass_on(collect(send_right, keep_right, 1), 1)
    feature_pieces = spread(feature_part, ("y", "x"))
    feature_pieces, left, right_half = lax.optimization_barrier((feature_pieces, left, right_half))
    left, right_half = deliver(left, 0), deliver(right_half, 1)
    result = student_end(place, feature_pieces, units, student_length, proto_size)
    result = spread(result, PROTOS)
    grad_protos = proto_end(place, left + right_half, student_protos)
    return (result.reshape(-1, MASKED, D), grad_protos)


def solution(mesh):
    fine = Mesh(mesh.devices.reshape(4, 8, 4, 2), ("y", "z", "x", "core"))
    return jax.shard_map(
        on_device,
        mesh=fine,
        in_specs=(
            P(ROWS, None, None),
            P(ROWS, None, None),
            P(ROWS, None),
            P(PROTOS, None),
            P(PROTOS, None),
        ),
        out_specs=(P(ROWS, None, None), P(PROTOS + ROWS, None)),
        check_vma=False,
    )
```

```python
import functools
import math

import jax
import jax.numpy as jnp
from jax import lax
from jax.experimental import pallas as pl
from jax.experimental.pallas import tpu as pltpu
from jax.sharding import Mesh, PartitionSpec as P

D = 256
MASKED = 128
ITERS = 3
LANES = 128

teacher_temp = 0.07
student_temp = 0.1
epsilon = 1e-06

teacher_power = math.log2(math.e) / teacher_temp
student_power = math.log2(math.e) / student_temp

ROWS = ("y", "z")
PROTOS = ("x", "core")

f32 = jnp.float32
bf16 = jnp.bfloat16


def params(mib):
    return pltpu.CompilerParams(vmem_limit_bytes=mib * 2**20)


def spread(value, axes):
    return lax.all_to_all(value, axes, 0, 0, tiled=True)


def work(flops, moved, powers=0):
    return pl.CostEstimate(flops=int(flops), bytes_accessed=int(moved), transcendentals=int(powers))


def in_hbm(value):
    return pltpu.with_memory_space_constraint(value, pltpu.HBM)


def nt_dot(a, b):
    return lax.dot_general(a, b, (((1,), (1,)), ((), ())), preferred_element_type=f32)


def unit_rows(values):
    length = jnp.sqrt(jnp.sum(values * values, axis=-1, keepdims=True) + epsilon)
    return (values / length, length)


def directions(values):
    values = values.astype(f32)
    return (values * lax.rsqrt(jnp.sum(values * values, axis=-1, keepdims=True) + epsilon)).astype(bf16)


def to_column(row):
    return jnp.broadcast_to(row, (LANES, LANES)).T


def fill_columns(rows, tile_ref):
    for k in range(rows.shape[0]):
        tile_ref[k * LANES : (k + 1) * LANES, :] = to_column(rows[k : k + 1, :])


def lane_totals(tile):
    parts = [
        jnp.sum(tile[k * LANES : (k + 1) * LANES, :].T, axis=0, keepdims=True)
        for k in range(tile.shape[0] // LANES)
    ]
    return jnp.concatenate(parts, axis=0)


def select_body(core_ref, teacher_ref, student_ref, order_ref, units_ref, length_ref, mine_ref):
    images, patches, _ = teacher_ref.shape
    for image in range(images):
        chosen = order_ref[image : image + 1, :MASKED]
        place = lax.broadcasted_iota(jnp.int32, (patches, MASKED), 0)
        onehot = jnp.where(place == chosen, 1.0, 0.0).astype(bf16)

        def pick(ref):
            return lax.dot_general(
                onehot, ref[image], (((0,), (0,)), ((), ())), preferred_element_type=f32
            )

        rows = slice(image * MASKED, (image + 1) * MASKED)
        teacher = unit_rows(pick(teacher_ref))[0]
        student, length_ref[rows, :] = unit_rows(pick(student_ref))
        units_ref[rows, :D] = teacher
        units_ref[rows, D:] = student
        mine_ref[rows, :] = jnp.where(core_ref[0] == 0, teacher, student)


def select_tokens(core, teacher_patches, student_patches, mask_order):
    tokens = teacher_patches.shape[0] * MASKED
    return pl.pallas_call(
        select_body,
        in_specs=[pl.BlockSpec(memory_space=pltpu.SMEM)]
        + [pl.BlockSpec(memory_space=pltpu.VMEM)] * 3,
        out_specs=[pl.BlockSpec(memory_space=pltpu.VMEM)] * 3,
        out_shape=[
            pltpu.HBM((tokens, 2 * D), f32),
            pltpu.HBM((tokens, 1), f32),
            pltpu.HBM((tokens, D), f32),
        ],
        compiler_params=params(8),
        name="select",
    )(core, in_hbm(teacher_patches), in_hbm(student_patches), in_hbm(mask_order))


def lane_rows(row):
    parts = [row[:, j * LANES : (j + 1) * LANES] for j in range(row.shape[1] // LANES)]
    return jnp.concatenate(parts, axis=0)


def chunks(tokens):
    return [slice(c, c + LANES) for c in range(0, tokens, LANES)]


FETCHES = 8
WIDE = 256


def fetch(protos_ref, buffer_ref, sems, i):
    size = buffer_ref.shape[0] // FETCHES
    rows = pl.ds(pl.multiple_of(i * size, size), size)
    return pltpu.make_async_copy(protos_ref.at[rows, :], buffer_ref.at[rows, :], sems.at[i])


def fetch_all(units_ref, column, unit_ref, protos_ref, buffer_ref, sems):
    units = pltpu.make_async_copy(
        units_ref.at[:, pl.ds(column, D)], unit_ref, sems.at[FETCHES]
    )
    units.start()
    for i in range(FETCHES):
        fetch(protos_ref, buffer_ref, sems, i).start()
    units.wait()


STEPS = [0, 1, 3, 2]


def energy_body(layout, before, place_ref, *refs):
    piece_refs, refs = refs[: len(layout)], refs[len(layout) :]
    protos_ref, refs = refs[0], refs[1:]
    before_refs, refs = refs[:before], refs[before:]
    energy_ref, sums_ref, cast_ref, weights_ref, total_ref = refs
    for ref, (rows, kind) in zip(piece_refs, layout):
        if kind is None:
            cast_ref[rows, :] = ref[...].astype(bf16)
    for core in range(2):

        @pl.when(place_ref[3] == core)
        def _(core=core):
            for ref, (rows, kind) in zip(piece_refs, layout):
                if kind is not None:
                    half = core if kind == 0 else 1 - core
                    cast_ref[rows, half * D : (half + 1) * D] = ref[...].astype(bf16)

    weights_ref[...] = directions(protos_ref[...])
    total_ref[...] = jnp.zeros_like(total_ref)
    size = 512
    parts = [slice(c, c + size) for c in range(0, weights_ref.shape[0], size)]

    def step(i, carry):
        chunk = cast_ref[pl.ds(pl.multiple_of(i * WIDE, WIDE), WIDE), :][:, :D]
        logits = nt_dot(weights_ref[parts[0], :], chunk)
        for k, part in enumerate(parts):
            following = nt_dot(weights_ref[parts[k + 1], :], chunk) if k + 1 < len(parts) else None
            energy = jnp.exp2(logits * teacher_power)
            total = total_ref[part, :]
            for j in range(WIDE // LANES):
                tile = energy[:, j * LANES : (j + 1) * LANES]
                energy_ref[i * (WIDE // LANES) + j, part, :] = tile.astype(bf16)
                total = total + tile
            total_ref[part, :] = total
            logits = following
        return carry

    lax.fori_loop(0, cast_ref.shape[0] // WIDE, step, 0)
    totals = lane_totals(total_ref[...])
    for ref in before_refs:
        totals = totals + ref[0]
    for copy in range(sums_ref.shape[0]):
        sums_ref[copy] = totals


def fixed(*shape):
    return pl.BlockSpec(shape, lambda i: (0,) * len(shape))


def left(tokens):
    return pl.BlockSpec((tokens, D), lambda *i: (0, 0))


def right(tokens):
    return pl.BlockSpec((tokens, D), lambda *i: (0, 1))


def energy_of(place, pieces, layout, tokens, protos, share, copies, before=()):
    direct = pl.BlockSpec(memory_space=pltpu.VMEM)
    whole = lambda value: pl.BlockSpec(value.shape, lambda i, p: (0,) * value.ndim)
    return pl.pallas_call(
        functools.partial(energy_body, layout, len(before)),
        grid_spec=pltpu.PrefetchScalarGridSpec(
            num_scalar_prefetch=1,
            grid=(1,),
            in_specs=[whole(piece) for piece in pieces]
            + [pl.BlockSpec((share, D), lambda i, p: (p[0], 0))]
            + [whole(value) for value in before],
            out_specs=[
                direct,
                pl.BlockSpec((copies, share // LANES, LANES), lambda i, p: (0, 0, 0)),
                pl.BlockSpec((tokens, 2 * D), lambda i, p: (0, 0)),
            ],
            scratch_shapes=[pltpu.VMEM((share, D), bf16), pltpu.VMEM((share, LANES), f32)],
        ),
        out_shape=[
            pltpu.VMEM((tokens // LANES, share, LANES), bf16),
            jax.ShapeDtypeStruct((copies, share // LANES, LANES), f32),
            pltpu.HBM((tokens, 2 * D), bf16),
        ],
        compiler_params=params(20),
        cost_estimate=work(4 * tokens * share * D, 8 * 2**20, tokens * share),
        name="energy",
    )(place, *pieces, in_hbm(protos), *before)


def student_body(units_ref, protos_ref, sums_ref, unit_ref, cast_ref, total_ref, buffer_ref, sems):
    size = buffer_ref.shape[0] // FETCHES
    fetch_all(units_ref, D, unit_ref, protos_ref, buffer_ref, sems)
    cast_ref[...] = unit_ref[...].astype(bf16)
    total_ref[...] = jnp.zeros_like(total_ref)

    def step(i, carry):
        fetch(protos_ref, buffer_ref, sems, i).wait()
        total = total_ref[...]

        def logits_of(part):
            rows = pl.ds(pl.multiple_of(i * size + part * WIDE, WIDE), WIDE)
            return nt_dot(cast_ref[...], directions(buffer_ref[rows, :]))

        parts = size // WIDE
        logits = logits_of(0)
        for part in range(parts):
            following = logits_of(part + 1) if part + 1 < parts else None
            values = jnp.exp2(logits * student_power)
            logits = following
            for j in range(WIDE // LANES):
                total = total + values[:, j * LANES : (j + 1) * LANES]
        total_ref[...] = total
        return carry

    lax.fori_loop(0, FETCHES, step, 0)
    sums_ref[...] = lane_totals(total_ref[...])


def student_sums(units, protos):
    tokens, count = units.shape[0], protos.shape[0]
    return pl.pallas_call(
        student_body,
        in_specs=[pl.BlockSpec(memory_space=pl.ANY)] * 2,
        out_specs=pl.BlockSpec(memory_space=pltpu.VMEM),
        out_shape=jax.ShapeDtypeStruct((tokens // LANES, LANES), f32),
        scratch_shapes=[
            pltpu.VMEM((tokens, D), f32),
            pltpu.VMEM((tokens, D), bf16),
            pltpu.VMEM((tokens, LANES), f32),
            pltpu.VMEM((count, D), bf16),
            pltpu.SemaphoreType.DMA((FETCHES + 1,)),
        ],
        compiler_params=params(16),
        cost_estimate=work(4 * tokens * count * D, 8 * 2**20, tokens * count),
        name="student",
    )(in_hbm(units), in_hbm(protos))


def right(tokens):
    return pl.BlockSpec((tokens, D), lambda *i: (0, 1))


def tiles_of(first_ref, second_ref):
    return [(ref, j) for ref in (first_ref, second_ref) for j in range(ref.shape[0])]


def row_at(place_ref, i, tiles):
    per_group = tiles // len(STEPS)
    return place_ref[4 + STEPS[i // per_group]] * per_group + i % per_group


def row_body(place_ref, first_ref, second_ref, pieces_ref, *refs):
    norm_refs, (scale_ref, sums_ref, tile_ref, rows_ref) = refs[:-4], refs[-4:]
    scale_ref[...] = 1.0 / jnp.sum(pieces_ref[...], axis=0)
    fill_columns(scale_ref[...], tile_ref)
    tiles = tiles_of(first_ref, second_ref)
    size = 512
    for i, (ref, j) in enumerate(tiles):
        total = jnp.zeros((1, LANES), f32)
        for start in range(0, ref.shape[1], size):
            part = slice(start, start + size)
            energy = ref[j, part, :].astype(f32)
            total = total + jnp.sum(energy * tile_ref[part, :], axis=0, keepdims=True)
        rows_ref[pl.ds(row_at(place_ref, i, len(tiles)), 1), :] = total
    for ref in norm_refs:
        rows_ref[len(tiles) :, :] = jnp.concatenate([ref[...], jnp.zeros_like(ref)], axis=0)
    rows = rows_ref[...]
    for copy in range(sums_ref.shape[0]):
        sums_ref[copy] = rows


def row_sums(place, energy, pieces, copies, norm_part=()):
    tiles = sum(part.shape[0] for part in energy)
    protos = energy[0].shape[1]
    whole = pl.BlockSpec(memory_space=pltpu.VMEM)
    rows = tiles + 2 * sum(part.shape[0] for part in norm_part)
    return pl.pallas_call(
        row_body,
        in_specs=[pl.BlockSpec(memory_space=pltpu.SMEM)] + [whole] * (3 + len(norm_part)),
        out_specs=[whole] * 2,
        out_shape=[
            jax.ShapeDtypeStruct((protos // LANES, LANES), f32),
            jax.ShapeDtypeStruct((copies, rows, LANES), f32),
        ],
        scratch_shapes=[pltpu.VMEM((protos, LANES), f32), pltpu.VMEM((rows, LANES), f32)],
        compiler_params=params(12),
        cost_estimate=work(2 * tiles * LANES * protos, 0),
        name="row_sums",
    )(place, *energy, pieces, *norm_part)


def column_body(place_ref, first_ref, second_ref, pieces_ref, sums_ref, scale_ref, rows_ref):
    tiles = tiles_of(first_ref, second_ref)
    rows_ref[...] = 1.0 / jnp.sum(pieces_ref[...], axis=0)
    for i in range(len(tiles)):
        scale_ref[i : i + 1, :] = rows_ref[pl.ds(row_at(place_ref, i, len(tiles)), 1), :]

    def step(k, carry):
        rows = pl.ds(pl.multiple_of(k * LANES, LANES), LANES)
        total = jnp.zeros((LANES, LANES), f32)
        for i, (ref, j) in enumerate(tiles):
            total = total + ref[j, rows, :].astype(f32) * scale_ref[i : i + 1, :]
        sums_ref[0, pl.ds(k, 1), :] = lane_totals(total)
        return carry

    lax.fori_loop(0, first_ref.shape[1] // LANES, step, 0, unroll=4)
    for copy in range(1, sums_ref.shape[0]):
        sums_ref[copy] = sums_ref[0]


def column_sums(place, energy, pieces, copies):
    tiles = sum(part.shape[0] for part in energy)
    protos = energy[0].shape[1]
    whole = pl.BlockSpec(memory_space=pltpu.VMEM)
    return pl.pallas_call(
        column_body,
        in_specs=[pl.BlockSpec(memory_space=pltpu.SMEM)] + [whole] * 3,
        out_specs=whole,
        out_shape=jax.ShapeDtypeStruct((copies, protos // LANES, LANES), f32),
        scratch_shapes=[pltpu.VMEM((tiles, LANES), f32)] * 2,
        compiler_params=params(12),
        cost_estimate=work(2 * tiles * LANES * protos, 0),
        name="column_sums",
    )(place, *energy, pieces)


LEFT_PLACE = [4, 5, 6, 7, 3, 2, 1, 0]
RIGHT_PLACE = [4, 0, 1, 2, 3, 7, 6, 5]


def collect(send, keep, offset):
    n = lax.axis_size("z")
    way = [1 if (z + offset) % 2 else -1 for z in range(n)]
    got = lax.ppermute(send, "z", [(z, (z - way[z]) % n) for z in range(n)])
    return keep[0] + got[0], keep[1] + got[1], keep[2:] + got[2:]


def pass_on(sums, offset):
    n = lax.axis_size("z")
    way = [1 if (z + offset) % 2 else -1 for z in range(n)]
    own, following, far = sums
    got = lax.ppermute(far, "z", [(z, (z + 2 * way[z]) % n) for z in range(n)])
    return own + got[0], following + got[1]


def deliver(sums, offset):
    n = lax.axis_size("z")
    way = [1 if (z + offset) % 2 else -1 for z in range(n)]
    own, following = sums
    return [own, lax.ppermute(following, "z", [(z, (z + way[z]) % n) for z in range(n)])]


def gradient_body(
    table_ref,
    units_first_ref,
    units_second_ref,
    energy_first_ref,
    energy_second_ref,
    pieces_ref,
    sw_first_ref,
    sw_second_ref,
    scale_ref,
    send_left_ref,
    send_right_ref,
    keep_left_ref,
    keep_right_ref,
    feature_send_ref,
    feature_keep_ref,
    r_ref,
    n_ref,
    total_ref,
    feature_ref,
    stage_ref,
    rows_ref,
    sems,
    feature_sems,
):
    step = pl.program_id(0)
    tiles = tiles_of(energy_first_ref, energy_second_ref)
    groups = pieces_ref.shape[0]
    own = len(tiles) // groups

    @pl.when(step == 0)
    def _():
        count = len(tiles)
        rows_ref[...] = (1.0 / student_temp) / jnp.sum(pieces_ref[:, :, :count, :], axis=(0, 1))
        for group in range(groups):
            slot = table_ref[5, group]
            total = jnp.sum(pieces_ref[slot][:, count : count + own, :], axis=0)
            inverse = (1.0 / student_temp) / total
            for k in range(own):
                lanes = slice((group * own + k) * LANES, (group * own + k + 1) * LANES)
                r_ref[:, lanes] = rows_ref[pl.ds(slot * own + k, 1), :]
                n_ref[:, lanes] = inverse[k : k + 1, :]
        feature_ref[...] = jnp.zeros_like(feature_ref)

    both = lambda first, second: jnp.concatenate([first, second], axis=0)
    block = sw_first_ref.shape[0]
    sw = both(directions(sw_first_ref[...]), directions(sw_second_ref[...]))
    local = [table_ref[3, 2 * step], table_ref[3, 2 * step + 1]]
    here = [pl.ds(pl.multiple_of(place * block, block), block) for place in local]
    columns = []
    for place in local:
        for k in range(block // LANES):
            row = scale_ref[pl.ds(place * (block // LANES) + k, 1), :]
            columns.append(to_column(row))
    col_scale = jnp.concatenate(columns, axis=0)

    parts = [
        (ref, slice(c, c + WIDE))
        for ref in (units_first_ref, units_second_ref)
        for c in range(0, ref.shape[0], WIDE)
    ]

    def tokens_of(i):
        ref, rows = parts[i]
        return ref[rows, D:]

    def first_row(i):
        per_group = len(parts) // groups
        return (table_ref[5, i // per_group] * per_group + i % per_group) * WIDE

    def feature_copies(i):
        size = feature_send_ref.shape[1]
        found = []
        for k in range(WIDE // size):
            start = pl.multiple_of(first_row(i) + k * size, size)
            source, sem = feature_ref.at[pl.ds(start, size), :], feature_sems.at[i * (WIDE // size) + k]
            at = first_row(i) // (2 * size) + k // 2
            kept = pltpu.make_async_copy(source, feature_keep_ref.at[at], sem)
            sent = pltpu.make_async_copy(source, feature_send_ref.at[at], sem)
            found += [(table_ref[4, 0] == k % 2, kept), (table_ref[4, 0] != k % 2, sent)]
        return found

    logits = nt_dot(sw, tokens_of(0))
    for i in range(len(parts)):
        following = nt_dot(sw, tokens_of(i + 1)) if i + 1 < len(parts) else None
        grads = []
        for j in range(WIDE // LANES):
            tile = i * (WIDE // LANES) + j
            lanes = slice(tile * LANES, (tile + 1) * LANES)
            ref, at = tiles[tile]
            energy = both(ref[at, here[0], :], ref[at, here[1], :]).astype(f32)
            probs = jnp.exp2(logits[:, j * LANES : (j + 1) * LANES] * student_power) * n_ref[:, lanes]
            grads.append((probs - energy * r_ref[:, lanes] * col_scale).astype(bf16))
        logit_grad = jnp.concatenate(grads, axis=1)
        added = jnp.dot(logit_grad, tokens_of(i), preferred_element_type=f32)
        total_ref[...] = added if i == 0 else total_ref[...] + added
        rows = pl.ds(pl.multiple_of(first_row(i), WIDE), WIDE)
        feature_ref[rows, :] += lax.dot_general(
            logit_grad, sw, (((0,), (0,)), ((), ())), preferred_element_type=f32
        )
        for wanted, copy in feature_copies(i):
            pl.when(jnp.logical_and(step == pl.num_programs(0) - 1, wanted))(copy.start)
        logits = following

    def copies(which, at):
        found = []
        for half, (sent_ref, kept_ref) in enumerate(
            ((send_left_ref, keep_left_ref), (send_right_ref, keep_right_ref))
        ):
            block_at = 2 * at + which
            place = table_ref[1 + half, block_at]
            source, sem = stage_ref.at[half, block_at], sems.at[half, block_at]
            sent = pltpu.make_async_copy(source, sent_ref.at[jnp.minimum(place, 3)], sem)
            kept = pltpu.make_async_copy(source, kept_ref.at[jnp.maximum(place - 4, 0)], sem)
            found += [(place < 4, sent), (place >= 4, kept)]
        return found

    for which in range(2):
        rows_here = slice(which * block, (which + 1) * block)
        for half in range(2):
            columns_here = slice(half * (D // 2), (half + 1) * (D // 2))
            stage_ref[half, 2 * step + which] = total_ref[rows_here, columns_here]
        for wanted, copy in copies(which, step):
            pl.when(wanted)(copy.start)

    @pl.when(step == pl.num_programs(0) - 1)
    def _():
        for i in range(len(parts)):
            for wanted, copy in feature_copies(i):
                pl.when(wanted)(copy.wait)
        for at in range(stage_ref.shape[1] // 2):
            for which in range(2):
                for wanted, copy in copies(which, at):
                    pl.when(wanted)(copy.wait)


def block_table(y, z, core, others):
    blocks = len(LEFT_PLACE)
    way = jnp.where(z % 2 == 1, 1, -1)
    local = (z + way * jnp.arange(blocks) + blocks) % blocks
    cores = jnp.full((blocks,), core)
    slots = jnp.stack([others[step] for step in STEPS] * 2)
    table = [y * blocks + local, jnp.array(LEFT_PLACE), jnp.array(RIGHT_PLACE), local, cores, slots]
    return jnp.stack(table).astype(jnp.int32)


def gradients(table, units_all, energy, pieces, student_protos, scale, shares):
    share = energy[0].shape[1]
    tokens = sum(part.shape[0] for part in units_all)
    block = 256
    blocks = share // block
    whole = lambda *shape: pl.BlockSpec(shape, lambda i, p: (0,) * len(shape))
    first = pl.BlockSpec((block, D), lambda i, p: (p[0, 2 * i], 0))
    second = pl.BlockSpec((block, D), lambda i, p: (p[0, 2 * i + 1], 0))
    direct = pl.BlockSpec(memory_space=pltpu.VMEM)
    half = pltpu.HBM((blocks // 2, block, D // 2), f32)
    return pl.pallas_call(
        gradient_body,
        grid_spec=pltpu.PrefetchScalarGridSpec(
            num_scalar_prefetch=1,
            grid=(blocks // 2,),
            in_specs=[
                whole(*units_all[0].shape),
                whole(*units_all[1].shape),
                direct,
                direct,
                whole(*pieces.shape),
                first,
                second,
                whole(*scale.shape),
            ],
            out_specs=[pl.BlockSpec(memory_space=pl.ANY)] * 6,
            scratch_shapes=[
                pltpu.VMEM((1, tokens), f32),
                pltpu.VMEM((1, tokens), f32),
                pltpu.VMEM((2 * block, D), f32),
                pltpu.VMEM((tokens, D), f32),
                pltpu.VMEM((2, blocks, block, D // 2), f32),
                pltpu.VMEM((tokens // LANES, LANES), f32),
                pltpu.SemaphoreType.DMA((2, blocks)),
                pltpu.SemaphoreType.DMA((shares,)),
            ],
        ),
        out_shape=[half] * 4
        + [
            pltpu.HBM((shares // 2, tokens // shares, D), f32),
            pltpu.VMEM((shares // 2, tokens // shares, D), f32),
        ],
        compiler_params=params(24),
        cost_estimate=work(8 * tokens * share * D, 8 * 2**20, tokens * share),
        name="gradients",
    )(
        table,
        *[in_hbm(part) for part in units_all],
        *energy,
        pieces,
        in_hbm(student_protos),
        in_hbm(student_protos),
        scale,
    )


def project(total, unit, length):
    return (total - unit * jnp.sum(unit * total, axis=-1, keepdims=True)) / length


def student_end_body(place_ref, pieces_ref, unit_ref, length_ref, out_ref):
    result = project(jnp.sum(pieces_ref[...], axis=0), unit_ref[...], length_ref[...])
    for copy in range(out_ref.shape[0]):
        out_ref[copy] = result


def student_end(place, pieces, units, length, copies):
    _, rows, _ = pieces.shape
    return pl.pallas_call(
        student_end_body,
        grid_spec=pltpu.PrefetchScalarGridSpec(
            num_scalar_prefetch=1,
            grid=(1,),
            in_specs=[
                pl.BlockSpec(pieces.shape, lambda i, p: (0, 0, 0)),
                pl.BlockSpec((rows, D), lambda i, p: (p[2], 1)),
                pl.BlockSpec((rows, 1), lambda i, p: (p[2], 0)),
            ],
            out_specs=pl.BlockSpec((copies, rows, D), lambda i, p: (0, 0, 0)),
        ),
        out_shape=jax.ShapeDtypeStruct((copies, rows, D), f32),
        compiler_params=params(8),
        name="student_end",
    )(place, pieces, in_hbm(units), in_hbm(length))


def proto_end_body(place_ref, *refs):
    piece_refs, (protos_ref, out_ref) = refs[:-2], refs[-2:]
    unit, length = unit_rows(protos_ref[...].astype(f32))
    half = len(piece_refs) // 2
    sums = []
    for group in (piece_refs[:half], piece_refs[half:]):
        total = group[0][...]
        for ref in group[1:]:
            total = total + ref[...]
        sums.append(total)
    out_ref[...] = project(jnp.concatenate(sums, axis=1), unit, length)


def proto_end(place, pieces, protos):
    rows, width = pieces[0].shape
    return pl.pallas_call(
        proto_end_body,
        grid_spec=pltpu.PrefetchScalarGridSpec(
            num_scalar_prefetch=1,
            grid=(1,),
            in_specs=[pl.BlockSpec((rows, width), lambda i, p: (0, 0))] * len(pieces)
            + [pl.BlockSpec((rows, D), lambda i, p: (p[1], 0))],
            out_specs=pl.BlockSpec((rows, D), lambda i, p: (0, 0)),
        ),
        out_shape=jax.ShapeDtypeStruct((rows, D), f32),
        compiler_params=params(8),
        name="proto_end",
    )(place, *pieces, in_hbm(protos))


def on_device(teacher_patches, student_patches, mask_order, teacher_protos, student_protos):
    y_size, z_size = lax.axis_size("y"), lax.axis_size("z")
    proto_size = lax.axis_size("x") * lax.axis_size("core")
    y, z = lax.axis_index("y"), lax.axis_index("z")
    others = [(y - step + y_size) % y_size for step in range(y_size)]
    core = lax.axis_index("core")
    place = [y, y * z_size + z, lax.axis_index(PROTOS), core] + others
    place = jnp.stack(place).astype(jnp.int32)
    table = block_table(y, z, core, others)
    share = teacher_protos.shape[0] // y_size

    units, student_length, mine = select_tokens(
        core.astype(jnp.int32)[None], teacher_patches, student_patches, mask_order
    )
    from_y = lambda value, step: lax.ppermute(
        value, "y", [(i, (i + step) % y_size) for i in range(y_size)]
    )
    from_core = lambda value: lax.ppermute(value, "core", [(0, 1), (1, 0)])
    own = mine.shape[0]
    half = own // 2
    first, third = from_y(mine, 1), from_y(mine, 3)
    norm_part = student_sums(units, student_protos)
    norm_part, first, third, place, table = lax.optimization_barrier(
        (norm_part, first, third, place, table)
    )
    second = [from_y(first[:half], 1), from_y(third[half:], 3)]
    rows = lambda start, size: slice(start, start + size)
    near = [units, first, third, from_core(first), from_core(third)]
    layout = [
        (rows(0, own), None),
        (rows(own, own), 0),
        (rows(2 * own, own), 0),
        (rows(own, own), 1),
        (rows(2 * own, own), 1),
    ]
    energy_near, sums, units_near = energy_of(
        place, near, layout, 3 * own, teacher_protos, share, 1
    )
    sums, second = lax.optimization_barrier((sums, second))
    far = second + [from_core(piece) for piece in second]
    layout = [(rows(0, half), 0), (rows(half, half), 0), (rows(0, half), 1), (rows(half, half), 1)]
    energy_far, sums, units_far = energy_of(
        place, far, layout, own, teacher_protos, share, z_size, (sums,)
    )
    energy, units_all = (energy_near, energy_far), (units_near, units_far)

    rows = ("y",) + PROTOS
    peers = y_size * proto_size
    for sweep in range(ITERS):
        if sweep > 0:
            sums = column_sums(place, energy, pieces, z_size)
        norms = (norm_part,) if sweep == ITERS - 1 else ()
        col_scale, row_part = row_sums(place, energy, spread(sums, "z"), peers, norms)
        pieces = spread(row_part, rows)
    pieces = pieces.reshape((y_size, proto_size) + pieces.shape[1:])

    send_left, send_right, keep_left, keep_right, feature_send, feature_keep = gradients(
        table, units_all, energy, pieces, student_protos, col_scale, peers
    )
    feature_part = feature_keep + from_core(feature_send)
    feature_part, keep_left, keep_right = lax.optimization_barrier(
        (feature_part, keep_left, keep_right)
    )
    left = pass_on(collect(send_left, keep_left, 0), 0)
    right_half = pass_on(collect(send_right, keep_right, 1), 1)
    feature_pieces = spread(feature_part, ("y", "x"))
    feature_pieces, left, right_half = lax.optimization_barrier((feature_pieces, left, right_half))
    left, right_half = deliver(left, 0), deliver(right_half, 1)
    result = student_end(place, feature_pieces, units, student_length, proto_size)
    result = spread(result, PROTOS)
    grad_protos = proto_end(place, left + right_half, student_protos)
    return (result.reshape(-1, MASKED, D), grad_protos)


def solution(mesh):
    fine = Mesh(mesh.devices.reshape(4, 8, 4, 2), ("y", "z", "x", "core"))
    return jax.shard_map(
        on_device,
        mesh=fine,
        in_specs=(
            P(ROWS, None, None),
            P(ROWS, None, None),
            P(ROWS, None),
            P(PROTOS, None),
            P(PROTOS, None),
        ),
        out_specs=(P(ROWS, None, None), P(PROTOS + ROWS, None)),
        check_vma=False,
    )
```

```python
import functools
import math

import jax
import jax.numpy as jnp
from jax import lax
from jax.experimental import pallas as pl
from jax.experimental.pallas import tpu as pltpu
from jax.sharding import Mesh, PartitionSpec as P

D = 256
MASKED = 128
ITERS = 3
LANES = 128

teacher_temp = 0.07
student_temp = 0.1
epsilon = 1e-06

teacher_power = math.log2(math.e) / teacher_temp
student_power = math.log2(math.e) / student_temp

ROWS = ("y", "z")
PROTOS = ("x", "core")

f32 = jnp.float32
bf16 = jnp.bfloat16


def params(mib):
    return pltpu.CompilerParams(vmem_limit_bytes=mib * 2**20)


def spread(value, axes):
    return lax.all_to_all(value, axes, 0, 0, tiled=True)


def work(flops, moved, powers=0):
    return pl.CostEstimate(flops=int(flops), bytes_accessed=int(moved), transcendentals=int(powers))


def in_hbm(value):
    return pltpu.with_memory_space_constraint(value, pltpu.HBM)


def nt_dot(a, b):
    return lax.dot_general(a, b, (((1,), (1,)), ((), ())), preferred_element_type=f32)


def unit_rows(values):
    length = jnp.sqrt(jnp.sum(values * values, axis=-1, keepdims=True) + epsilon)
    return (values / length, length)


def directions(values):
    values = values.astype(f32)
    return (values * lax.rsqrt(jnp.sum(values * values, axis=-1, keepdims=True) + epsilon)).astype(bf16)


def to_column(row):
    return jnp.broadcast_to(row, (LANES, LANES)).T


def fill_columns(rows, tile_ref):
    for k in range(rows.shape[0]):
        tile_ref[k * LANES : (k + 1) * LANES, :] = to_column(rows[k : k + 1, :])


def lane_totals(tile):
    parts = [
        jnp.sum(tile[k * LANES : (k + 1) * LANES, :].T, axis=0, keepdims=True)
        for k in range(tile.shape[0] // LANES)
    ]
    return jnp.concatenate(parts, axis=0)


def select_body(core_ref, teacher_ref, student_ref, order_ref, units_ref, length_ref, mine_ref):
    images, patches, _ = teacher_ref.shape
    for image in range(images):
        chosen = order_ref[image : image + 1, :MASKED]
        place = lax.broadcasted_iota(jnp.int32, (patches, MASKED), 0)
        onehot = jnp.where(place == chosen, 1.0, 0.0).astype(bf16)

        def pick(ref):
            return lax.dot_general(
                onehot, ref[image], (((0,), (0,)), ((), ())), preferred_element_type=f32
            )

        rows = slice(image * MASKED, (image + 1) * MASKED)
        teacher = unit_rows(pick(teacher_ref))[0]
        student, length_ref[rows, :] = unit_rows(pick(student_ref))
        units_ref[rows, :D] = teacher
        units_ref[rows, D:] = student
        mine_ref[rows, :] = jnp.where(core_ref[0] == 0, teacher, student)


def select_tokens(core, teacher_patches, student_patches, mask_order):
    tokens = teacher_patches.shape[0] * MASKED
    return pl.pallas_call(
        select_body,
        in_specs=[pl.BlockSpec(memory_space=pltpu.SMEM)]
        + [pl.BlockSpec(memory_space=pltpu.VMEM)] * 3,
        out_specs=[pl.BlockSpec(memory_space=pltpu.VMEM)] * 3,
        out_shape=[
            pltpu.HBM((tokens, 2 * D), f32),
            pltpu.HBM((tokens, 1), f32),
            pltpu.HBM((tokens, D), f32),
        ],
        compiler_params=params(8),
        name="select",
    )(core, in_hbm(teacher_patches), in_hbm(student_patches), in_hbm(mask_order))


def lane_rows(row):
    parts = [row[:, j * LANES : (j + 1) * LANES] for j in range(row.shape[1] // LANES)]
    return jnp.concatenate(parts, axis=0)


def chunks(tokens):
    return [slice(c, c + LANES) for c in range(0, tokens, LANES)]


FETCHES = 8
WIDE = 256


def fetch(protos_ref, buffer_ref, sems, i):
    size = buffer_ref.shape[0] // FETCHES
    rows = pl.ds(pl.multiple_of(i * size, size), size)
    return pltpu.make_async_copy(protos_ref.at[rows, :], buffer_ref.at[rows, :], sems.at[i])


def fetch_all(units_ref, column, unit_ref, protos_ref, buffer_ref, sems):
    units = pltpu.make_async_copy(
        units_ref.at[:, pl.ds(column, D)], unit_ref, sems.at[FETCHES]
    )
    units.start()
    for i in range(FETCHES):
        fetch(protos_ref, buffer_ref, sems, i).start()
    units.wait()


STEPS = [0, 1, 3, 2]


def energy_body(layout, before, place_ref, *refs):
    piece_refs, refs = refs[: len(layout)], refs[len(layout) :]
    protos_ref, refs = refs[0], refs[1:]
    before_refs, refs = refs[:before], refs[before:]
    energy_ref, sums_ref, cast_ref, weights_ref, total_ref = refs
    for ref, (rows, kind) in zip(piece_refs, layout):
        if kind is None:
            cast_ref[rows, :] = ref[...].astype(bf16)
    for core in range(2):

        @pl.when(place_ref[3] == core)
        def _(core=core):
            for ref, (rows, kind) in zip(piece_refs, layout):
                if kind is not None:
                    half = core if kind == 0 else 1 - core
                    cast_ref[rows, half * D : (half + 1) * D] = ref[...].astype(bf16)

    weights_ref[...] = directions(protos_ref[...])
    total_ref[...] = jnp.zeros_like(total_ref)
    size = 512
    parts = [slice(c, c + size) for c in range(0, weights_ref.shape[0], size)]

    def step(i, carry):
        chunk = cast_ref[pl.ds(pl.multiple_of(i * WIDE, WIDE), WIDE), :][:, :D]
        logits = nt_dot(weights_ref[parts[0], :], chunk)
        for k, part in enumerate(parts):
            following = nt_dot(weights_ref[parts[k + 1], :], chunk) if k + 1 < len(parts) else None
            energy = jnp.exp2(logits * teacher_power)
            total = total_ref[part, :]
            for j in range(WIDE // LANES):
                tile = energy[:, j * LANES : (j + 1) * LANES]
                energy_ref[i * (WIDE // LANES) + j, part, :] = tile.astype(bf16)
                total = total + tile
            total_ref[part, :] = total
            logits = following
        return carry

    lax.fori_loop(0, cast_ref.shape[0] // WIDE, step, 0)
    totals = lane_totals(total_ref[...])
    for ref in before_refs:
        totals = totals + ref[0]
    for copy in range(sums_ref.shape[0]):
        sums_ref[copy] = totals


def fixed(*shape):
    return pl.BlockSpec(shape, lambda i: (0,) * len(shape))


def left(tokens):
    return pl.BlockSpec((tokens, D), lambda *i: (0, 0))


def right(tokens):
    return pl.BlockSpec((tokens, D), lambda *i: (0, 1))


def energy_of(place, pieces, layout, tokens, protos, share, copies, before=()):
    direct = pl.BlockSpec(memory_space=pltpu.VMEM)
    whole = lambda value: pl.BlockSpec(value.shape, lambda i, p: (0,) * value.ndim)
    return pl.pallas_call(
        functools.partial(energy_body, layout, len(before)),
        grid_spec=pltpu.PrefetchScalarGridSpec(
            num_scalar_prefetch=1,
            grid=(1,),
            in_specs=[whole(piece) for piece in pieces]
            + [pl.BlockSpec((share, D), lambda i, p: (p[0], 0))]
            + [whole(value) for value in before],
            out_specs=[
                direct,
                pl.BlockSpec((copies, share // LANES, LANES), lambda i, p: (0, 0, 0)),
                pl.BlockSpec((tokens, 2 * D), lambda i, p: (0, 0)),
            ],
            scratch_shapes=[pltpu.VMEM((share, D), bf16), pltpu.VMEM((share, LANES), f32)],
        ),
        out_shape=[
            pltpu.VMEM((tokens // LANES, share, LANES), bf16),
            jax.ShapeDtypeStruct((copies, share // LANES, LANES), f32),
            pltpu.HBM((tokens, 2 * D), bf16),
        ],
        compiler_params=params(20),
        cost_estimate=work(4 * tokens * share * D, 8 * 2**20, tokens * share),
        name="energy",
    )(place, *pieces, in_hbm(protos), *before)


def student_body(units_ref, protos_ref, sums_ref, unit_ref, cast_ref, total_ref, buffer_ref, sems):
    size = buffer_ref.shape[0] // FETCHES
    fetch_all(units_ref, D, unit_ref, protos_ref, buffer_ref, sems)
    cast_ref[...] = unit_ref[...].astype(bf16)
    total_ref[...] = jnp.zeros_like(total_ref)

    def step(i, carry):
        fetch(protos_ref, buffer_ref, sems, i).wait()
        total = total_ref[...]

        def logits_of(part):
            rows = pl.ds(pl.multiple_of(i * size + part * WIDE, WIDE), WIDE)
            return nt_dot(cast_ref[...], directions(buffer_ref[rows, :]))

        parts = size // WIDE
        logits = logits_of(0)
        for part in range(parts):
            following = logits_of(part + 1) if part + 1 < parts else None
            values = jnp.exp2(logits * student_power)
            logits = following
            for j in range(WIDE // LANES):
                total = total + values[:, j * LANES : (j + 1) * LANES]
        total_ref[...] = total
        return carry

    lax.fori_loop(0, FETCHES, step, 0)
    sums_ref[...] = lane_totals(total_ref[...])


def student_sums(units, protos):
    tokens, count = units.shape[0], protos.shape[0]
    return pl.pallas_call(
        student_body,
        in_specs=[pl.BlockSpec(memory_space=pl.ANY)] * 2,
        out_specs=pl.BlockSpec(memory_space=pltpu.VMEM),
        out_shape=jax.ShapeDtypeStruct((tokens // LANES, LANES), f32),
        scratch_shapes=[
            pltpu.VMEM((tokens, D), f32),
            pltpu.VMEM((tokens, D), bf16),
            pltpu.VMEM((tokens, LANES), f32),
            pltpu.VMEM((count, D), bf16),
            pltpu.SemaphoreType.DMA((FETCHES + 1,)),
        ],
        compiler_params=params(16),
        cost_estimate=work(4 * tokens * count * D, 8 * 2**20, tokens * count),
        name="student",
    )(in_hbm(units), in_hbm(protos))


def right(tokens):
    return pl.BlockSpec((tokens, D), lambda *i: (0, 1))


def tiles_of(first_ref, second_ref):
    return [(ref, j) for ref in (first_ref, second_ref) for j in range(ref.shape[0])]


def row_body(place_ref, first_ref, second_ref, pieces_ref, *refs):
    norm_refs, (scale_ref, sums_ref, tile_ref) = refs[:-3], refs[-3:]
    scale_ref[...] = 1.0 / jnp.sum(pieces_ref[...], axis=0)
    fill_columns(scale_ref[...], tile_ref)
    tiles = tiles_of(first_ref, second_ref)
    size = 512
    totals = []
    for ref, j in tiles:
        total = jnp.zeros((1, LANES), f32)
        for start in range(0, ref.shape[1], size):
            part = slice(start, start + size)
            energy = ref[j, part, :].astype(f32)
            total = total + jnp.sum(energy * tile_ref[part, :], axis=0, keepdims=True)
        totals.append(total)
    rows = sums_ref.shape[2]
    for group, step in enumerate(STEPS):
        value = jnp.concatenate(totals[group * rows : (group + 1) * rows], axis=0)
        for copy in range(sums_ref.shape[0]):
            sums_ref[copy, place_ref[4 + step]] = value
    for ref in norm_refs:
        for copy in range(sums_ref.shape[0]):
            sums_ref[copy, len(STEPS)] = ref[...]


def row_sums(place, energy, pieces, copies, norm_part=()):
    tiles = sum(part.shape[0] for part in energy)
    protos = energy[0].shape[1]
    whole = pl.BlockSpec(memory_space=pltpu.VMEM)
    groups = len(STEPS)
    return pl.pallas_call(
        row_body,
        in_specs=[pl.BlockSpec(memory_space=pltpu.SMEM)] + [whole] * (3 + len(norm_part)),
        out_specs=[whole] * 2,
        out_shape=[
            jax.ShapeDtypeStruct((protos // LANES, LANES), f32),
            jax.ShapeDtypeStruct((copies, groups + len(norm_part), tiles // groups, LANES), f32),
        ],
        scratch_shapes=[pltpu.VMEM((protos, LANES), f32)],
        compiler_params=params(12),
        cost_estimate=work(2 * tiles * LANES * protos, 0),
        name="row_sums",
    )(place, *energy, pieces, *norm_part)


def column_body(place_ref, first_ref, second_ref, pieces_ref, sums_ref, scale_ref, rows_ref):
    tiles = tiles_of(first_ref, second_ref)
    rows_ref[...] = 1.0 / jnp.sum(pieces_ref[...], axis=0)
    for group, step in enumerate(STEPS):
        scale_ref[group] = rows_ref[place_ref[4 + step]]
    rows = rows_ref.shape[1]

    def step(k, carry):
        part = pl.ds(pl.multiple_of(k * LANES, LANES), LANES)
        total = jnp.zeros((LANES, LANES), f32)
        for i, (ref, j) in enumerate(tiles):
            scale = scale_ref[i // rows, i % rows : i % rows + 1, :]
            total = total + ref[j, part, :].astype(f32) * scale
        sums_ref[0, pl.ds(k, 1), :] = lane_totals(total)
        return carry

    lax.fori_loop(0, first_ref.shape[1] // LANES, step, 0, unroll=4)
    for copy in range(1, sums_ref.shape[0]):
        sums_ref[copy] = sums_ref[0]


def column_sums(place, energy, pieces, copies):
    tiles = sum(part.shape[0] for part in energy)
    protos = energy[0].shape[1]
    whole = pl.BlockSpec(memory_space=pltpu.VMEM)
    return pl.pallas_call(
        column_body,
        in_specs=[pl.BlockSpec(memory_space=pltpu.SMEM)] + [whole] * 3,
        out_specs=whole,
        out_shape=jax.ShapeDtypeStruct((copies, protos // LANES, LANES), f32),
        scratch_shapes=[pltpu.VMEM(pieces.shape[1:], f32)] * 2,
        compiler_params=params(12),
        cost_estimate=work(2 * tiles * LANES * protos, 0),
        name="column_sums",
    )(place, *energy, pieces)


LEFT_PLACE = [4, 5, 6, 7, 3, 2, 1, 0]
RIGHT_PLACE = [4, 0, 1, 2, 3, 7, 6, 5]


def collect(send, keep, offset):
    n = lax.axis_size("z")
    way = [1 if (z + offset) % 2 else -1 for z in range(n)]
    got = lax.ppermute(send, "z", [(z, (z - way[z]) % n) for z in range(n)])
    return keep[0] + got[0], keep[1] + got[1], keep[2:] + got[2:]


def pass_on(sums, offset):
    n = lax.axis_size("z")
    way = [1 if (z + offset) % 2 else -1 for z in range(n)]
    own, following, far = sums
    got = lax.ppermute(far, "z", [(z, (z + 2 * way[z]) % n) for z in range(n)])
    return own + got[0], following + got[1]


def deliver(sums, offset):
    n = lax.axis_size("z")
    way = [1 if (z + offset) % 2 else -1 for z in range(n)]
    own, following = sums
    return [own, lax.ppermute(following, "z", [(z, (z + way[z]) % n) for z in range(n)])]


def gradient_body(
    table_ref,
    units_first_ref,
    units_second_ref,
    energy_first_ref,
    energy_second_ref,
    pieces_ref,
    sw_first_ref,
    sw_second_ref,
    scale_ref,
    send_left_ref,
    send_right_ref,
    keep_left_ref,
    keep_right_ref,
    feature_send_ref,
    feature_keep_ref,
    r_ref,
    n_ref,
    total_ref,
    feature_ref,
    stage_ref,
    rows_ref,
    sems,
    feature_sems,
):
    step = pl.program_id(0)
    tiles = tiles_of(energy_first_ref, energy_second_ref)
    groups = pieces_ref.shape[0]
    own = len(tiles) // groups

    @pl.when(step == 0)
    def _():
        total = jnp.sum(pieces_ref[:, :, :groups], axis=(0, 1))
        rows_ref[...] = (1.0 / student_temp) / total
        for group in range(groups):
            slot = table_ref[5, group]
            row_scale = rows_ref[slot]
            inverse = (1.0 / student_temp) / jnp.sum(pieces_ref[slot][:, groups], axis=0)
            for k in range(own):
                lanes = slice((group * own + k) * LANES, (group * own + k + 1) * LANES)
                r_ref[:, lanes] = row_scale[k : k + 1, :]
                n_ref[:, lanes] = inverse[k : k + 1, :]
        feature_ref[...] = jnp.zeros_like(feature_ref)

    both = lambda first, second: jnp.concatenate([first, second], axis=0)
    block = sw_first_ref.shape[0]
    sw = both(directions(sw_first_ref[...]), directions(sw_second_ref[...]))
    local = [table_ref[3, 2 * step], table_ref[3, 2 * step + 1]]
    here = [pl.ds(pl.multiple_of(place * block, block), block) for place in local]
    columns = []
    for place in local:
        for k in range(block // LANES):
            row = scale_ref[pl.ds(place * (block // LANES) + k, 1), :]
            columns.append(to_column(row))
    col_scale = jnp.concatenate(columns, axis=0)

    parts = [
        (ref, slice(c, c + WIDE))
        for ref in (units_first_ref, units_second_ref)
        for c in range(0, ref.shape[0], WIDE)
    ]

    def tokens_of(i):
        ref, rows = parts[i]
        return ref[rows, D:]

    def first_row(i):
        per_group = len(parts) // groups
        return (table_ref[5, i // per_group] * per_group + i % per_group) * WIDE

    def feature_copies(i):
        size = feature_send_ref.shape[1]
        found = []
        for k in range(WIDE // size):
            source = feature_ref.at[pl.ds(i * WIDE + k * size, size), :]
            sem = feature_sems.at[i * (WIDE // size) + k]
            at = first_row(i) // (2 * size) + k // 2
            kept = pltpu.make_async_copy(source, feature_keep_ref.at[at], sem)
            sent = pltpu.make_async_copy(source, feature_send_ref.at[at], sem)
            found += [(table_ref[4, 0] == k % 2, kept), (table_ref[4, 0] != k % 2, sent)]
        return found

    logits = nt_dot(sw, tokens_of(0))
    for i in range(len(parts)):
        following = nt_dot(sw, tokens_of(i + 1)) if i + 1 < len(parts) else None
        grads = []
        for j in range(WIDE // LANES):
            tile = i * (WIDE // LANES) + j
            lanes = slice(tile * LANES, (tile + 1) * LANES)
            ref, at = tiles[tile]
            energy = both(ref[at, here[0], :], ref[at, here[1], :]).astype(f32)
            probs = jnp.exp2(logits[:, j * LANES : (j + 1) * LANES] * student_power) * n_ref[:, lanes]
            grads.append((probs - energy * r_ref[:, lanes] * col_scale).astype(bf16))
        logit_grad = jnp.concatenate(grads, axis=1)
        added = jnp.dot(logit_grad, tokens_of(i), preferred_element_type=f32)
        total_ref[...] = added if i == 0 else total_ref[...] + added
        feature_ref[i * WIDE : (i + 1) * WIDE, :] += lax.dot_general(
            logit_grad, sw, (((0,), (0,)), ((), ())), preferred_element_type=f32
        )
        logits = following
        if (i + 1) % (len(parts) // 2) == 0:

            @pl.when(step == pl.num_programs(0) - 1)
            def _(done=i + 1):
                for chunk in range(done - len(parts) // 2, done):
                    for wanted, copy in feature_copies(chunk):
                        pl.when(wanted)(copy.start)


    def copies(which, at):
        found = []
        for half, (sent_ref, kept_ref) in enumerate(
            ((send_left_ref, keep_left_ref), (send_right_ref, keep_right_ref))
        ):
            block_at = 2 * at + which
            place = table_ref[1 + half, block_at]
            source, sem = stage_ref.at[half, block_at], sems.at[half, block_at]
            sent = pltpu.make_async_copy(source, sent_ref.at[jnp.minimum(place, 3)], sem)
            kept = pltpu.make_async_copy(source, kept_ref.at[jnp.maximum(place - 4, 0)], sem)
            found += [(place < 4, sent), (place >= 4, kept)]
        return found

    for which in range(2):
        rows_here = slice(which * block, (which + 1) * block)
        for half in range(2):
            columns_here = slice(half * (D // 2), (half + 1) * (D // 2))
            stage_ref[half, 2 * step + which] = total_ref[rows_here, columns_here]
        for wanted, copy in copies(which, step):
            pl.when(wanted)(copy.start)

    @pl.when(step == pl.num_programs(0) - 1)
    def _():
        for i in range(len(parts)):
            for wanted, copy in feature_copies(i):
                pl.when(wanted)(copy.wait)
        for at in range(stage_ref.shape[1] // 2):
            for which in range(2):
                for wanted, copy in copies(which, at):
                    pl.when(wanted)(copy.wait)


def block_table(y, z, core, others):
    blocks = len(LEFT_PLACE)
    way = jnp.where(z % 2 == 1, 1, -1)
    local = (z + way * jnp.arange(blocks) + blocks) % blocks
    cores = jnp.full((blocks,), core)
    slots = jnp.stack([others[step] for step in STEPS] * 2)
    table = [y * blocks + local, jnp.array(LEFT_PLACE), jnp.array(RIGHT_PLACE), local, cores, slots]
    return jnp.stack(table).astype(jnp.int32)


def gradients(table, units_all, energy, pieces, student_protos, scale, shares):
    share = energy[0].shape[1]
    tokens = sum(part.shape[0] for part in units_all)
    block = 256
    blocks = share // block
    whole = lambda *shape: pl.BlockSpec(shape, lambda i, p: (0,) * len(shape))
    first = pl.BlockSpec((block, D), lambda i, p: (p[0, 2 * i], 0))
    second = pl.BlockSpec((block, D), lambda i, p: (p[0, 2 * i + 1], 0))
    direct = pl.BlockSpec(memory_space=pltpu.VMEM)
    half = pltpu.HBM((blocks // 2, block, D // 2), f32)
    return pl.pallas_call(
        gradient_body,
        grid_spec=pltpu.PrefetchScalarGridSpec(
            num_scalar_prefetch=1,
            grid=(blocks // 2,),
            in_specs=[
                whole(*units_all[0].shape),
                whole(*units_all[1].shape),
                direct,
                direct,
                whole(*pieces.shape),
                first,
                second,
                whole(*scale.shape),
            ],
            out_specs=[pl.BlockSpec(memory_space=pl.ANY)] * 6,
            scratch_shapes=[
                pltpu.VMEM((1, tokens), f32),
                pltpu.VMEM((1, tokens), f32),
                pltpu.VMEM((2 * block, D), f32),
                pltpu.VMEM((tokens, D), f32),
                pltpu.VMEM((2, blocks, block, D // 2), f32),
                pltpu.VMEM((len(STEPS), tokens // LANES // len(STEPS), LANES), f32),
                pltpu.SemaphoreType.DMA((2, blocks)),
                pltpu.SemaphoreType.DMA((shares,)),
            ],
        ),
        out_shape=[half] * 4
        + [
            pltpu.HBM((shares // 2, tokens // shares, D), f32),
            pltpu.VMEM((shares // 2, tokens // shares, D), f32),
        ],
        compiler_params=params(24),
        cost_estimate=work(8 * tokens * share * D, 8 * 2**20, tokens * share),
        name="gradients",
    )(
        table,
        *[in_hbm(part) for part in units_all],
        *energy,
        pieces,
        in_hbm(student_protos),
        in_hbm(student_protos),
        scale,
    )


def project(total, unit, length):
    return (total - unit * jnp.sum(unit * total, axis=-1, keepdims=True)) / length


def student_end_body(place_ref, pieces_ref, unit_ref, length_ref, out_ref):
    result = project(jnp.sum(pieces_ref[...], axis=0), unit_ref[...], length_ref[...])
    for copy in range(out_ref.shape[0]):
        out_ref[copy] = result


def student_end(place, pieces, units, length, copies):
    _, rows, _ = pieces.shape
    return pl.pallas_call(
        student_end_body,
        grid_spec=pltpu.PrefetchScalarGridSpec(
            num_scalar_prefetch=1,
            grid=(1,),
            in_specs=[
                pl.BlockSpec(memory_space=pltpu.VMEM),
                pl.BlockSpec((rows, D), lambda i, p: (p[2], 1)),
                pl.BlockSpec((rows, 1), lambda i, p: (p[2], 0)),
            ],
            out_specs=pl.BlockSpec((copies, rows, D), lambda i, p: (0, 0, 0)),
        ),
        out_shape=jax.ShapeDtypeStruct((copies, rows, D), f32),
        compiler_params=params(8),
        name="student_end",
    )(place, pieces, in_hbm(units), in_hbm(length))


def proto_end_body(place_ref, *refs):
    piece_refs, (protos_ref, out_ref) = refs[:-2], refs[-2:]
    unit, length = unit_rows(protos_ref[...].astype(f32))
    half = len(piece_refs) // 2
    sums = []
    for group in (piece_refs[:half], piece_refs[half:]):
        total = group[0][...]
        for ref in group[1:]:
            total = total + ref[...]
        sums.append(total)
    out_ref[...] = project(jnp.concatenate(sums, axis=1), unit, length)


def proto_end(place, pieces, protos):
    rows, width = pieces[0].shape
    return pl.pallas_call(
        proto_end_body,
        grid_spec=pltpu.PrefetchScalarGridSpec(
            num_scalar_prefetch=1,
            grid=(1,),
            in_specs=[pl.BlockSpec(memory_space=pltpu.VMEM)] * len(pieces)
            + [pl.BlockSpec((rows, D), lambda i, p: (p[1], 0))],
            out_specs=pl.BlockSpec((rows, D), lambda i, p: (0, 0)),
        ),
        out_shape=jax.ShapeDtypeStruct((rows, D), f32),
        compiler_params=params(8),
        name="proto_end",
    )(place, *pieces, in_hbm(protos))


def on_device(teacher_patches, student_patches, mask_order, teacher_protos, student_protos):
    y_size, z_size = lax.axis_size("y"), lax.axis_size("z")
    proto_size = lax.axis_size("x") * lax.axis_size("core")
    y, z = lax.axis_index("y"), lax.axis_index("z")
    others = [(y - step + y_size) % y_size for step in range(y_size)]
    core = lax.axis_index("core")
    place = [y, y * z_size + z, lax.axis_index(PROTOS), core] + others
    place = jnp.stack(place).astype(jnp.int32)
    table = block_table(y, z, core, others)
    share = teacher_protos.shape[0] // y_size

    units, student_length, mine = select_tokens(
        core.astype(jnp.int32)[None], teacher_patches, student_patches, mask_order
    )
    from_y = lambda value, step: lax.ppermute(
        value, "y", [(i, (i + step) % y_size) for i in range(y_size)]
    )
    from_core = lambda value: lax.ppermute(value, "core", [(0, 1), (1, 0)])
    own = mine.shape[0]
    half = own // 2
    first, third = from_y(mine, 1), from_y(mine, 3)
    norm_part = student_sums(units, student_protos)
    norm_part, first, third, place, table = lax.optimization_barrier(
        (norm_part, first, third, place, table)
    )
    second = [from_y(first[:half], 1), from_y(third[half:], 3)]
    rows = lambda start, size: slice(start, start + size)
    near = [units, first, third, from_core(first), from_core(third)]
    layout = [
        (rows(0, own), None),
        (rows(own, own), 0),
        (rows(2 * own, own), 0),
        (rows(own, own), 1),
        (rows(2 * own, own), 1),
    ]
    energy_near, sums, units_near = energy_of(
        place, near, layout, 3 * own, teacher_protos, share, 1
    )
    sums, second = lax.optimization_barrier((sums, second))
    far = second + [from_core(piece) for piece in second]
    layout = [(rows(0, half), 0), (rows(half, half), 0), (rows(0, half), 1), (rows(half, half), 1)]
    energy_far, sums, units_far = energy_of(
        place, far, layout, own, teacher_protos, share, z_size, (sums,)
    )
    energy, units_all = (energy_near, energy_far), (units_near, units_far)

    rows = ("y",) + PROTOS
    peers = y_size * proto_size
    for sweep in range(ITERS):
        if sweep > 0:
            sums = column_sums(place, energy, pieces, z_size)
        norms = (norm_part,) if sweep == ITERS - 1 else ()
        col_scale, row_part = row_sums(place, energy, spread(sums, "z"), peers, norms)
        pieces = spread(row_part, rows)
    pieces = pieces.reshape((y_size, proto_size) + pieces.shape[1:])

    send_left, send_right, keep_left, keep_right, feature_send, feature_keep = gradients(
        table, units_all, energy, pieces, student_protos, col_scale, peers
    )
    feature_part = feature_keep + from_core(feature_send)
    feature_part, keep_left, keep_right = lax.optimization_barrier(
        (feature_part, keep_left, keep_right)
    )
    left = pass_on(collect(send_left, keep_left, 0), 0)
    right_half = pass_on(collect(send_right, keep_right, 1), 1)
    feature_pieces = spread(feature_part, ("y", "x"))
    feature_pieces, left, right_half = lax.optimization_barrier((feature_pieces, left, right_half))
    left, right_half = deliver(left, 0), deliver(right_half, 1)
    result = student_end(place, feature_pieces, units, student_length, proto_size)
    result = spread(result, PROTOS)
    grad_protos = proto_end(place, left + right_half, student_protos)
    return (result.reshape(-1, MASKED, D), grad_protos)


def solution(mesh):
    fine = Mesh(mesh.devices.reshape(4, 8, 4, 2), ("y", "z", "x", "core"))
    return jax.shard_map(
        on_device,
        mesh=fine,
        in_specs=(
            P(ROWS, None, None),
            P(ROWS, None, None),
            P(ROWS, None),
            P(PROTOS, None),
            P(PROTOS, None),
        ),
        out_specs=(P(ROWS, None, None), P(PROTOS + ROWS, None)),
        check_vma=False,
    )
```

```python
import math

import jax
import jax.numpy as jnp
from jax import lax
from jax.experimental import pallas as pl
from jax.experimental.pallas import tpu as pltpu
from jax.sharding import Mesh, PartitionSpec as P

D = 256
MASKED = 128
ITERS = 3
LANES = 128

teacher_temp = 0.07
student_temp = 0.1
epsilon = 1e-06

teacher_power = math.log2(math.e) / teacher_temp
student_power = math.log2(math.e) / student_temp

ROWS = ("y", "z")
PROTOS = ("x", "core")

f32 = jnp.float32
bf16 = jnp.bfloat16


def params(mib):
    return pltpu.CompilerParams(vmem_limit_bytes=mib * 2**20)


def spread(value, axes):
    return lax.all_to_all(value, axes, 0, 0, tiled=True)


def work(flops, moved, powers=0):
    return pl.CostEstimate(flops=int(flops), bytes_accessed=int(moved), transcendentals=int(powers))


def in_hbm(value):
    return pltpu.with_memory_space_constraint(value, pltpu.HBM)


def nt_dot(a, b):
    return lax.dot_general(a, b, (((1,), (1,)), ((), ())), preferred_element_type=f32)


def unit_rows(values):
    length = jnp.sqrt(jnp.sum(values * values, axis=-1, keepdims=True) + epsilon)
    return (values / length, length)


def directions(values):
    values = values.astype(f32)
    return (values * lax.rsqrt(jnp.sum(values * values, axis=-1, keepdims=True) + epsilon)).astype(bf16)


def to_column(row):
    return jnp.broadcast_to(row, (LANES, LANES)).T


def fill_columns(rows, tile_ref):
    for k in range(rows.shape[0]):
        tile_ref[k * LANES : (k + 1) * LANES, :] = to_column(rows[k : k + 1, :])


def lane_totals(tile):
    parts = [
        jnp.sum(tile[k * LANES : (k + 1) * LANES, :].T, axis=0, keepdims=True)
        for k in range(tile.shape[0] // LANES)
    ]
    return jnp.concatenate(parts, axis=0)


def select_body(core_ref, teacher_ref, student_ref, order_ref, units_ref, length_ref, mine_ref):
    images, patches, _ = teacher_ref.shape
    for image in range(images):
        chosen = order_ref[image : image + 1, :MASKED]
        place = lax.broadcasted_iota(jnp.int32, (patches, MASKED), 0)
        onehot = jnp.where(place == chosen, 1.0, 0.0).astype(bf16)

        def pick(ref):
            return lax.dot_general(
                onehot, ref[image], (((0,), (0,)), ((), ())), preferred_element_type=f32
            )

        rows = slice(image * MASKED, (image + 1) * MASKED)
        teacher = unit_rows(pick(teacher_ref))[0]
        student, length_ref[rows, :] = unit_rows(pick(student_ref))
        units_ref[rows, :D] = teacher
        units_ref[rows, D:] = student
        mine_ref[rows, :] = jnp.where(core_ref[0] == 0, teacher, student)


def select_tokens(core, teacher_patches, student_patches, mask_order):
    tokens = teacher_patches.shape[0] * MASKED
    return pl.pallas_call(
        select_body,
        in_specs=[pl.BlockSpec(memory_space=pltpu.SMEM)]
        + [pl.BlockSpec(memory_space=pltpu.VMEM)] * 3,
        out_specs=[pl.BlockSpec(memory_space=pltpu.VMEM)] * 3,
        out_shape=[
            pltpu.HBM((tokens, 2 * D), f32),
            pltpu.HBM((tokens, 1), f32),
            pltpu.HBM((tokens, D), f32),
        ],
        compiler_params=params(8),
        name="select",
    )(core, in_hbm(teacher_patches), in_hbm(student_patches), in_hbm(mask_order))


def lane_rows(row):
    parts = [row[:, j * LANES : (j + 1) * LANES] for j in range(row.shape[1] // LANES)]
    return jnp.concatenate(parts, axis=0)


def chunks(tokens):
    return [slice(c, c + LANES) for c in range(0, tokens, LANES)]


FETCHES = 8
WIDE = 256


def fetch(protos_ref, buffer_ref, sems, i):
    size = buffer_ref.shape[0] // FETCHES
    rows = pl.ds(pl.multiple_of(i * size, size), size)
    return pltpu.make_async_copy(protos_ref.at[rows, :], buffer_ref.at[rows, :], sems.at[i])


def fetch_all(units_ref, column, unit_ref, protos_ref, buffer_ref, sems):
    units = pltpu.make_async_copy(
        units_ref.at[:, pl.ds(column, D)], unit_ref, sems.at[FETCHES]
    )
    units.start()
    for i in range(FETCHES):
        fetch(protos_ref, buffer_ref, sems, i).start()
    units.wait()


def energy_body(
    place_ref, units_ref, *refs
):
    piece_refs, (protos_ref, energy_ref, sums_ref, cast_ref, weights_ref, total_ref) = refs[:8], refs[8:]
    own = units_ref.shape[0]
    tokens = cast_ref.shape[0]

    def rows_of(slot, start, size):
        return pl.ds(pl.multiple_of(place_ref[4 + slot] * own + start, size), size)

    cast_ref[rows_of(0, 0, own), :] = units_ref[...].astype(bf16)
    places = [(1, 0, own), (3, 0, own), (2, 0, own // 2), (2, own // 2, own // 2)]
    for core in range(2):

        @pl.when(place_ref[3] == core)
        def _(core=core):
            for i, ref in enumerate(piece_refs):
                kind = core if i < 4 else 1 - core
                cast_ref[rows_of(*places[i % 4]), kind * D : (kind + 1) * D] = ref[...].astype(bf16)

    weights_ref[...] = directions(protos_ref[...])
    total_ref[...] = jnp.zeros_like(total_ref)
    size = 512
    parts = [slice(c, c + size) for c in range(0, weights_ref.shape[0], size)]

    def step(i, carry):
        chunk = cast_ref[pl.ds(pl.multiple_of(i * WIDE, WIDE), WIDE), :][:, :D]
        logits = nt_dot(weights_ref[parts[0], :], chunk)
        for k, part in enumerate(parts):
            following = nt_dot(weights_ref[parts[k + 1], :], chunk) if k + 1 < len(parts) else None
            energy = jnp.exp2(logits * teacher_power)
            total = total_ref[part, :]
            for j in range(WIDE // LANES):
                tile = energy[:, j * LANES : (j + 1) * LANES]
                energy_ref[i * (WIDE // LANES) + j, part, :] = tile.astype(bf16)
                total = total + tile
            total_ref[part, :] = total
            logits = following
        return carry

    lax.fori_loop(0, tokens // WIDE, step, 0)
    totals = lane_totals(total_ref[...])
    for copy in range(sums_ref.shape[0]):
        sums_ref[copy] = totals


def fixed(*shape):
    return pl.BlockSpec(shape, lambda i: (0,) * len(shape))


def left(tokens):
    return pl.BlockSpec((tokens, D), lambda *i: (0, 0))


def right(tokens):
    return pl.BlockSpec((tokens, D), lambda *i: (0, 1))


def energy_of(place, units, pieces, protos, share, copies):
    own = units.shape[0]
    tokens = own * 4
    direct = pl.BlockSpec(memory_space=pltpu.VMEM)
    return pl.pallas_call(
        energy_body,
        grid_spec=pltpu.PrefetchScalarGridSpec(
            num_scalar_prefetch=1,
            grid=(1,),
            in_specs=[pl.BlockSpec(units.shape, lambda i, p: (0, 0))]
            + [direct] * len(pieces)
            + [pl.BlockSpec((share, D), lambda i, p: (p[0], 0))],
            out_specs=[
                direct,
                pl.BlockSpec((copies, share // LANES, LANES), lambda i, p: (0, 0, 0)),
                pl.BlockSpec((tokens, 2 * D), lambda i, p: (0, 0)),
            ],
            scratch_shapes=[pltpu.VMEM((share, D), bf16), pltpu.VMEM((share, LANES), f32)],
        ),
        out_shape=[
            pltpu.VMEM((tokens // LANES, share, LANES), bf16),
            jax.ShapeDtypeStruct((copies, share // LANES, LANES), f32),
            pltpu.HBM((tokens, 2 * D), bf16),
        ],
        compiler_params=params(24),
        cost_estimate=work(4 * tokens * share * D, 8 * 2**20, tokens * share),
        name="energy",
    )(place, in_hbm(units), *pieces, in_hbm(protos))


def student_body(units_ref, protos_ref, sums_ref, unit_ref, cast_ref, total_ref, buffer_ref, sems):
    size = buffer_ref.shape[0] // FETCHES
    fetch_all(units_ref, D, unit_ref, protos_ref, buffer_ref, sems)
    cast_ref[...] = unit_ref[...].astype(bf16)
    total_ref[...] = jnp.zeros_like(total_ref)

    def step(i, carry):
        fetch(protos_ref, buffer_ref, sems, i).wait()
        total = total_ref[...]

        def logits_of(part):
            rows = pl.ds(pl.multiple_of(i * size + part * WIDE, WIDE), WIDE)
            return nt_dot(cast_ref[...], directions(buffer_ref[rows, :]))

        parts = size // WIDE
        logits = logits_of(0)
        for part in range(parts):
            following = logits_of(part + 1) if part + 1 < parts else None
            values = jnp.exp2(logits * student_power)
            logits = following
            for j in range(WIDE // LANES):
                total = total + values[:, j * LANES : (j + 1) * LANES]
        total_ref[...] = total
        return carry

    lax.fori_loop(0, FETCHES, step, 0)
    sums_ref[...] = lane_totals(total_ref[...])


def student_sums(units, protos):
    tokens, count = units.shape[0], protos.shape[0]
    return pl.pallas_call(
        student_body,
        in_specs=[pl.BlockSpec(memory_space=pl.ANY)] * 2,
        out_specs=pl.BlockSpec(memory_space=pltpu.VMEM),
        out_shape=jax.ShapeDtypeStruct((tokens // LANES, LANES), f32),
        scratch_shapes=[
            pltpu.VMEM((tokens, D), f32),
            pltpu.VMEM((tokens, D), bf16),
            pltpu.VMEM((tokens, LANES), f32),
            pltpu.VMEM((count, D), bf16),
            pltpu.SemaphoreType.DMA((FETCHES + 1,)),
        ],
        compiler_params=params(16),
        cost_estimate=work(4 * tokens * count * D, 8 * 2**20, tokens * count),
        name="student",
    )(in_hbm(units), in_hbm(protos))


def right(tokens):
    return pl.BlockSpec((tokens, D), lambda *i: (0, 1))


def row_body(energy_ref, pieces_ref, *refs):
    norm_refs, (scale_ref, sums_ref, tile_ref) = refs[:-3], refs[-3:]
    scale_ref[...] = 1.0 / jnp.sum(pieces_ref[...], axis=0)
    fill_columns(scale_ref[...], tile_ref)
    tiles, protos, _ = energy_ref.shape
    size = 512
    totals = []
    for j in range(tiles):
        total = jnp.zeros((1, LANES), f32)
        for start in range(0, protos, size):
            part = slice(start, start + size)
            energy = energy_ref[j, part, :].astype(f32)
            total = total + jnp.sum(energy * tile_ref[part, :], axis=0, keepdims=True)
        totals.append(total)
    for ref in norm_refs:
        totals += [ref[...], jnp.zeros_like(ref)]
    totals = jnp.concatenate(totals, axis=0)
    for copy in range(sums_ref.shape[0]):
        sums_ref[copy] = totals


def row_sums(energy, pieces, copies, norm_part=()):
    tiles, protos, _ = energy.shape
    whole = pl.BlockSpec(memory_space=pltpu.VMEM)
    rows = tiles + 2 * sum(part.shape[0] for part in norm_part)
    return pl.pallas_call(
        row_body,
        in_specs=[whole] * (2 + len(norm_part)),
        out_specs=[whole] * 2,
        out_shape=[
            jax.ShapeDtypeStruct((protos // LANES, LANES), f32),
            jax.ShapeDtypeStruct((copies, rows, LANES), f32),
        ],
        scratch_shapes=[pltpu.VMEM((protos, LANES), f32)],
        compiler_params=params(12),
        cost_estimate=work(2 * energy.size, 0),
        name="row_sums",
    )(energy, pieces, *norm_part)


def column_body(energy_ref, pieces_ref, sums_ref, scale_ref):
    tiles, protos, _ = energy_ref.shape
    scale_ref[...] = 1.0 / jnp.sum(pieces_ref[...], axis=0)

    def step(k, carry):
        rows = pl.ds(pl.multiple_of(k * LANES, LANES), LANES)
        total = jnp.zeros((LANES, LANES), f32)
        for j in range(tiles):
            total = total + energy_ref[j, rows, :].astype(f32) * scale_ref[j : j + 1, :]
        sums_ref[0, pl.ds(k, 1), :] = lane_totals(total)
        return carry

    lax.fori_loop(0, protos // LANES, step, 0, unroll=4)
    for copy in range(1, sums_ref.shape[0]):
        sums_ref[copy] = sums_ref[0]


def column_sums(energy, pieces, copies):
    tiles, protos, _ = energy.shape
    whole = pl.BlockSpec(memory_space=pltpu.VMEM)
    return pl.pallas_call(
        column_body,
        in_specs=[whole] * 2,
        out_specs=whole,
        out_shape=jax.ShapeDtypeStruct((copies, protos // LANES, LANES), f32),
        scratch_shapes=[pltpu.VMEM((tiles, LANES), f32)],
        compiler_params=params(12),
        cost_estimate=work(2 * energy.size, 0),
        name="column_sums",
    )(energy, pieces)


LEFT_PLACE = [4, 5, 6, 7, 3, 2, 1, 0]
RIGHT_PLACE = [4, 0, 1, 2, 3, 7, 6, 5]


def collect(send, keep, offset):
    n = lax.axis_size("z")
    way = [1 if (z + offset) % 2 else -1 for z in range(n)]
    got = lax.ppermute(send, "z", [(z, (z - way[z]) % n) for z in range(n)])
    return keep[0] + got[0], keep[1] + got[1], keep[2:] + got[2:]


def pass_on(sums, offset):
    n = lax.axis_size("z")
    way = [1 if (z + offset) % 2 else -1 for z in range(n)]
    own, following, far = sums
    got = lax.ppermute(far, "z", [(z, (z + 2 * way[z]) % n) for z in range(n)])
    return own + got[0], following + got[1]


def deliver(sums, offset):
    n = lax.axis_size("z")
    way = [1 if (z + offset) % 2 else -1 for z in range(n)]
    own, following = sums
    return [own, lax.ppermute(following, "z", [(z, (z + way[z]) % n) for z in range(n)])]


def gradient_body(
    table_ref,
    units_ref,
    energy_ref,
    pieces_ref,
    sw_first_ref,
    sw_second_ref,
    scale_ref,
    send_left_ref,
    send_right_ref,
    keep_left_ref,
    keep_right_ref,
    feature_send_ref,
    feature_keep_ref,
    r_ref,
    n_ref,
    total_ref,
    feature_ref,
    stage_ref,
    sems,
):
    step = pl.program_id(0)
    tiles = energy_ref.shape[0]
    groups = pieces_ref.shape[0]
    own = tiles // groups

    @pl.when(step == 0)
    def _():
        scale = (1.0 / student_temp) / jnp.sum(pieces_ref[:, :, :tiles, :], axis=(0, 1))
        for k in range(tiles):
            r_ref[:, k * LANES : (k + 1) * LANES] = scale[k : k + 1, :]
        for group in range(groups):
            total = jnp.sum(pieces_ref[group, :, tiles : tiles + own, :], axis=0)
            inverse = (1.0 / student_temp) / total
            for k in range(own):
                lanes = slice((group * own + k) * LANES, (group * own + k + 1) * LANES)
                n_ref[:, lanes] = inverse[k : k + 1, :]
        feature_ref[...] = jnp.zeros_like(feature_ref)

    both = lambda first, second: jnp.concatenate([first, second], axis=0)
    block = sw_first_ref.shape[0]
    sw = both(directions(sw_first_ref[...]), directions(sw_second_ref[...]))
    local = [table_ref[3, 2 * step], table_ref[3, 2 * step + 1]]
    here = [pl.ds(pl.multiple_of(place * block, block), block) for place in local]
    columns = []
    for place in local:
        for k in range(block // LANES):
            row = scale_ref[pl.ds(place * (block // LANES) + k, 1), :]
            columns.append(to_column(row))
    col_scale = jnp.concatenate(columns, axis=0)

    def logits_of(part):
        return nt_dot(sw, units_ref[part, D:])

    parts = [slice(c, c + WIDE) for c in range(0, units_ref.shape[0], WIDE)]

    logits = logits_of(parts[0])
    for i, part in enumerate(parts):
        following = logits_of(parts[i + 1]) if i + 1 < len(parts) else None
        grads = []
        for j in range(WIDE // LANES):
            tile = i * (WIDE // LANES) + j
            lanes = slice(tile * LANES, (tile + 1) * LANES)
            energy = both(energy_ref[tile, here[0], :], energy_ref[tile, here[1], :]).astype(f32)
            probs = jnp.exp2(logits[:, j * LANES : (j + 1) * LANES] * student_power) * n_ref[:, lanes]
            grads.append((probs - energy * r_ref[:, lanes] * col_scale).astype(bf16))
        logit_grad = jnp.concatenate(grads, axis=1)
        added = jnp.dot(logit_grad, units_ref[part, D:], preferred_element_type=f32)
        total_ref[...] = added if i == 0 else total_ref[...] + added
        feature_ref[part, :] += lax.dot_general(
            logit_grad, sw, (((0,), (0,)), ((), ())), preferred_element_type=f32
        )
        logits = following

    def copies(which, at):
        found = []
        for half, (sent_ref, kept_ref) in enumerate(
            ((send_left_ref, keep_left_ref), (send_right_ref, keep_right_ref))
        ):
            block_at = 2 * at + which
            place = table_ref[1 + half, block_at]
            source, sem = stage_ref.at[half, block_at], sems.at[half, block_at]
            sent = pltpu.make_async_copy(source, sent_ref.at[jnp.minimum(place, 3)], sem)
            kept = pltpu.make_async_copy(source, kept_ref.at[jnp.maximum(place - 4, 0)], sem)
            found += [(place < 4, sent), (place >= 4, kept)]
        return found

    for which in range(2):
        rows_here = slice(which * block, (which + 1) * block)
        for half in range(2):
            columns_here = slice(half * (D // 2), (half + 1) * (D // 2))
            stage_ref[half, 2 * step + which] = total_ref[rows_here, columns_here]
        for wanted, copy in copies(which, step):
            pl.when(wanted)(copy.start)

    @pl.when(step == pl.num_programs(0) - 1)
    def _():
        size = feature_send_ref.shape[1]
        for core in range(2):

            @pl.when(table_ref[4, 0] == core)
            def _(core=core):
                for at in range(feature_ref.shape[0] // size):
                    out_ref = feature_keep_ref if at % 2 == core else feature_send_ref
                    out_ref[at // 2] = feature_ref[at * size : (at + 1) * size, :]

        for at in range(stage_ref.shape[1] // 2):
            for which in range(2):
                for wanted, copy in copies(which, at):
                    pl.when(wanted)(copy.wait)


def block_table(y, z, core):
    blocks = len(LEFT_PLACE)
    way = jnp.where(z % 2 == 1, 1, -1)
    local = (z + way * jnp.arange(blocks) + blocks) % blocks
    cores = jnp.full((blocks,), core)
    table = [y * blocks + local, jnp.array(LEFT_PLACE), jnp.array(RIGHT_PLACE), local, cores]
    return jnp.stack(table).astype(jnp.int32)


def gradients(table, units_all, energy, pieces, student_protos, scale, shares):
    tiles, share, _ = energy.shape
    tokens = units_all.shape[0]
    block = 256
    blocks = share // block
    whole = lambda *shape: pl.BlockSpec(shape, lambda i, p: (0,) * len(shape))
    first = pl.BlockSpec((block, D), lambda i, p: (p[0, 2 * i], 0))
    second = pl.BlockSpec((block, D), lambda i, p: (p[0, 2 * i + 1], 0))
    direct = pl.BlockSpec(memory_space=pltpu.VMEM)
    half = pltpu.HBM((blocks // 2, block, D // 2), f32)
    return pl.pallas_call(
        gradient_body,
        grid_spec=pltpu.PrefetchScalarGridSpec(
            num_scalar_prefetch=1,
            grid=(blocks // 2,),
            in_specs=[
                whole(tokens, 2 * D),
                direct,
                whole(*pieces.shape),
                first,
                second,
                whole(*scale.shape),
            ],
            out_specs=[pl.BlockSpec(memory_space=pl.ANY)] * 4 + [direct] * 2,
            scratch_shapes=[
                pltpu.VMEM((1, tokens), f32),
                pltpu.VMEM((1, tokens), f32),
                pltpu.VMEM((2 * block, D), f32),
                pltpu.VMEM((tokens, D), f32),
                pltpu.VMEM((2, blocks, block, D // 2), f32),
                pltpu.SemaphoreType.DMA((2, blocks)),
            ],
        ),
        out_shape=[half] * 4 + [pltpu.VMEM((shares // 2, tokens // shares, D), f32)] * 2,
        compiler_params=params(24),
        cost_estimate=work(8 * tokens * share * D, 8 * 2**20, tokens * share),
        name="gradients",
    )(
        table,
        in_hbm(units_all),
        energy,
        pieces,
        in_hbm(student_protos),
        in_hbm(student_protos),
        scale,
    )


def project(total, unit, length):
    return (total - unit * jnp.sum(unit * total, axis=-1, keepdims=True)) / length


def student_end_body(place_ref, pieces_ref, unit_ref, length_ref, out_ref):
    result = project(jnp.sum(pieces_ref[...], axis=0), unit_ref[...], length_ref[...])
    for copy in range(out_ref.shape[0]):
        out_ref[copy] = result


def student_end(place, pieces, units, length, copies):
    _, rows, _ = pieces.shape
    return pl.pallas_call(
        student_end_body,
        grid_spec=pltpu.PrefetchScalarGridSpec(
            num_scalar_prefetch=1,
            grid=(1,),
            in_specs=[
                pl.BlockSpec(memory_space=pltpu.VMEM),
                pl.BlockSpec((rows, D), lambda i, p: (p[2], 1)),
                pl.BlockSpec((rows, 1), lambda i, p: (p[2], 0)),
            ],
            out_specs=pl.BlockSpec((copies, rows, D), lambda i, p: (0, 0, 0)),
        ),
        out_shape=jax.ShapeDtypeStruct((copies, rows, D), f32),
        compiler_params=params(8),
        name="student_end",
    )(place, pieces, in_hbm(units), in_hbm(length))


def proto_end_body(place_ref, *refs):
    piece_refs, (protos_ref, out_ref) = refs[:-2], refs[-2:]
    unit, length = unit_rows(protos_ref[...].astype(f32))
    half = len(piece_refs) // 2
    sums = []
    for group in (piece_refs[:half], piece_refs[half:]):
        total = group[0][...]
        for ref in group[1:]:
            total = total + ref[...]
        sums.append(total)
    out_ref[...] = project(jnp.concatenate(sums, axis=1), unit, length)


def proto_end(place, pieces, protos):
    rows, width = pieces[0].shape
    return pl.pallas_call(
        proto_end_body,
        grid_spec=pltpu.PrefetchScalarGridSpec(
            num_scalar_prefetch=1,
            grid=(1,),
            in_specs=[pl.BlockSpec(memory_space=pltpu.VMEM)] * len(pieces)
            + [pl.BlockSpec((rows, D), lambda i, p: (p[1], 0))],
            out_specs=pl.BlockSpec((rows, D), lambda i, p: (0, 0)),
        ),
        out_shape=jax.ShapeDtypeStruct((rows, D), f32),
        compiler_params=params(8),
        name="proto_end",
    )(place, *pieces, in_hbm(protos))


def on_device(teacher_patches, student_patches, mask_order, teacher_protos, student_protos):
    y_size, z_size = lax.axis_size("y"), lax.axis_size("z")
    proto_size = lax.axis_size("x") * lax.axis_size("core")
    y, z = lax.axis_index("y"), lax.axis_index("z")
    others = [(y - step + y_size) % y_size for step in range(y_size)]
    core = lax.axis_index("core")
    place = [y, y * z_size + z, lax.axis_index(PROTOS), core] + others
    place = jnp.stack(place).astype(jnp.int32)
    table = block_table(y, z, core)
    share = teacher_protos.shape[0] // y_size

    units, student_length, mine = select_tokens(
        core.astype(jnp.int32)[None], teacher_patches, student_patches, mask_order
    )
    from_y = lambda value, step: lax.ppermute(
        value, "y", [(i, (i + step) % y_size) for i in range(y_size)]
    )
    from_core = lambda value: lax.ppermute(value, "core", [(0, 1), (1, 0)])
    half = mine.shape[0] // 2
    first, third = from_y(mine, 1), from_y(mine, 3)
    norm_part = student_sums(units, student_protos)
    norm_part, first, third, place, table = lax.optimization_barrier(
        (norm_part, first, third, place, table)
    )
    got = [first, third, from_y(first[:half], 1), from_y(third[half:], 3)]
    got = got + [from_core(piece) for piece in got]

    rows = ("y",) + PROTOS
    peers = y_size * proto_size
    energy, sums, units_all = energy_of(place, units, got, teacher_protos, share, z_size)
    for sweep in range(ITERS):
        if sweep > 0:
            sums = column_sums(energy, pieces, z_size)
        norms = (norm_part,) if sweep == ITERS - 1 else ()
        col_scale, row_part = row_sums(energy, spread(sums, "z"), peers, norms)
        pieces = spread(row_part, rows)
    pieces = pieces.reshape((y_size, proto_size) + pieces.shape[1:])

    send_left, send_right, keep_left, keep_right, feature_send, feature_keep = gradients(
        table, units_all, energy, pieces, student_protos, col_scale, peers
    )
    feature_part = feature_keep + from_core(feature_send)
    feature_part, keep_left, keep_right = lax.optimization_barrier(
        (feature_part, keep_left, keep_right)
    )
    left = pass_on(collect(send_left, keep_left, 0), 0)
    right_half = pass_on(collect(send_right, keep_right, 1), 1)
    feature_pieces = spread(feature_part, ("y", "x"))
    feature_pieces, left, right_half = lax.optimization_barrier((feature_pieces, left, right_half))
    left, right_half = deliver(left, 0), deliver(right_half, 1)
    result = student_end(place, feature_pieces, units, student_length, proto_size)
    result = spread(result, PROTOS)
    grad_protos = proto_end(place, left + right_half, student_protos)
    return (result.reshape(-1, MASKED, D), grad_protos)


def solution(mesh):
    fine = Mesh(mesh.devices.reshape(4, 8, 4, 2), ("y", "z", "x", "core"))
    return jax.shard_map(
        on_device,
        mesh=fine,
        in_specs=(
            P(ROWS, None, None),
            P(ROWS, None, None),
            P(ROWS, None),
            P(PROTOS, None),
            P(PROTOS, None),
        ),
        out_specs=(P(ROWS, None, None), P(PROTOS + ROWS, None)),
        check_vma=False,
    )
```

```python
import math

import jax
import jax.numpy as jnp
from jax import lax
from jax.experimental import pallas as pl
from jax.experimental.pallas import tpu as pltpu
from jax.sharding import Mesh, PartitionSpec as P

D = 256
MASKED = 128
ITERS = 3
LANES = 128

teacher_temp = 0.07
student_temp = 0.1
epsilon = 1e-06

teacher_power = math.log2(math.e) / teacher_temp
student_power = math.log2(math.e) / student_temp

ROWS = ("y", "z")
PROTOS = ("x", "core")

f32 = jnp.float32
bf16 = jnp.bfloat16


def params(mib):
    return pltpu.CompilerParams(vmem_limit_bytes=mib * 2**20)


def spread(value, axes):
    return lax.all_to_all(value, axes, 0, 0, tiled=True)


def work(flops, moved, powers=0):
    return pl.CostEstimate(flops=int(flops), bytes_accessed=int(moved), transcendentals=int(powers))


def in_hbm(value):
    return pltpu.with_memory_space_constraint(value, pltpu.HBM)


def nt_dot(a, b):
    return lax.dot_general(a, b, (((1,), (1,)), ((), ())), preferred_element_type=f32)


def unit_rows(values):
    length = jnp.sqrt(jnp.sum(values * values, axis=-1, keepdims=True) + epsilon)
    return (values / length, length)


def directions(values):
    values = values.astype(f32)
    return (values * lax.rsqrt(jnp.sum(values * values, axis=-1, keepdims=True) + epsilon)).astype(bf16)


def to_column(row):
    return jnp.broadcast_to(row, (LANES, LANES)).T


def fill_columns(rows, tile_ref):
    for k in range(rows.shape[0]):
        tile_ref[k * LANES : (k + 1) * LANES, :] = to_column(rows[k : k + 1, :])


def lane_totals(tile):
    parts = [
        jnp.sum(tile[k * LANES : (k + 1) * LANES, :].T, axis=0, keepdims=True)
        for k in range(tile.shape[0] // LANES)
    ]
    return jnp.concatenate(parts, axis=0)


def select_body(core_ref, teacher_ref, student_ref, order_ref, units_ref, length_ref, top_ref, bottom_ref):
    images, patches, _ = teacher_ref.shape
    for image in range(images):
        chosen = order_ref[image : image + 1, :MASKED]
        place = lax.broadcasted_iota(jnp.int32, (patches, MASKED), 0)
        onehot = jnp.where(place == chosen, 1.0, 0.0).astype(bf16)

        def pick(ref):
            return lax.dot_general(
                onehot, ref[image], (((0,), (0,)), ((), ())), preferred_element_type=f32
            )

        rows = slice(image * MASKED, (image + 1) * MASKED)
        teacher = unit_rows(pick(teacher_ref))[0]
        student, length_ref[rows, :] = unit_rows(pick(student_ref))
        units_ref[rows, :D] = teacher
        units_ref[rows, D:] = student
        mine = jnp.where(core_ref[0] == 0, teacher, student)
        half = top_ref.shape[0]
        if image * MASKED < half:
            top_ref[rows, :] = mine
        else:
            bottom_ref[image * MASKED - half : (image + 1) * MASKED - half, :] = mine


def select_tokens(core, teacher_patches, student_patches, mask_order):
    tokens = teacher_patches.shape[0] * MASKED
    return pl.pallas_call(
        select_body,
        in_specs=[pl.BlockSpec(memory_space=pltpu.SMEM)]
        + [pl.BlockSpec(memory_space=pltpu.VMEM)] * 3,
        out_specs=[pl.BlockSpec(memory_space=pltpu.VMEM)] * 4,
        out_shape=[
            pltpu.HBM((tokens, 2 * D), f32),
            pltpu.HBM((tokens, 1), f32),
            pltpu.HBM((tokens // 2, D), f32),
            pltpu.HBM((tokens // 2, D), f32),
        ],
        compiler_params=params(8),
        name="select",
    )(core, in_hbm(teacher_patches), in_hbm(student_patches), in_hbm(mask_order))


def lane_rows(row):
    parts = [row[:, j * LANES : (j + 1) * LANES] for j in range(row.shape[1] // LANES)]
    return jnp.concatenate(parts, axis=0)


def chunks(tokens):
    return [slice(c, c + LANES) for c in range(0, tokens, LANES)]


FETCHES = 8
WIDE = 256


def fetch(protos_ref, buffer_ref, sems, i):
    size = buffer_ref.shape[0] // FETCHES
    rows = pl.ds(pl.multiple_of(i * size, size), size)
    return pltpu.make_async_copy(protos_ref.at[rows, :], buffer_ref.at[rows, :], sems.at[i])


def fetch_all(units_ref, column, unit_ref, protos_ref, buffer_ref, sems):
    units = pltpu.make_async_copy(
        units_ref.at[:, pl.ds(column, D)], unit_ref, sems.at[FETCHES]
    )
    units.start()
    for i in range(FETCHES):
        fetch(protos_ref, buffer_ref, sems, i).start()
    units.wait()


def energy_body(
    place_ref, units_ref, *refs
):
    piece_refs, (protos_ref, energy_ref, sums_ref, cast_ref, weights_ref, total_ref) = refs[:12], refs[12:]
    own = units_ref.shape[0]
    tokens = cast_ref.shape[0]

    def rows_of(slot, start, size):
        return pl.ds(pl.multiple_of(place_ref[4 + slot] * own + start, size), size)

    cast_ref[rows_of(0, 0, own), :] = units_ref[...].astype(bf16)
    places = [(slot, start, own // 2) for slot in (1, 3, 2) for start in (0, own // 2)]
    for core in range(2):

        @pl.when(place_ref[3] == core)
        def _(core=core):
            for i, ref in enumerate(piece_refs):
                kind = core if i < len(places) else 1 - core
                rows = rows_of(*places[i % len(places)])
                cast_ref[rows, kind * D : (kind + 1) * D] = ref[...].astype(bf16)

    weights_ref[...] = directions(protos_ref[...])
    total_ref[...] = jnp.zeros_like(total_ref)
    size = 512
    parts = [slice(c, c + size) for c in range(0, weights_ref.shape[0], size)]

    def step(i, carry):
        chunk = cast_ref[pl.ds(pl.multiple_of(i * WIDE, WIDE), WIDE), :][:, :D]
        logits = nt_dot(weights_ref[parts[0], :], chunk)
        for k, part in enumerate(parts):
            following = nt_dot(weights_ref[parts[k + 1], :], chunk) if k + 1 < len(parts) else None
            energy = jnp.exp2(logits * teacher_power)
            total = total_ref[part, :]
            for j in range(WIDE // LANES):
                tile = energy[:, j * LANES : (j + 1) * LANES]
                energy_ref[i * (WIDE // LANES) + j, part, :] = tile.astype(bf16)
                total = total + tile
            total_ref[part, :] = total
            logits = following
        return carry

    lax.fori_loop(0, tokens // WIDE, step, 0)
    totals = lane_totals(total_ref[...])
    for copy in range(sums_ref.shape[0]):
        sums_ref[copy] = totals


def fixed(*shape):
    return pl.BlockSpec(shape, lambda i: (0,) * len(shape))


def left(tokens):
    return pl.BlockSpec((tokens, D), lambda *i: (0, 0))


def right(tokens):
    return pl.BlockSpec((tokens, D), lambda *i: (0, 1))


def energy_of(place, units, pieces, protos, share, copies):
    own = units.shape[0]
    tokens = own * 4
    direct = pl.BlockSpec(memory_space=pltpu.VMEM)
    return pl.pallas_call(
        energy_body,
        grid_spec=pltpu.PrefetchScalarGridSpec(
            num_scalar_prefetch=1,
            grid=(1,),
            in_specs=[pl.BlockSpec(units.shape, lambda i, p: (0, 0))]
            + [direct] * len(pieces)
            + [pl.BlockSpec((share, D), lambda i, p: (p[0], 0))],
            out_specs=[
                direct,
                pl.BlockSpec((copies, share // LANES, LANES), lambda i, p: (0, 0, 0)),
                pl.BlockSpec((tokens, 2 * D), lambda i, p: (0, 0)),
            ],
            scratch_shapes=[pltpu.VMEM((share, D), bf16), pltpu.VMEM((share, LANES), f32)],
        ),
        out_shape=[
            pltpu.VMEM((tokens // LANES, share, LANES), bf16),
            jax.ShapeDtypeStruct((copies, share // LANES, LANES), f32),
            pltpu.HBM((tokens, 2 * D), bf16),
        ],
        compiler_params=params(24),
        cost_estimate=work(4 * tokens * share * D, 8 * 2**20, tokens * share),
        name="energy",
    )(place, in_hbm(units), *pieces, in_hbm(protos))


def student_body(units_ref, protos_ref, sums_ref, unit_ref, cast_ref, total_ref, buffer_ref, sems):
    size = buffer_ref.shape[0] // FETCHES
    fetch_all(units_ref, D, unit_ref, protos_ref, buffer_ref, sems)
    cast_ref[...] = unit_ref[...].astype(bf16)
    total_ref[...] = jnp.zeros_like(total_ref)

    def step(i, carry):
        fetch(protos_ref, buffer_ref, sems, i).wait()
        total = total_ref[...]

        def logits_of(part):
            rows = pl.ds(pl.multiple_of(i * size + part * WIDE, WIDE), WIDE)
            return nt_dot(cast_ref[...], directions(buffer_ref[rows, :]))

        parts = size // WIDE
        logits = logits_of(0)
        for part in range(parts):
            following = logits_of(part + 1) if part + 1 < parts else None
            values = jnp.exp2(logits * student_power)
            logits = following
            for j in range(WIDE // LANES):
                total = total + values[:, j * LANES : (j + 1) * LANES]
        total_ref[...] = total
        return carry

    lax.fori_loop(0, FETCHES, step, 0)
    sums_ref[...] = lane_totals(total_ref[...])


def student_sums(units, protos):
    tokens, count = units.shape[0], protos.shape[0]
    return pl.pallas_call(
        student_body,
        in_specs=[pl.BlockSpec(memory_space=pl.ANY)] * 2,
        out_specs=pl.BlockSpec(memory_space=pltpu.VMEM),
        out_shape=jax.ShapeDtypeStruct((tokens // LANES, LANES), f32),
        scratch_shapes=[
            pltpu.VMEM((tokens, D), f32),
            pltpu.VMEM((tokens, D), bf16),
            pltpu.VMEM((tokens, LANES), f32),
            pltpu.VMEM((count, D), bf16),
            pltpu.SemaphoreType.DMA((FETCHES + 1,)),
        ],
        compiler_params=params(16),
        cost_estimate=work(4 * tokens * count * D, 8 * 2**20, tokens * count),
        name="student",
    )(in_hbm(units), in_hbm(protos))


def right(tokens):
    return pl.BlockSpec((tokens, D), lambda *i: (0, 1))


def row_body(energy_ref, pieces_ref, *refs):
    norm_refs, (scale_ref, sums_ref, tile_ref) = refs[:-3], refs[-3:]
    scale_ref[...] = 1.0 / jnp.sum(pieces_ref[...], axis=0)
    fill_columns(scale_ref[...], tile_ref)
    tiles, protos, _ = energy_ref.shape
    size = 512
    totals = []
    for j in range(tiles):
        total = jnp.zeros((1, LANES), f32)
        for start in range(0, protos, size):
            part = slice(start, start + size)
            energy = energy_ref[j, part, :].astype(f32)
            total = total + jnp.sum(energy * tile_ref[part, :], axis=0, keepdims=True)
        totals.append(total)
    for ref in norm_refs:
        totals += [ref[...], jnp.zeros_like(ref)]
    totals = jnp.concatenate(totals, axis=0)
    for copy in range(sums_ref.shape[0]):
        sums_ref[copy] = totals


def row_sums(energy, pieces, copies, norm_part=()):
    tiles, protos, _ = energy.shape
    whole = pl.BlockSpec(memory_space=pltpu.VMEM)
    rows = tiles + 2 * sum(part.shape[0] for part in norm_part)
    return pl.pallas_call(
        row_body,
        in_specs=[whole] * (2 + len(norm_part)),
        out_specs=[whole] * 2,
        out_shape=[
            jax.ShapeDtypeStruct((protos // LANES, LANES), f32),
            jax.ShapeDtypeStruct((copies, rows, LANES), f32),
        ],
        scratch_shapes=[pltpu.VMEM((protos, LANES), f32)],
        compiler_params=params(12),
        cost_estimate=work(2 * energy.size, 0),
        name="row_sums",
    )(energy, pieces, *norm_part)


def column_body(energy_ref, pieces_ref, sums_ref, scale_ref):
    tiles, protos, _ = energy_ref.shape
    scale_ref[...] = 1.0 / jnp.sum(pieces_ref[...], axis=0)

    def step(k, carry):
        rows = pl.ds(pl.multiple_of(k * LANES, LANES), LANES)
        total = jnp.zeros((LANES, LANES), f32)
        for j in range(tiles):
            total = total + energy_ref[j, rows, :].astype(f32) * scale_ref[j : j + 1, :]
        sums_ref[0, pl.ds(k, 1), :] = lane_totals(total)
        return carry

    lax.fori_loop(0, protos // LANES, step, 0, unroll=4)
    for copy in range(1, sums_ref.shape[0]):
        sums_ref[copy] = sums_ref[0]


def column_sums(energy, pieces, copies):
    tiles, protos, _ = energy.shape
    whole = pl.BlockSpec(memory_space=pltpu.VMEM)
    return pl.pallas_call(
        column_body,
        in_specs=[whole] * 2,
        out_specs=whole,
        out_shape=jax.ShapeDtypeStruct((copies, protos // LANES, LANES), f32),
        scratch_shapes=[pltpu.VMEM((tiles, LANES), f32)],
        compiler_params=params(12),
        cost_estimate=work(2 * energy.size, 0),
        name="column_sums",
    )(energy, pieces)


LEFT_PLACE = [4, 5, 6, 7, 3, 2, 1, 0]
RIGHT_PLACE = [4, 0, 1, 2, 3, 7, 6, 5]


def collect(send, keep, offset):
    n = lax.axis_size("z")
    way = [1 if (z + offset) % 2 else -1 for z in range(n)]
    got = lax.ppermute(send, "z", [(z, (z - way[z]) % n) for z in range(n)])
    return keep[0] + got[0], keep[1] + got[1], keep[2:] + got[2:]


def pass_on(sums, offset):
    n = lax.axis_size("z")
    way = [1 if (z + offset) % 2 else -1 for z in range(n)]
    own, following, far = sums
    got = lax.ppermute(far, "z", [(z, (z + 2 * way[z]) % n) for z in range(n)])
    return own + got[0], following + got[1]


def deliver(sums, offset):
    n = lax.axis_size("z")
    way = [1 if (z + offset) % 2 else -1 for z in range(n)]
    own, following = sums
    return [own, lax.ppermute(following, "z", [(z, (z + way[z]) % n) for z in range(n)])]


def gradient_body(
    table_ref,
    units_ref,
    energy_ref,
    pieces_ref,
    sw_first_ref,
    sw_second_ref,
    scale_ref,
    send_left_ref,
    send_right_ref,
    keep_left_ref,
    keep_right_ref,
    feature_send_ref,
    feature_keep_ref,
    r_ref,
    n_ref,
    total_ref,
    feature_ref,
    stage_ref,
    sems,
):
    step = pl.program_id(0)
    tiles = energy_ref.shape[0]
    groups = pieces_ref.shape[0]
    own = tiles // groups

    @pl.when(step == 0)
    def _():
        scale = (1.0 / student_temp) / jnp.sum(pieces_ref[:, :, :tiles, :], axis=(0, 1))
        for k in range(tiles):
            r_ref[:, k * LANES : (k + 1) * LANES] = scale[k : k + 1, :]
        for group in range(groups):
            total = jnp.sum(pieces_ref[group, :, tiles : tiles + own, :], axis=0)
            inverse = (1.0 / student_temp) / total
            for k in range(own):
                lanes = slice((group * own + k) * LANES, (group * own + k + 1) * LANES)
                n_ref[:, lanes] = inverse[k : k + 1, :]
        feature_ref[...] = jnp.zeros_like(feature_ref)

    both = lambda first, second: jnp.concatenate([first, second], axis=0)
    block = sw_first_ref.shape[0]
    sw = both(directions(sw_first_ref[...]), directions(sw_second_ref[...]))
    local = [table_ref[3, 2 * step], table_ref[3, 2 * step + 1]]
    here = [pl.ds(pl.multiple_of(place * block, block), block) for place in local]
    columns = []
    for place in local:
        for k in range(block // LANES):
            row = scale_ref[pl.ds(place * (block // LANES) + k, 1), :]
            columns.append(to_column(row))
    col_scale = jnp.concatenate(columns, axis=0)

    def logits_of(part):
        return nt_dot(sw, units_ref[part, D:])

    parts = [slice(c, c + WIDE) for c in range(0, units_ref.shape[0], WIDE)]

    logits = logits_of(parts[0])
    for i, part in enumerate(parts):
        following = logits_of(parts[i + 1]) if i + 1 < len(parts) else None
        grads = []
        for j in range(WIDE // LANES):
            tile = i * (WIDE // LANES) + j
            lanes = slice(tile * LANES, (tile + 1) * LANES)
            energy = both(energy_ref[tile, here[0], :], energy_ref[tile, here[1], :]).astype(f32)
            probs = jnp.exp2(logits[:, j * LANES : (j + 1) * LANES] * student_power) * n_ref[:, lanes]
            grads.append((probs - energy * r_ref[:, lanes] * col_scale).astype(bf16))
        logit_grad = jnp.concatenate(grads, axis=1)
        added = jnp.dot(logit_grad, units_ref[part, D:], preferred_element_type=f32)
        total_ref[...] = added if i == 0 else total_ref[...] + added
        feature_ref[part, :] += lax.dot_general(
            logit_grad, sw, (((0,), (0,)), ((), ())), preferred_element_type=f32
        )
        logits = following

    def copies(which, at):
        found = []
        for half, (sent_ref, kept_ref) in enumerate(
            ((send_left_ref, keep_left_ref), (send_right_ref, keep_right_ref))
        ):
            block_at = 2 * at + which
            place = table_ref[1 + half, block_at]
            source, sem = stage_ref.at[half, block_at], sems.at[half, block_at]
            sent = pltpu.make_async_copy(source, sent_ref.at[jnp.minimum(place, 3)], sem)
            kept = pltpu.make_async_copy(source, kept_ref.at[jnp.maximum(place - 4, 0)], sem)
            found += [(place < 4, sent), (place >= 4, kept)]
        return found

    for which in range(2):
        rows_here = slice(which * block, (which + 1) * block)
        for half in range(2):
            columns_here = slice(half * (D // 2), (half + 1) * (D // 2))
            stage_ref[half, 2 * step + which] = total_ref[rows_here, columns_here]
        for wanted, copy in copies(which, step):
            pl.when(wanted)(copy.start)

    @pl.when(step == pl.num_programs(0) - 1)
    def _():
        size = feature_send_ref.shape[1]
        for core in range(2):

            @pl.when(table_ref[4, 0] == core)
            def _(core=core):
                for at in range(feature_ref.shape[0] // size):
                    out_ref = feature_keep_ref if at % 2 == core else feature_send_ref
                    out_ref[at // 2] = feature_ref[at * size : (at + 1) * size, :]

        for at in range(stage_ref.shape[1] // 2):
            for which in range(2):
                for wanted, copy in copies(which, at):
                    pl.when(wanted)(copy.wait)


def block_table(y, z, core):
    blocks = len(LEFT_PLACE)
    way = jnp.where(z % 2 == 1, 1, -1)
    local = (z + way * jnp.arange(blocks) + blocks) % blocks
    cores = jnp.full((blocks,), core)
    table = [y * blocks + local, jnp.array(LEFT_PLACE), jnp.array(RIGHT_PLACE), local, cores]
    return jnp.stack(table).astype(jnp.int32)


def gradients(table, units_all, energy, pieces, student_protos, scale, shares):
    tiles, share, _ = energy.shape
    tokens = units_all.shape[0]
    block = 256
    blocks = share // block
    whole = lambda *shape: pl.BlockSpec(shape, lambda i, p: (0,) * len(shape))
    first = pl.BlockSpec((block, D), lambda i, p: (p[0, 2 * i], 0))
    second = pl.BlockSpec((block, D), lambda i, p: (p[0, 2 * i + 1], 0))
    direct = pl.BlockSpec(memory_space=pltpu.VMEM)
    half = pltpu.HBM((blocks // 2, block, D // 2), f32)
    return pl.pallas_call(
        gradient_body,
        grid_spec=pltpu.PrefetchScalarGridSpec(
            num_scalar_prefetch=1,
            grid=(blocks // 2,),
            in_specs=[
                whole(tokens, 2 * D),
                direct,
                whole(*pieces.shape),
                first,
                second,
                whole(*scale.shape),
            ],
            out_specs=[pl.BlockSpec(memory_space=pl.ANY)] * 4 + [direct] * 2,
            scratch_shapes=[
                pltpu.VMEM((1, tokens), f32),
                pltpu.VMEM((1, tokens), f32),
                pltpu.VMEM((2 * block, D), f32),
                pltpu.VMEM((tokens, D), f32),
                pltpu.VMEM((2, blocks, block, D // 2), f32),
                pltpu.SemaphoreType.DMA((2, blocks)),
            ],
        ),
        out_shape=[half] * 4 + [pltpu.VMEM((shares // 2, tokens // shares, D), f32)] * 2,
        compiler_params=params(24),
        cost_estimate=work(8 * tokens * share * D, 8 * 2**20, tokens * share),
        name="gradients",
    )(
        table,
        in_hbm(units_all),
        energy,
        pieces,
        in_hbm(student_protos),
        in_hbm(student_protos),
        scale,
    )


def project(total, unit, length):
    return (total - unit * jnp.sum(unit * total, axis=-1, keepdims=True)) / length


def student_end_body(place_ref, pieces_ref, unit_ref, length_ref, out_ref):
    result = project(jnp.sum(pieces_ref[...], axis=0), unit_ref[...], length_ref[...])
    for copy in range(out_ref.shape[0]):
        out_ref[copy] = result


def student_end(place, pieces, units, length, copies):
    _, rows, _ = pieces.shape
    return pl.pallas_call(
        student_end_body,
        grid_spec=pltpu.PrefetchScalarGridSpec(
            num_scalar_prefetch=1,
            grid=(1,),
            in_specs=[
                pl.BlockSpec(memory_space=pltpu.VMEM),
                pl.BlockSpec((rows, D), lambda i, p: (p[2], 1)),
                pl.BlockSpec((rows, 1), lambda i, p: (p[2], 0)),
            ],
            out_specs=pl.BlockSpec((copies, rows, D), lambda i, p: (0, 0, 0)),
        ),
        out_shape=jax.ShapeDtypeStruct((copies, rows, D), f32),
        compiler_params=params(8),
        name="student_end",
    )(place, pieces, in_hbm(units), in_hbm(length))


def proto_end_body(place_ref, *refs):
    piece_refs, (protos_ref, out_ref) = refs[:-2], refs[-2:]
    unit, length = unit_rows(protos_ref[...].astype(f32))
    half = len(piece_refs) // 2
    sums = []
    for group in (piece_refs[:half], piece_refs[half:]):
        total = group[0][...]
        for ref in group[1:]:
            total = total + ref[...]
        sums.append(total)
    out_ref[...] = project(jnp.concatenate(sums, axis=1), unit, length)


def proto_end(place, pieces, protos):
    rows, width = pieces[0].shape
    return pl.pallas_call(
        proto_end_body,
        grid_spec=pltpu.PrefetchScalarGridSpec(
            num_scalar_prefetch=1,
            grid=(1,),
            in_specs=[pl.BlockSpec(memory_space=pltpu.VMEM)] * len(pieces)
            + [pl.BlockSpec((rows, D), lambda i, p: (p[1], 0))],
            out_specs=pl.BlockSpec((rows, D), lambda i, p: (0, 0)),
        ),
        out_shape=jax.ShapeDtypeStruct((rows, D), f32),
        compiler_params=params(8),
        name="proto_end",
    )(place, *pieces, in_hbm(protos))


def on_device(teacher_patches, student_patches, mask_order, teacher_protos, student_protos):
    y_size, z_size = lax.axis_size("y"), lax.axis_size("z")
    proto_size = lax.axis_size("x") * lax.axis_size("core")
    y, z = lax.axis_index("y"), lax.axis_index("z")
    others = [(y - step + y_size) % y_size for step in range(y_size)]
    core = lax.axis_index("core")
    place = [y, y * z_size + z, lax.axis_index(PROTOS), core] + others
    place = jnp.stack(place).astype(jnp.int32)
    table = block_table(y, z, core)
    share = teacher_protos.shape[0] // y_size

    units, student_length, top, bottom = select_tokens(
        core.astype(jnp.int32)[None], teacher_patches, student_patches, mask_order
    )
    from_y = lambda value, step: lax.ppermute(
        value, "y", [(i, (i + step) % y_size) for i in range(y_size)]
    )
    from_core = lambda value: lax.ppermute(value, "core", [(0, 1), (1, 0)])
    first_top, third_bottom = from_y(top, 1), from_y(bottom, 3)
    first_bottom, third_top = from_y(bottom, 1), from_y(top, 3)
    units, first_top, third_bottom = lax.optimization_barrier((units, first_top, third_bottom))
    second_top, second_bottom = from_y(first_top, 1), from_y(third_bottom, 3)
    norm_part = student_sums(units, student_protos)
    got = [first_top, first_bottom, third_top, third_bottom, second_top, second_bottom]
    norm_part, got, place, table = lax.optimization_barrier((norm_part, got, place, table))
    got = got + [from_core(piece) for piece in got]

    rows = ("y",) + PROTOS
    peers = y_size * proto_size
    energy, sums, units_all = energy_of(place, units, got, teacher_protos, share, z_size)
    for sweep in range(ITERS):
        if sweep > 0:
            sums = column_sums(energy, pieces, z_size)
        norms = (norm_part,) if sweep == ITERS - 1 else ()
        col_scale, row_part = row_sums(energy, spread(sums, "z"), peers, norms)
        pieces = spread(row_part, rows)
    pieces = pieces.reshape((y_size, proto_size) + pieces.shape[1:])

    send_left, send_right, keep_left, keep_right, feature_send, feature_keep = gradients(
        table, units_all, energy, pieces, student_protos, col_scale, peers
    )
    feature_part = feature_keep + from_core(feature_send)
    feature_part, keep_left, keep_right = lax.optimization_barrier(
        (feature_part, keep_left, keep_right)
    )
    left, right_half = collect(send_left, keep_left, 0), collect(send_right, keep_right, 1)
    feature_pieces = spread(feature_part, ("y", "x"))
    feature_pieces, _, _ = lax.optimization_barrier((feature_pieces, left, right_half))
    left, right_half = pass_on(left, 0), pass_on(right_half, 1)
    left, right_half = deliver(left, 0), deliver(right_half, 1)
    result = student_end(place, feature_pieces, units, student_length, proto_size)
    result = spread(result, PROTOS)
    grad_protos = proto_end(place, left + right_half, student_protos)
    return (result.reshape(-1, MASKED, D), grad_protos)


def solution(mesh):
    fine = Mesh(mesh.devices.reshape(4, 8, 4, 2), ("y", "z", "x", "core"))
    return jax.shard_map(
        on_device,
        mesh=fine,
        in_specs=(
            P(ROWS, None, None),
            P(ROWS, None, None),
            P(ROWS, None),
            P(PROTOS, None),
            P(PROTOS, None),
        ),
        out_specs=(P(ROWS, None, None), P(PROTOS + ROWS, None)),
        check_vma=False,
    )
```

```python
import math

import jax
import jax.numpy as jnp
from jax import lax
from jax.experimental import pallas as pl
from jax.experimental.pallas import tpu as pltpu
from jax.sharding import Mesh, PartitionSpec as P

D = 256
MASKED = 128
ITERS = 3
LANES = 128

teacher_temp = 0.07
student_temp = 0.1
epsilon = 1e-06

teacher_power = math.log2(math.e) / teacher_temp
student_power = math.log2(math.e) / student_temp

ROWS = ("y", "z")
PROTOS = ("x", "core")

f32 = jnp.float32
bf16 = jnp.bfloat16


def params(mib):
    return pltpu.CompilerParams(vmem_limit_bytes=mib * 2**20)


def spread(value, axes):
    return lax.all_to_all(value, axes, 0, 0, tiled=True)


def work(flops, moved, powers=0):
    return pl.CostEstimate(flops=int(flops), bytes_accessed=int(moved), transcendentals=int(powers))


def in_hbm(value):
    return pltpu.with_memory_space_constraint(value, pltpu.HBM)


def nt_dot(a, b):
    return lax.dot_general(a, b, (((1,), (1,)), ((), ())), preferred_element_type=f32)


def unit_rows(values):
    length = jnp.sqrt(jnp.sum(values * values, axis=-1, keepdims=True) + epsilon)
    return (values / length, length)


def directions(values):
    values = values.astype(f32)
    return (values * lax.rsqrt(jnp.sum(values * values, axis=-1, keepdims=True) + epsilon)).astype(bf16)


def to_column(row):
    return jnp.broadcast_to(row, (LANES, LANES)).T


def fill_columns(rows, tile_ref):
    for k in range(rows.shape[0]):
        tile_ref[k * LANES : (k + 1) * LANES, :] = to_column(rows[k : k + 1, :])


def lane_totals(tile):
    parts = [
        jnp.sum(tile[k * LANES : (k + 1) * LANES, :].T, axis=0, keepdims=True)
        for k in range(tile.shape[0] // LANES)
    ]
    return jnp.concatenate(parts, axis=0)


def select_body(core_ref, teacher_ref, student_ref, order_ref, units_ref, length_ref, top_ref, bottom_ref):
    images, patches, _ = teacher_ref.shape
    for image in range(images):
        chosen = order_ref[image : image + 1, :MASKED]
        place = lax.broadcasted_iota(jnp.int32, (patches, MASKED), 0)
        onehot = jnp.where(place == chosen, 1.0, 0.0).astype(bf16)

        def pick(ref):
            return lax.dot_general(
                onehot, ref[image], (((0,), (0,)), ((), ())), preferred_element_type=f32
            )

        rows = slice(image * MASKED, (image + 1) * MASKED)
        teacher = unit_rows(pick(teacher_ref))[0]
        student, length_ref[rows, :] = unit_rows(pick(student_ref))
        units_ref[rows, :D] = teacher
        units_ref[rows, D:] = student
        mine = jnp.where(core_ref[0] == 0, teacher, student)
        half = top_ref.shape[0]
        if image * MASKED < half:
            top_ref[rows, :] = mine
        else:
            bottom_ref[image * MASKED - half : (image + 1) * MASKED - half, :] = mine


def select_tokens(core, teacher_patches, student_patches, mask_order):
    tokens = teacher_patches.shape[0] * MASKED
    return pl.pallas_call(
        select_body,
        in_specs=[pl.BlockSpec(memory_space=pltpu.SMEM)]
        + [pl.BlockSpec(memory_space=pltpu.VMEM)] * 3,
        out_specs=[pl.BlockSpec(memory_space=pltpu.VMEM)] * 4,
        out_shape=[
            pltpu.HBM((tokens, 2 * D), f32),
            pltpu.HBM((tokens, 1), f32),
            pltpu.HBM((tokens // 2, D), f32),
            pltpu.HBM((tokens // 2, D), f32),
        ],
        compiler_params=params(8),
        name="select",
    )(core, in_hbm(teacher_patches), in_hbm(student_patches), in_hbm(mask_order))


def lane_rows(row):
    parts = [row[:, j * LANES : (j + 1) * LANES] for j in range(row.shape[1] // LANES)]
    return jnp.concatenate(parts, axis=0)


def chunks(tokens):
    return [slice(c, c + LANES) for c in range(0, tokens, LANES)]


FETCHES = 8
WIDE = 256


def fetch(protos_ref, buffer_ref, sems, i):
    size = buffer_ref.shape[0] // FETCHES
    rows = pl.ds(pl.multiple_of(i * size, size), size)
    return pltpu.make_async_copy(protos_ref.at[rows, :], buffer_ref.at[rows, :], sems.at[i])


def fetch_all(units_ref, column, unit_ref, protos_ref, buffer_ref, sems):
    units = pltpu.make_async_copy(
        units_ref.at[:, pl.ds(column, D)], unit_ref, sems.at[FETCHES]
    )
    units.start()
    for i in range(FETCHES):
        fetch(protos_ref, buffer_ref, sems, i).start()
    units.wait()


def energy_body(
    place_ref, units_ref, *refs
):
    piece_refs, (protos_ref, energy_ref, sums_ref, cast_ref, weights_ref, total_ref) = refs[:12], refs[12:]
    own = units_ref.shape[0]
    tokens = cast_ref.shape[0]

    def rows_of(slot, start, size):
        return pl.ds(pl.multiple_of(place_ref[4 + slot] * own + start, size), size)

    cast_ref[rows_of(0, 0, own), :] = units_ref[...].astype(bf16)
    places = [(slot, start, own // 2) for slot in (1, 3, 2) for start in (0, own // 2)]
    for core in range(2):

        @pl.when(place_ref[3] == core)
        def _(core=core):
            for i, ref in enumerate(piece_refs):
                kind = core if i < len(places) else 1 - core
                rows = rows_of(*places[i % len(places)])
                cast_ref[rows, kind * D : (kind + 1) * D] = ref[...].astype(bf16)

    weights_ref[...] = directions(protos_ref[...])
    total_ref[...] = jnp.zeros_like(total_ref)
    size = 512
    parts = [slice(c, c + size) for c in range(0, weights_ref.shape[0], size)]

    def step(i, carry):
        chunk = cast_ref[pl.ds(pl.multiple_of(i * WIDE, WIDE), WIDE), :][:, :D]
        logits = nt_dot(weights_ref[parts[0], :], chunk)
        for k, part in enumerate(parts):
            following = nt_dot(weights_ref[parts[k + 1], :], chunk) if k + 1 < len(parts) else None
            energy = jnp.exp2(logits * teacher_power)
            total = total_ref[part, :]
            for j in range(WIDE // LANES):
                tile = energy[:, j * LANES : (j + 1) * LANES]
                energy_ref[i * (WIDE // LANES) + j, part, :] = tile.astype(bf16)
                total = total + tile
            total_ref[part, :] = total
            logits = following
        return carry

    lax.fori_loop(0, tokens // WIDE, step, 0)
    totals = lane_totals(total_ref[...])
    for copy in range(sums_ref.shape[0]):
        sums_ref[copy] = totals


def fixed(*shape):
    return pl.BlockSpec(shape, lambda i: (0,) * len(shape))


def left(tokens):
    return pl.BlockSpec((tokens, D), lambda *i: (0, 0))


def right(tokens):
    return pl.BlockSpec((tokens, D), lambda *i: (0, 1))


def energy_of(place, units, pieces, protos, share, copies):
    own = units.shape[0]
    tokens = own * 4
    direct = pl.BlockSpec(memory_space=pltpu.VMEM)
    return pl.pallas_call(
        energy_body,
        grid_spec=pltpu.PrefetchScalarGridSpec(
            num_scalar_prefetch=1,
            grid=(1,),
            in_specs=[pl.BlockSpec(units.shape, lambda i, p: (0, 0))]
            + [direct] * len(pieces)
            + [pl.BlockSpec((share, D), lambda i, p: (p[0], 0))],
            out_specs=[
                direct,
                pl.BlockSpec((copies, share // LANES, LANES), lambda i, p: (0, 0, 0)),
                direct,
            ],
            scratch_shapes=[pltpu.VMEM((share, D), bf16), pltpu.VMEM((share, LANES), f32)],
        ),
        out_shape=[
            pltpu.VMEM((tokens // LANES, share, LANES), bf16),
            jax.ShapeDtypeStruct((copies, share // LANES, LANES), f32),
            pltpu.VMEM((tokens, 2 * D), bf16),
        ],
        compiler_params=params(24),
        cost_estimate=work(4 * tokens * share * D, 8 * 2**20, tokens * share),
        name="energy",
    )(place, in_hbm(units), *pieces, in_hbm(protos))


def student_body(units_ref, protos_ref, sums_ref, unit_ref, cast_ref, total_ref, buffer_ref, sems):
    size = buffer_ref.shape[0] // FETCHES
    fetch_all(units_ref, D, unit_ref, protos_ref, buffer_ref, sems)
    cast_ref[...] = unit_ref[...].astype(bf16)
    total_ref[...] = jnp.zeros_like(total_ref)

    def step(i, carry):
        fetch(protos_ref, buffer_ref, sems, i).wait()
        total = total_ref[...]

        def logits_of(part):
            rows = pl.ds(pl.multiple_of(i * size + part * WIDE, WIDE), WIDE)
            return nt_dot(cast_ref[...], directions(buffer_ref[rows, :]))

        parts = size // WIDE
        logits = logits_of(0)
        for part in range(parts):
            following = logits_of(part + 1) if part + 1 < parts else None
            values = jnp.exp2(logits * student_power)
            logits = following
            for j in range(WIDE // LANES):
                total = total + values[:, j * LANES : (j + 1) * LANES]
        total_ref[...] = total
        return carry

    lax.fori_loop(0, FETCHES, step, 0)
    sums_ref[...] = lane_totals(total_ref[...])


def student_sums(units, protos):
    tokens, count = units.shape[0], protos.shape[0]
    return pl.pallas_call(
        student_body,
        in_specs=[pl.BlockSpec(memory_space=pl.ANY)] * 2,
        out_specs=pl.BlockSpec(memory_space=pltpu.VMEM),
        out_shape=jax.ShapeDtypeStruct((tokens // LANES, LANES), f32),
        scratch_shapes=[
            pltpu.VMEM((tokens, D), f32),
            pltpu.VMEM((tokens, D), bf16),
            pltpu.VMEM((tokens, LANES), f32),
            pltpu.VMEM((count, D), bf16),
            pltpu.SemaphoreType.DMA((FETCHES + 1,)),
        ],
        compiler_params=params(16),
        cost_estimate=work(4 * tokens * count * D, 8 * 2**20, tokens * count),
        name="student",
    )(in_hbm(units), in_hbm(protos))


def right(tokens):
    return pl.BlockSpec((tokens, D), lambda *i: (0, 1))


def row_body(energy_ref, pieces_ref, *refs):
    norm_refs, (scale_ref, sums_ref, tile_ref) = refs[:-3], refs[-3:]
    scale_ref[...] = 1.0 / jnp.sum(pieces_ref[...], axis=0)
    fill_columns(scale_ref[...], tile_ref)
    tiles, protos, _ = energy_ref.shape
    size = 512
    totals = []
    for j in range(tiles):
        total = jnp.zeros((1, LANES), f32)
        for start in range(0, protos, size):
            part = slice(start, start + size)
            energy = energy_ref[j, part, :].astype(f32)
            total = total + jnp.sum(energy * tile_ref[part, :], axis=0, keepdims=True)
        totals.append(total)
    for ref in norm_refs:
        totals += [ref[...], jnp.zeros_like(ref)]
    totals = jnp.concatenate(totals, axis=0)
    for copy in range(sums_ref.shape[0]):
        sums_ref[copy] = totals


def row_sums(energy, pieces, copies, norm_part=()):
    tiles, protos, _ = energy.shape
    whole = pl.BlockSpec(memory_space=pltpu.VMEM)
    rows = tiles + 2 * sum(part.shape[0] for part in norm_part)
    return pl.pallas_call(
        row_body,
        in_specs=[whole] * (2 + len(norm_part)),
        out_specs=[whole] * 2,
        out_shape=[
            jax.ShapeDtypeStruct((protos // LANES, LANES), f32),
            jax.ShapeDtypeStruct((copies, rows, LANES), f32),
        ],
        scratch_shapes=[pltpu.VMEM((protos, LANES), f32)],
        compiler_params=params(12),
        cost_estimate=work(2 * energy.size, 0),
        name="row_sums",
    )(energy, pieces, *norm_part)


def column_body(energy_ref, pieces_ref, sums_ref, scale_ref):
    tiles, protos, _ = energy_ref.shape
    scale_ref[...] = 1.0 / jnp.sum(pieces_ref[...], axis=0)

    def step(k, carry):
        rows = pl.ds(pl.multiple_of(k * LANES, LANES), LANES)
        total = jnp.zeros((LANES, LANES), f32)
        for j in range(tiles):
            total = total + energy_ref[j, rows, :].astype(f32) * scale_ref[j : j + 1, :]
        sums_ref[0, pl.ds(k, 1), :] = lane_totals(total)
        return carry

    lax.fori_loop(0, protos // LANES, step, 0, unroll=4)
    for copy in range(1, sums_ref.shape[0]):
        sums_ref[copy] = sums_ref[0]


def column_sums(energy, pieces, copies):
    tiles, protos, _ = energy.shape
    whole = pl.BlockSpec(memory_space=pltpu.VMEM)
    return pl.pallas_call(
        column_body,
        in_specs=[whole] * 2,
        out_specs=whole,
        out_shape=jax.ShapeDtypeStruct((copies, protos // LANES, LANES), f32),
        scratch_shapes=[pltpu.VMEM((tiles, LANES), f32)],
        compiler_params=params(12),
        cost_estimate=work(2 * energy.size, 0),
        name="column_sums",
    )(energy, pieces)


LEFT_PLACE = [4, 5, 6, 7, 3, 2, 1, 0]
RIGHT_PLACE = [4, 0, 1, 2, 3, 7, 6, 5]


def collect(send, keep, offset):
    n = lax.axis_size("z")
    way = [1 if (z + offset) % 2 else -1 for z in range(n)]
    got = lax.ppermute(send, "z", [(z, (z - way[z]) % n) for z in range(n)])
    return keep[0] + got[0], keep[1] + got[1], keep[2:] + got[2:]


def pass_on(sums, offset, after):
    n = lax.axis_size("z")
    way = [1 if (z + offset) % 2 else -1 for z in range(n)]
    own, following, far = sums
    got = lax.ppermute(far, "z", [(z, (z + 2 * way[z]) % n) for z in range(n)])
    own, following, _ = lax.optimization_barrier((own, following, after))
    return own + got[0], following + got[1]


def deliver(sums, offset):
    n = lax.axis_size("z")
    way = [1 if (z + offset) % 2 else -1 for z in range(n)]
    own, following = sums
    return [own, lax.ppermute(following, "z", [(z, (z + way[z]) % n) for z in range(n)])]


def gradient_body(
    table_ref,
    units_ref,
    energy_ref,
    pieces_ref,
    sw_first_ref,
    sw_second_ref,
    scale_ref,
    send_left_ref,
    send_right_ref,
    keep_left_ref,
    keep_right_ref,
    feature_send_ref,
    feature_keep_ref,
    r_ref,
    n_ref,
    total_ref,
    feature_ref,
    stage_ref,
    sems,
):
    step = pl.program_id(0)
    tiles = energy_ref.shape[0]
    groups = pieces_ref.shape[0]
    own = tiles // groups

    @pl.when(step == 0)
    def _():
        scale = (1.0 / student_temp) / jnp.sum(pieces_ref[:, :, :tiles, :], axis=(0, 1))
        for k in range(tiles):
            r_ref[:, k * LANES : (k + 1) * LANES] = scale[k : k + 1, :]
        for group in range(groups):
            total = jnp.sum(pieces_ref[group, :, tiles : tiles + own, :], axis=0)
            inverse = (1.0 / student_temp) / total
            for k in range(own):
                lanes = slice((group * own + k) * LANES, (group * own + k + 1) * LANES)
                n_ref[:, lanes] = inverse[k : k + 1, :]
        feature_ref[...] = jnp.zeros_like(feature_ref)

    both = lambda first, second: jnp.concatenate([first, second], axis=0)
    block = sw_first_ref.shape[0]
    sw = both(directions(sw_first_ref[...]), directions(sw_second_ref[...]))
    local = [table_ref[3, 2 * step], table_ref[3, 2 * step + 1]]
    here = [pl.ds(pl.multiple_of(place * block, block), block) for place in local]
    columns = []
    for place in local:
        for k in range(block // LANES):
            row = scale_ref[pl.ds(place * (block // LANES) + k, 1), :]
            columns.append(to_column(row))
    col_scale = jnp.concatenate(columns, axis=0)

    def logits_of(part):
        return nt_dot(sw, units_ref[part, D:])

    parts = [slice(c, c + WIDE) for c in range(0, units_ref.shape[0], WIDE)]

    logits = logits_of(parts[0])
    for i, part in enumerate(parts):
        following = logits_of(parts[i + 1]) if i + 1 < len(parts) else None
        grads = []
        for j in range(WIDE // LANES):
            tile = i * (WIDE // LANES) + j
            lanes = slice(tile * LANES, (tile + 1) * LANES)
            energy = both(energy_ref[tile, here[0], :], energy_ref[tile, here[1], :]).astype(f32)
            probs = jnp.exp2(logits[:, j * LANES : (j + 1) * LANES] * student_power) * n_ref[:, lanes]
            grads.append((probs - energy * r_ref[:, lanes] * col_scale).astype(bf16))
        logit_grad = jnp.concatenate(grads, axis=1)
        added = jnp.dot(logit_grad, units_ref[part, D:], preferred_element_type=f32)
        total_ref[...] = added if i == 0 else total_ref[...] + added
        feature_ref[part, :] += lax.dot_general(
            logit_grad, sw, (((0,), (0,)), ((), ())), preferred_element_type=f32
        )
        logits = following

    def copies(which, at):
        found = []
        for half, (sent_ref, kept_ref) in enumerate(
            ((send_left_ref, keep_left_ref), (send_right_ref, keep_right_ref))
        ):
            block_at = 2 * at + which
            place = table_ref[1 + half, block_at]
            source, sem = stage_ref.at[half, block_at], sems.at[half, block_at]
            sent = pltpu.make_async_copy(source, sent_ref.at[jnp.minimum(place, 3)], sem)
            kept = pltpu.make_async_copy(source, kept_ref.at[jnp.maximum(place - 4, 0)], sem)
            found += [(place < 4, sent), (place >= 4, kept)]
        return found

    for which in range(2):
        rows_here = slice(which * block, (which + 1) * block)
        for half in range(2):
            columns_here = slice(half * (D // 2), (half + 1) * (D // 2))
            stage_ref[half, 2 * step + which] = total_ref[rows_here, columns_here]
        for wanted, copy in copies(which, step):
            pl.when(wanted)(copy.start)

    @pl.when(step == pl.num_programs(0) - 1)
    def _():
        size = feature_send_ref.shape[1]
        for core in range(2):

            @pl.when(table_ref[4, 0] == core)
            def _(core=core):
                for at in range(feature_ref.shape[0] // size):
                    out_ref = feature_keep_ref if at % 2 == core else feature_send_ref
                    out_ref[at // 2] = feature_ref[at * size : (at + 1) * size, :]

        for at in range(stage_ref.shape[1] // 2):
            for which in range(2):
                for wanted, copy in copies(which, at):
                    pl.when(wanted)(copy.wait)


def block_table(y, z, core):
    blocks = len(LEFT_PLACE)
    way = jnp.where(z % 2 == 1, 1, -1)
    local = (z + way * jnp.arange(blocks) + blocks) % blocks
    cores = jnp.full((blocks,), core)
    table = [y * blocks + local, jnp.array(LEFT_PLACE), jnp.array(RIGHT_PLACE), local, cores]
    return jnp.stack(table).astype(jnp.int32)


def gradients(table, units_all, energy, pieces, student_protos, scale, shares):
    tiles, share, _ = energy.shape
    tokens = units_all.shape[0]
    block = 256
    blocks = share // block
    whole = lambda *shape: pl.BlockSpec(shape, lambda i, p: (0,) * len(shape))
    first = pl.BlockSpec((block, D), lambda i, p: (p[0, 2 * i], 0))
    second = pl.BlockSpec((block, D), lambda i, p: (p[0, 2 * i + 1], 0))
    direct = pl.BlockSpec(memory_space=pltpu.VMEM)
    half = pltpu.HBM((blocks // 2, block, D // 2), f32)
    return pl.pallas_call(
        gradient_body,
        grid_spec=pltpu.PrefetchScalarGridSpec(
            num_scalar_prefetch=1,
            grid=(blocks // 2,),
            in_specs=[
                direct,
                direct,
                whole(*pieces.shape),
                first,
                second,
                whole(*scale.shape),
            ],
            out_specs=[pl.BlockSpec(memory_space=pl.ANY)] * 4 + [direct] * 2,
            scratch_shapes=[
                pltpu.VMEM((1, tokens), f32),
                pltpu.VMEM((1, tokens), f32),
                pltpu.VMEM((2 * block, D), f32),
                pltpu.VMEM((tokens, D), f32),
                pltpu.VMEM((2, blocks, block, D // 2), f32),
                pltpu.SemaphoreType.DMA((2, blocks)),
            ],
        ),
        out_shape=[half] * 4 + [pltpu.VMEM((shares // 2, tokens // shares, D), f32)] * 2,
        compiler_params=params(24),
        cost_estimate=work(8 * tokens * share * D, 8 * 2**20, tokens * share),
        name="gradients",
    )(
        table,
        units_all,
        energy,
        pieces,
        in_hbm(student_protos),
        in_hbm(student_protos),
        scale,
    )


def project(total, unit, length):
    return (total - unit * jnp.sum(unit * total, axis=-1, keepdims=True)) / length


def student_end_body(place_ref, pieces_ref, unit_ref, length_ref, out_ref):
    result = project(jnp.sum(pieces_ref[...], axis=0), unit_ref[...], length_ref[...])
    for copy in range(out_ref.shape[0]):
        out_ref[copy] = result


def student_end(place, pieces, units, length, copies):
    _, rows, _ = pieces.shape
    return pl.pallas_call(
        student_end_body,
        grid_spec=pltpu.PrefetchScalarGridSpec(
            num_scalar_prefetch=1,
            grid=(1,),
            in_specs=[
                pl.BlockSpec(memory_space=pltpu.VMEM),
                pl.BlockSpec((rows, D), lambda i, p: (p[2], 1)),
                pl.BlockSpec((rows, 1), lambda i, p: (p[2], 0)),
            ],
            out_specs=pl.BlockSpec((copies, rows, D), lambda i, p: (0, 0, 0)),
        ),
        out_shape=jax.ShapeDtypeStruct((copies, rows, D), f32),
        compiler_params=params(8),
        name="student_end",
    )(place, pieces, in_hbm(units), in_hbm(length))


def proto_end_body(place_ref, *refs):
    piece_refs, (protos_ref, out_ref) = refs[:-2], refs[-2:]
    unit, length = unit_rows(protos_ref[...].astype(f32))
    half = len(piece_refs) // 2
    sums = []
    for group in (piece_refs[:half], piece_refs[half:]):
        total = group[0][...]
        for ref in group[1:]:
            total = total + ref[...]
        sums.append(total)
    out_ref[...] = project(jnp.concatenate(sums, axis=1), unit, length)


def proto_end(place, pieces, protos):
    rows, width = pieces[0].shape
    return pl.pallas_call(
        proto_end_body,
        grid_spec=pltpu.PrefetchScalarGridSpec(
            num_scalar_prefetch=1,
            grid=(1,),
            in_specs=[pl.BlockSpec(memory_space=pltpu.VMEM)] * len(pieces)
            + [pl.BlockSpec((rows, D), lambda i, p: (p[1], 0))],
            out_specs=pl.BlockSpec((rows, D), lambda i, p: (0, 0)),
        ),
        out_shape=jax.ShapeDtypeStruct((rows, D), f32),
        compiler_params=params(8),
        name="proto_end",
    )(place, *pieces, in_hbm(protos))


def on_device(teacher_patches, student_patches, mask_order, teacher_protos, student_protos):
    y_size, z_size = lax.axis_size("y"), lax.axis_size("z")
    proto_size = lax.axis_size("x") * lax.axis_size("core")
    y, z = lax.axis_index("y"), lax.axis_index("z")
    others = [(y - step + y_size) % y_size for step in range(y_size)]
    core = lax.axis_index("core")
    place = [y, y * z_size + z, lax.axis_index(PROTOS), core] + others
    place = jnp.stack(place).astype(jnp.int32)
    table = block_table(y, z, core)
    share = teacher_protos.shape[0] // y_size

    units, student_length, top, bottom = select_tokens(
        core.astype(jnp.int32)[None], teacher_patches, student_patches, mask_order
    )
    from_y = lambda value, step: lax.ppermute(
        value, "y", [(i, (i + step) % y_size) for i in range(y_size)]
    )
    from_core = lambda value: lax.ppermute(value, "core", [(0, 1), (1, 0)])
    first_top, third_bottom = from_y(top, 1), from_y(bottom, 3)
    first_bottom, third_top = from_y(bottom, 1), from_y(top, 3)
    units, first_top, third_bottom = lax.optimization_barrier((units, first_top, third_bottom))
    second_top, second_bottom = from_y(first_top, 1), from_y(third_bottom, 3)
    norm_part = student_sums(units, student_protos)
    got = [first_top, first_bottom, third_top, third_bottom, second_top, second_bottom]
    norm_part, got, place, table = lax.optimization_barrier((norm_part, got, place, table))
    got = got + [from_core(piece) for piece in got]

    rows = ("y",) + PROTOS
    peers = y_size * proto_size
    energy, sums, units_all = energy_of(place, units, got, teacher_protos, share, z_size)
    for sweep in range(ITERS):
        if sweep > 0:
            sums = column_sums(energy, pieces, z_size)
        norms = (norm_part,) if sweep == ITERS - 1 else ()
        col_scale, row_part = row_sums(energy, spread(sums, "z"), peers, norms)
        pieces = spread(row_part, rows)
    pieces = pieces.reshape((y_size, proto_size) + pieces.shape[1:])

    send_left, send_right, keep_left, keep_right, feature_send, feature_keep = gradients(
        table, units_all, energy, pieces, student_protos, col_scale, peers
    )
    feature_part = feature_keep + from_core(feature_send)
    feature_part, keep_left, keep_right = lax.optimization_barrier(
        (feature_part, keep_left, keep_right)
    )
    left, right_half = collect(send_left, keep_left, 0), collect(send_right, keep_right, 1)
    feature_pieces = spread(feature_part, ("y", "x"))
    feature_pieces, _, _ = lax.optimization_barrier((feature_pieces, left, right_half))
    result = student_end(place, feature_pieces, units, student_length, proto_size)
    left, right_half = pass_on(left, 0, result), pass_on(right_half, 1, result)
    left, right_half = deliver(left, 0), deliver(right_half, 1)
    result = spread(result, PROTOS)
    grad_protos = proto_end(place, left + right_half, student_protos)
    return (result.reshape(-1, MASKED, D), grad_protos)


def solution(mesh):
    fine = Mesh(mesh.devices.reshape(4, 8, 4, 2), ("y", "z", "x", "core"))
    return jax.shard_map(
        on_device,
        mesh=fine,
        in_specs=(
            P(ROWS, None, None),
            P(ROWS, None, None),
            P(ROWS, None),
            P(PROTOS, None),
            P(PROTOS, None),
        ),
        out_specs=(P(ROWS, None, None), P(PROTOS + ROWS, None)),
        check_vma=False,
    )
```

```python
import math

import jax
import jax.numpy as jnp
from jax import lax
from jax.experimental import pallas as pl
from jax.experimental.pallas import tpu as pltpu
from jax.sharding import Mesh, PartitionSpec as P

D = 256
MASKED = 128
ITERS = 3
LANES = 128

teacher_temp = 0.07
student_temp = 0.1
epsilon = 1e-06

teacher_power = math.log2(math.e) / teacher_temp
student_power = math.log2(math.e) / student_temp

ROWS = ("y", "z")
PROTOS = ("x", "core")

f32 = jnp.float32
bf16 = jnp.bfloat16


def params(mib):
    return pltpu.CompilerParams(vmem_limit_bytes=mib * 2**20)


def spread(value, axes):
    return lax.all_to_all(value, axes, 0, 0, tiled=True)


def work(flops, moved, powers=0):
    return pl.CostEstimate(flops=int(flops), bytes_accessed=int(moved), transcendentals=int(powers))


def in_hbm(value):
    return pltpu.with_memory_space_constraint(value, pltpu.HBM)


def nt_dot(a, b):
    return lax.dot_general(a, b, (((1,), (1,)), ((), ())), preferred_element_type=f32)


def unit_rows(values):
    length = jnp.sqrt(jnp.sum(values * values, axis=-1, keepdims=True) + epsilon)
    return (values / length, length)


def directions(values):
    values = values.astype(f32)
    return (values * lax.rsqrt(jnp.sum(values * values, axis=-1, keepdims=True) + epsilon)).astype(bf16)


def to_column(row):
    return jnp.broadcast_to(row, (LANES, LANES)).T


def fill_columns(rows, tile_ref):
    for k in range(rows.shape[0]):
        tile_ref[k * LANES : (k + 1) * LANES, :] = to_column(rows[k : k + 1, :])


def lane_totals(tile):
    parts = [
        jnp.sum(tile[k * LANES : (k + 1) * LANES, :].T, axis=0, keepdims=True)
        for k in range(tile.shape[0] // LANES)
    ]
    return jnp.concatenate(parts, axis=0)


def select_body(core_ref, teacher_ref, student_ref, order_ref, units_ref, length_ref, top_ref, bottom_ref):
    images, patches, _ = teacher_ref.shape
    for image in range(images):
        chosen = order_ref[image : image + 1, :MASKED]
        place = lax.broadcasted_iota(jnp.int32, (patches, MASKED), 0)
        onehot = jnp.where(place == chosen, 1.0, 0.0).astype(bf16)

        def pick(ref):
            return lax.dot_general(
                onehot, ref[image], (((0,), (0,)), ((), ())), preferred_element_type=f32
            )

        rows = slice(image * MASKED, (image + 1) * MASKED)
        teacher = unit_rows(pick(teacher_ref))[0]
        student, length_ref[rows, :] = unit_rows(pick(student_ref))
        units_ref[rows, :D] = teacher
        units_ref[rows, D:] = student
        mine = jnp.where(core_ref[0] == 0, teacher, student)
        half = top_ref.shape[0]
        if image * MASKED < half:
            top_ref[rows, :] = mine
        else:
            bottom_ref[image * MASKED - half : (image + 1) * MASKED - half, :] = mine


def select_tokens(core, teacher_patches, student_patches, mask_order):
    tokens = teacher_patches.shape[0] * MASKED
    return pl.pallas_call(
        select_body,
        in_specs=[pl.BlockSpec(memory_space=pltpu.SMEM)]
        + [pl.BlockSpec(memory_space=pltpu.VMEM)] * 3,
        out_specs=[pl.BlockSpec(memory_space=pltpu.VMEM)] * 4,
        out_shape=[
            pltpu.HBM((tokens, 2 * D), f32),
            pltpu.HBM((tokens, 1), f32),
            pltpu.HBM((tokens // 2, D), f32),
            pltpu.HBM((tokens // 2, D), f32),
        ],
        compiler_params=params(8),
        name="select",
    )(core, in_hbm(teacher_patches), in_hbm(student_patches), in_hbm(mask_order))


def lane_rows(row):
    parts = [row[:, j * LANES : (j + 1) * LANES] for j in range(row.shape[1] // LANES)]
    return jnp.concatenate(parts, axis=0)


def chunks(tokens):
    return [slice(c, c + LANES) for c in range(0, tokens, LANES)]


FETCHES = 8
WIDE = 256


def fetch(protos_ref, buffer_ref, sems, i):
    size = buffer_ref.shape[0] // FETCHES
    rows = pl.ds(pl.multiple_of(i * size, size), size)
    return pltpu.make_async_copy(protos_ref.at[rows, :], buffer_ref.at[rows, :], sems.at[i])


def fetch_all(units_ref, column, unit_ref, protos_ref, buffer_ref, sems):
    units = pltpu.make_async_copy(
        units_ref.at[:, pl.ds(column, D)], unit_ref, sems.at[FETCHES]
    )
    units.start()
    for i in range(FETCHES):
        fetch(protos_ref, buffer_ref, sems, i).start()
    units.wait()


def energy_body(
    place_ref, units_ref, *refs
):
    piece_refs, (protos_ref, energy_ref, sums_ref, cast_ref, weights_ref, total_ref) = refs[:12], refs[12:]
    own = units_ref.shape[0]
    tokens = cast_ref.shape[0]

    def rows_of(slot, start, size):
        return pl.ds(pl.multiple_of(place_ref[4 + slot] * own + start, size), size)

    cast_ref[rows_of(0, 0, own), :] = units_ref[...].astype(bf16)
    places = [(slot, start, own // 2) for slot in (1, 3, 2) for start in (0, own // 2)]
    for core in range(2):

        @pl.when(place_ref[3] == core)
        def _(core=core):
            for i, ref in enumerate(piece_refs):
                kind = core if i < len(places) else 1 - core
                rows = rows_of(*places[i % len(places)])
                cast_ref[rows, kind * D : (kind + 1) * D] = ref[...].astype(bf16)

    weights_ref[...] = directions(protos_ref[...])
    total_ref[...] = jnp.zeros_like(total_ref)
    size = 512
    parts = [slice(c, c + size) for c in range(0, weights_ref.shape[0], size)]

    def step(i, carry):
        chunk = cast_ref[pl.ds(pl.multiple_of(i * WIDE, WIDE), WIDE), :][:, :D]
        logits = nt_dot(weights_ref[parts[0], :], chunk)
        for k, part in enumerate(parts):
            following = nt_dot(weights_ref[parts[k + 1], :], chunk) if k + 1 < len(parts) else None
            energy = jnp.exp2(logits * teacher_power)
            total = total_ref[part, :]
            for j in range(WIDE // LANES):
                tile = energy[:, j * LANES : (j + 1) * LANES]
                energy_ref[i * (WIDE // LANES) + j, part, :] = tile.astype(bf16)
                total = total + tile
            total_ref[part, :] = total
            logits = following
        return carry

    lax.fori_loop(0, tokens // WIDE, step, 0)
    totals = lane_totals(total_ref[...])
    for copy in range(sums_ref.shape[0]):
        sums_ref[copy] = totals


def fixed(*shape):
    return pl.BlockSpec(shape, lambda i: (0,) * len(shape))


def left(tokens):
    return pl.BlockSpec((tokens, D), lambda *i: (0, 0))


def right(tokens):
    return pl.BlockSpec((tokens, D), lambda *i: (0, 1))


def energy_of(place, units, pieces, protos, share, copies):
    own = units.shape[0]
    tokens = own * 4
    direct = pl.BlockSpec(memory_space=pltpu.VMEM)
    return pl.pallas_call(
        energy_body,
        grid_spec=pltpu.PrefetchScalarGridSpec(
            num_scalar_prefetch=1,
            grid=(1,),
            in_specs=[pl.BlockSpec(units.shape, lambda i, p: (0, 0))]
            + [direct] * len(pieces)
            + [pl.BlockSpec((share, D), lambda i, p: (p[0], 0))],
            out_specs=[
                direct,
                pl.BlockSpec((copies, share // LANES, LANES), lambda i, p: (0, 0, 0)),
                direct,
            ],
            scratch_shapes=[pltpu.VMEM((share, D), bf16), pltpu.VMEM((share, LANES), f32)],
        ),
        out_shape=[
            pltpu.VMEM((tokens // LANES, share, LANES), bf16),
            jax.ShapeDtypeStruct((copies, share // LANES, LANES), f32),
            pltpu.VMEM((tokens, 2 * D), bf16),
        ],
        compiler_params=params(24),
        cost_estimate=work(4 * tokens * share * D, 8 * 2**20, tokens * share),
        name="energy",
    )(place, in_hbm(units), *pieces, in_hbm(protos))


def student_body(units_ref, protos_ref, sums_ref, unit_ref, cast_ref, total_ref, buffer_ref, sems):
    size = buffer_ref.shape[0] // FETCHES
    fetch_all(units_ref, D, unit_ref, protos_ref, buffer_ref, sems)
    cast_ref[...] = unit_ref[...].astype(bf16)
    total_ref[...] = jnp.zeros_like(total_ref)

    def step(i, carry):
        fetch(protos_ref, buffer_ref, sems, i).wait()
        total = total_ref[...]

        def logits_of(part):
            rows = pl.ds(pl.multiple_of(i * size + part * WIDE, WIDE), WIDE)
            return nt_dot(cast_ref[...], directions(buffer_ref[rows, :]))

        parts = size // WIDE
        logits = logits_of(0)
        for part in range(parts):
            following = logits_of(part + 1) if part + 1 < parts else None
            values = jnp.exp2(logits * student_power)
            logits = following
            for j in range(WIDE // LANES):
                total = total + values[:, j * LANES : (j + 1) * LANES]
        total_ref[...] = total
        return carry

    lax.fori_loop(0, FETCHES, step, 0)
    sums_ref[...] = lane_totals(total_ref[...])


def student_sums(units, protos):
    tokens, count = units.shape[0], protos.shape[0]
    return pl.pallas_call(
        student_body,
        in_specs=[pl.BlockSpec(memory_space=pl.ANY)] * 2,
        out_specs=pl.BlockSpec(memory_space=pltpu.VMEM),
        out_shape=jax.ShapeDtypeStruct((tokens // LANES, LANES), f32),
        scratch_shapes=[
            pltpu.VMEM((tokens, D), f32),
            pltpu.VMEM((tokens, D), bf16),
            pltpu.VMEM((tokens, LANES), f32),
            pltpu.VMEM((count, D), bf16),
            pltpu.SemaphoreType.DMA((FETCHES + 1,)),
        ],
        compiler_params=params(16),
        cost_estimate=work(4 * tokens * count * D, 8 * 2**20, tokens * count),
        name="student",
    )(in_hbm(units), in_hbm(protos))


def right(tokens):
    return pl.BlockSpec((tokens, D), lambda *i: (0, 1))


def row_body(energy_ref, pieces_ref, *refs):
    norm_refs, (scale_ref, sums_ref, tile_ref) = refs[:-3], refs[-3:]
    scale_ref[...] = 1.0 / jnp.sum(pieces_ref[...], axis=0)
    fill_columns(scale_ref[...], tile_ref)
    tiles, protos, _ = energy_ref.shape
    size = 512
    totals = []
    for j in range(tiles):
        total = jnp.zeros((1, LANES), f32)
        for start in range(0, protos, size):
            part = slice(start, start + size)
            energy = energy_ref[j, part, :].astype(f32)
            total = total + jnp.sum(energy * tile_ref[part, :], axis=0, keepdims=True)
        totals.append(total)
    for ref in norm_refs:
        totals += [ref[...], jnp.zeros_like(ref)]
    totals = jnp.concatenate(totals, axis=0)
    for copy in range(sums_ref.shape[0]):
        sums_ref[copy] = totals


def row_sums(energy, pieces, copies, norm_part=()):
    tiles, protos, _ = energy.shape
    whole = pl.BlockSpec(memory_space=pltpu.VMEM)
    rows = tiles + 2 * sum(part.shape[0] for part in norm_part)
    return pl.pallas_call(
        row_body,
        in_specs=[whole] * (2 + len(norm_part)),
        out_specs=[whole] * 2,
        out_shape=[
            jax.ShapeDtypeStruct((protos // LANES, LANES), f32),
            jax.ShapeDtypeStruct((copies, rows, LANES), f32),
        ],
        scratch_shapes=[pltpu.VMEM((protos, LANES), f32)],
        compiler_params=params(12),
        cost_estimate=work(2 * energy.size, 0),
        name="row_sums",
    )(energy, pieces, *norm_part)


def column_body(energy_ref, pieces_ref, sums_ref, scale_ref):
    tiles, protos, _ = energy_ref.shape
    scale_ref[...] = 1.0 / jnp.sum(pieces_ref[...], axis=0)

    def step(k, carry):
        rows = pl.ds(pl.multiple_of(k * LANES, LANES), LANES)
        total = jnp.zeros((LANES, LANES), f32)
        for j in range(tiles):
            total = total + energy_ref[j, rows, :].astype(f32) * scale_ref[j : j + 1, :]
        sums_ref[0, pl.ds(k, 1), :] = lane_totals(total)
        return carry

    lax.fori_loop(0, protos // LANES, step, 0, unroll=4)
    for copy in range(1, sums_ref.shape[0]):
        sums_ref[copy] = sums_ref[0]


def column_sums(energy, pieces, copies):
    tiles, protos, _ = energy.shape
    whole = pl.BlockSpec(memory_space=pltpu.VMEM)
    return pl.pallas_call(
        column_body,
        in_specs=[whole] * 2,
        out_specs=whole,
        out_shape=jax.ShapeDtypeStruct((copies, protos // LANES, LANES), f32),
        scratch_shapes=[pltpu.VMEM((tiles, LANES), f32)],
        compiler_params=params(12),
        cost_estimate=work(2 * energy.size, 0),
        name="column_sums",
    )(energy, pieces)


LEFT_PLACE = [4, 5, 6, 7, 3, 2, 1, 0]
RIGHT_PLACE = [4, 0, 1, 2, 3, 7, 6, 5]


def collect(send, keep, offset):
    n = lax.axis_size("z")
    way = [1 if (z + offset) % 2 else -1 for z in range(n)]
    got = lax.ppermute(send, "z", [(z, (z - way[z]) % n) for z in range(n)])
    return keep[0] + got[0], keep[1] + got[1], keep[2:] + got[2:]


def pass_on(sums, offset, after):
    n = lax.axis_size("z")
    way = [1 if (z + offset) % 2 else -1 for z in range(n)]
    own, following, far = sums
    got = lax.ppermute(far, "z", [(z, (z + 2 * way[z]) % n) for z in range(n)])
    following, _ = lax.optimization_barrier((following, after))
    return [own, got], following + got[1]


def deliver(sums, offset):
    n = lax.axis_size("z")
    way = [1 if (z + offset) % 2 else -1 for z in range(n)]
    own, following = sums
    return own + [lax.ppermute(following, "z", [(z, (z + way[z]) % n) for z in range(n)])]


def gradient_body(
    table_ref,
    units_ref,
    energy_ref,
    pieces_ref,
    sw_first_ref,
    sw_second_ref,
    scale_ref,
    send_left_ref,
    send_right_ref,
    keep_left_ref,
    keep_right_ref,
    feature_send_ref,
    feature_keep_ref,
    r_ref,
    n_ref,
    total_ref,
    feature_ref,
    stage_ref,
    sems,
):
    step = pl.program_id(0)
    tiles = energy_ref.shape[0]
    groups = pieces_ref.shape[0]
    own = tiles // groups

    @pl.when(step == 0)
    def _():
        scale = (1.0 / student_temp) / jnp.sum(pieces_ref[:, :, :tiles, :], axis=(0, 1))
        for k in range(tiles):
            r_ref[:, k * LANES : (k + 1) * LANES] = scale[k : k + 1, :]
        for group in range(groups):
            total = jnp.sum(pieces_ref[group, :, tiles : tiles + own, :], axis=0)
            inverse = (1.0 / student_temp) / total
            for k in range(own):
                lanes = slice((group * own + k) * LANES, (group * own + k + 1) * LANES)
                n_ref[:, lanes] = inverse[k : k + 1, :]
        feature_ref[...] = jnp.zeros_like(feature_ref)

    both = lambda first, second: jnp.concatenate([first, second], axis=0)
    block = sw_first_ref.shape[0]
    sw = both(directions(sw_first_ref[...]), directions(sw_second_ref[...]))
    local = [table_ref[3, 2 * step], table_ref[3, 2 * step + 1]]
    here = [pl.ds(pl.multiple_of(place * block, block), block) for place in local]
    columns = []
    for place in local:
        for k in range(block // LANES):
            row = scale_ref[pl.ds(place * (block // LANES) + k, 1), :]
            columns.append(to_column(row))
    col_scale = jnp.concatenate(columns, axis=0)

    def logits_of(part):
        return nt_dot(sw, units_ref[part, D:])

    parts = [slice(c, c + WIDE) for c in range(0, units_ref.shape[0], WIDE)]

    logits = logits_of(parts[0])
    for i, part in enumerate(parts):
        following = logits_of(parts[i + 1]) if i + 1 < len(parts) else None
        grads = []
        for j in range(WIDE // LANES):
            tile = i * (WIDE // LANES) + j
            lanes = slice(tile * LANES, (tile + 1) * LANES)
            energy = both(energy_ref[tile, here[0], :], energy_ref[tile, here[1], :]).astype(f32)
            probs = jnp.exp2(logits[:, j * LANES : (j + 1) * LANES] * student_power) * n_ref[:, lanes]
            grads.append((probs - energy * r_ref[:, lanes] * col_scale).astype(bf16))
        logit_grad = jnp.concatenate(grads, axis=1)
        added = jnp.dot(logit_grad, units_ref[part, D:], preferred_element_type=f32)
        total_ref[...] = added if i == 0 else total_ref[...] + added
        feature_ref[part, :] += lax.dot_general(
            logit_grad, sw, (((0,), (0,)), ((), ())), preferred_element_type=f32
        )
        logits = following

    def copies(which, at):
        found = []
        for half, (sent_ref, kept_ref) in enumerate(
            ((send_left_ref, keep_left_ref), (send_right_ref, keep_right_ref))
        ):
            block_at = 2 * at + which
            place = table_ref[1 + half, block_at]
            source, sem = stage_ref.at[half, block_at], sems.at[half, block_at]
            sent = pltpu.make_async_copy(source, sent_ref.at[jnp.minimum(place, 3)], sem)
            kept = pltpu.make_async_copy(source, kept_ref.at[jnp.maximum(place - 4, 0)], sem)
            found += [(place < 4, sent), (place >= 4, kept)]
        return found

    for which in range(2):
        rows_here = slice(which * block, (which + 1) * block)
        for half in range(2):
            columns_here = slice(half * (D // 2), (half + 1) * (D // 2))
            stage_ref[half, 2 * step + which] = total_ref[rows_here, columns_here]
        for wanted, copy in copies(which, step):
            pl.when(wanted)(copy.start)

    @pl.when(step == pl.num_programs(0) - 1)
    def _():
        size = feature_send_ref.shape[1]
        for core in range(2):

            @pl.when(table_ref[4, 0] == core)
            def _(core=core):
                for at in range(feature_ref.shape[0] // size):
                    out_ref = feature_keep_ref if at % 2 == core else feature_send_ref
                    out_ref[at // 2] = feature_ref[at * size : (at + 1) * size, :]

        for at in range(stage_ref.shape[1] // 2):
            for which in range(2):
                for wanted, copy in copies(which, at):
                    pl.when(wanted)(copy.wait)


def block_table(y, z, core):
    blocks = len(LEFT_PLACE)
    way = jnp.where(z % 2 == 1, 1, -1)
    local = (z + way * jnp.arange(blocks) + blocks) % blocks
    cores = jnp.full((blocks,), core)
    table = [y * blocks + local, jnp.array(LEFT_PLACE), jnp.array(RIGHT_PLACE), local, cores]
    return jnp.stack(table).astype(jnp.int32)


def gradients(table, units_all, energy, pieces, student_protos, scale, shares):
    tiles, share, _ = energy.shape
    tokens = units_all.shape[0]
    block = 256
    blocks = share // block
    whole = lambda *shape: pl.BlockSpec(shape, lambda i, p: (0,) * len(shape))
    first = pl.BlockSpec((block, D), lambda i, p: (p[0, 2 * i], 0))
    second = pl.BlockSpec((block, D), lambda i, p: (p[0, 2 * i + 1], 0))
    direct = pl.BlockSpec(memory_space=pltpu.VMEM)
    half = pltpu.HBM((blocks // 2, block, D // 2), f32)
    return pl.pallas_call(
        gradient_body,
        grid_spec=pltpu.PrefetchScalarGridSpec(
            num_scalar_prefetch=1,
            grid=(blocks // 2,),
            in_specs=[
                direct,
                direct,
                whole(*pieces.shape),
                first,
                second,
                whole(*scale.shape),
            ],
            out_specs=[pl.BlockSpec(memory_space=pl.ANY)] * 4 + [direct] * 2,
            scratch_shapes=[
                pltpu.VMEM((1, tokens), f32),
                pltpu.VMEM((1, tokens), f32),
                pltpu.VMEM((2 * block, D), f32),
                pltpu.VMEM((tokens, D), f32),
                pltpu.VMEM((2, blocks, block, D // 2), f32),
                pltpu.SemaphoreType.DMA((2, blocks)),
            ],
        ),
        out_shape=[half] * 4 + [pltpu.VMEM((shares // 2, tokens // shares, D), f32)] * 2,
        compiler_params=params(24),
        cost_estimate=work(8 * tokens * share * D, 8 * 2**20, tokens * share),
        name="gradients",
    )(
        table,
        units_all,
        energy,
        pieces,
        in_hbm(student_protos),
        in_hbm(student_protos),
        scale,
    )


def project(total, unit, length):
    return (total - unit * jnp.sum(unit * total, axis=-1, keepdims=True)) / length


def student_end_body(place_ref, pieces_ref, unit_ref, length_ref, out_ref):
    result = project(jnp.sum(pieces_ref[...], axis=0), unit_ref[...], length_ref[...])
    for copy in range(out_ref.shape[0]):
        out_ref[copy] = result


def student_end(place, pieces, units, length, copies):
    _, rows, _ = pieces.shape
    return pl.pallas_call(
        student_end_body,
        grid_spec=pltpu.PrefetchScalarGridSpec(
            num_scalar_prefetch=1,
            grid=(1,),
            in_specs=[
                pl.BlockSpec(memory_space=pltpu.VMEM),
                pl.BlockSpec((rows, D), lambda i, p: (p[2], 1)),
                pl.BlockSpec((rows, 1), lambda i, p: (p[2], 0)),
            ],
            out_specs=pl.BlockSpec((copies, rows, D), lambda i, p: (0, 0, 0)),
        ),
        out_shape=jax.ShapeDtypeStruct((copies, rows, D), f32),
        compiler_params=params(8),
        name="student_end",
    )(place, pieces, in_hbm(units), in_hbm(length))


def proto_end_body(place_ref, *refs):
    piece_refs, (protos_ref, out_ref) = refs[:-2], refs[-2:]
    unit, length = unit_rows(protos_ref[...].astype(f32))
    half = len(piece_refs) // 2
    sums = []
    for group in (piece_refs[:half], piece_refs[half:]):
        total = group[0][...]
        for ref in group[1:]:
            total = total + (ref[0] if len(ref.shape) == 3 else ref[...])
        sums.append(total)
    out_ref[...] = project(jnp.concatenate(sums, axis=1), unit, length)


def proto_end(place, pieces, protos):
    rows, width = pieces[0].shape
    return pl.pallas_call(
        proto_end_body,
        grid_spec=pltpu.PrefetchScalarGridSpec(
            num_scalar_prefetch=1,
            grid=(1,),
            in_specs=[pl.BlockSpec(memory_space=pltpu.VMEM)] * len(pieces)
            + [pl.BlockSpec((rows, D), lambda i, p: (p[1], 0))],
            out_specs=pl.BlockSpec((rows, D), lambda i, p: (0, 0)),
        ),
        out_shape=jax.ShapeDtypeStruct((rows, D), f32),
        compiler_params=params(8),
        name="proto_end",
    )(place, *pieces, in_hbm(protos))


def on_device(teacher_patches, student_patches, mask_order, teacher_protos, student_protos):
    y_size, z_size = lax.axis_size("y"), lax.axis_size("z")
    proto_size = lax.axis_size("x") * lax.axis_size("core")
    y, z = lax.axis_index("y"), lax.axis_index("z")
    others = [(y - step + y_size) % y_size for step in range(y_size)]
    core = lax.axis_index("core")
    place = [y, y * z_size + z, lax.axis_index(PROTOS), core] + others
    place = jnp.stack(place).astype(jnp.int32)
    table = block_table(y, z, core)
    share = teacher_protos.shape[0] // y_size

    units, student_length, top, bottom = select_tokens(
        core.astype(jnp.int32)[None], teacher_patches, student_patches, mask_order
    )
    from_y = lambda value, step: lax.ppermute(
        value, "y", [(i, (i + step) % y_size) for i in range(y_size)]
    )
    from_core = lambda value: lax.ppermute(value, "core", [(0, 1), (1, 0)])
    first_top, third_bottom = from_y(top, 1), from_y(bottom, 3)
    first_bottom, third_top = from_y(bottom, 1), from_y(top, 3)
    units, first_top, third_bottom = lax.optimization_barrier((units, first_top, third_bottom))
    second_top, second_bottom = from_y(first_top, 1), from_y(third_bottom, 3)
    norm_part = student_sums(units, student_protos)
    got = [first_top, first_bottom, third_top, third_bottom, second_top, second_bottom]
    norm_part, got, place, table = lax.optimization_barrier((norm_part, got, place, table))
    got = got + [from_core(piece) for piece in got]

    energy, sums, units_all = energy_of(place, units, got, teacher_protos, share, z_size)
    peers = y_size * lax.axis_size("x")
    for sweep in range(ITERS):
        if sweep > 0:
            sums = column_sums(energy, pieces, z_size)
        norms = (norm_part,) if sweep == ITERS - 1 else ()
        col_scale, row_part = row_sums(energy, spread(sums, "z"), 1, norms)
        row_part = row_part + from_core(row_part)
        pieces = spread(jnp.broadcast_to(row_part, (peers,) + row_part.shape[1:]), ("y", "x"))
    pieces = pieces.reshape((y_size, peers // y_size) + pieces.shape[1:])

    send_left, send_right, keep_left, keep_right, feature_send, feature_keep = gradients(
        table, units_all, energy, pieces, student_protos, col_scale, y_size * proto_size
    )
    feature_part = feature_keep + from_core(feature_send)
    feature_part, keep_left, keep_right = lax.optimization_barrier(
        (feature_part, keep_left, keep_right)
    )
    left, right_half = collect(send_left, keep_left, 0), collect(send_right, keep_right, 1)
    feature_pieces = spread(feature_part, ("y", "x"))
    feature_pieces, _, _ = lax.optimization_barrier((feature_pieces, left, right_half))
    result = student_end(place, feature_pieces, units, student_length, proto_size)
    left, right_half = pass_on(left, 0, result), pass_on(right_half, 1, result)
    left, right_half = deliver(left, 0), deliver(right_half, 1)
    result = spread(result, PROTOS)
    grad_protos = proto_end(place, left + right_half, student_protos)
    return (result.reshape(-1, MASKED, D), grad_protos)


def solution(mesh):
    fine = Mesh(mesh.devices.reshape(4, 8, 4, 2), ("y", "z", "x", "core"))
    return jax.shard_map(
        on_device,
        mesh=fine,
        in_specs=(
            P(ROWS, None, None),
            P(ROWS, None, None),
            P(ROWS, None),
            P(PROTOS, None),
            P(PROTOS, None),
        ),
        out_specs=(P(ROWS, None, None), P(PROTOS + ROWS, None)),
        check_vma=False,
    )
```

```python
import math

import jax
import jax.numpy as jnp
from jax import lax
from jax.experimental import pallas as pl
from jax.experimental.pallas import tpu as pltpu
from jax.sharding import Mesh, PartitionSpec as P

D = 256
MASKED = 128
ITERS = 3
LANES = 128

teacher_temp = 0.07
student_temp = 0.1
epsilon = 1e-06

teacher_power = math.log2(math.e) / teacher_temp
student_power = math.log2(math.e) / student_temp

ROWS = ("y", "z")
PROTOS = ("x", "core")

f32 = jnp.float32
bf16 = jnp.bfloat16


def params(mib):
    return pltpu.CompilerParams(vmem_limit_bytes=mib * 2**20)


def spread(value, axes):
    return lax.all_to_all(value, axes, 0, 0, tiled=True)


def work(flops, moved, powers=0):
    return pl.CostEstimate(flops=int(flops), bytes_accessed=int(moved), transcendentals=int(powers))


def in_hbm(value):
    return pltpu.with_memory_space_constraint(value, pltpu.HBM)


def nt_dot(a, b):
    return lax.dot_general(a, b, (((1,), (1,)), ((), ())), preferred_element_type=f32)


def unit_rows(values):
    length = jnp.sqrt(jnp.sum(values * values, axis=-1, keepdims=True) + epsilon)
    return (values / length, length)


def directions(values):
    values = values.astype(f32)
    return (values * lax.rsqrt(jnp.sum(values * values, axis=-1, keepdims=True) + epsilon)).astype(bf16)


def to_column(row):
    return jnp.broadcast_to(row, (LANES, LANES)).T


def fill_columns(rows, tile_ref):
    for k in range(rows.shape[0]):
        tile_ref[k * LANES : (k + 1) * LANES, :] = to_column(rows[k : k + 1, :])


def lane_totals(tile):
    parts = [
        jnp.sum(tile[k * LANES : (k + 1) * LANES, :].T, axis=0, keepdims=True)
        for k in range(tile.shape[0] // LANES)
    ]
    return jnp.concatenate(parts, axis=0)


def select_body(core_ref, teacher_ref, student_ref, order_ref, units_ref, length_ref, top_ref, bottom_ref):
    images, patches, _ = teacher_ref.shape
    for image in range(images):
        chosen = order_ref[image : image + 1, :MASKED]
        place = lax.broadcasted_iota(jnp.int32, (patches, MASKED), 0)
        onehot = jnp.where(place == chosen, 1.0, 0.0).astype(bf16)

        def pick(ref):
            return lax.dot_general(
                onehot, ref[image], (((0,), (0,)), ((), ())), preferred_element_type=f32
            )

        rows = slice(image * MASKED, (image + 1) * MASKED)
        teacher = unit_rows(pick(teacher_ref))[0]
        student, length_ref[rows, :] = unit_rows(pick(student_ref))
        units_ref[rows, :D] = teacher
        units_ref[rows, D:] = student
        mine = jnp.where(core_ref[0] == 0, teacher, student)
        half = top_ref.shape[0]
        if image * MASKED < half:
            top_ref[rows, :] = mine
        else:
            bottom_ref[image * MASKED - half : (image + 1) * MASKED - half, :] = mine


def select_tokens(core, teacher_patches, student_patches, mask_order):
    tokens = teacher_patches.shape[0] * MASKED
    return pl.pallas_call(
        select_body,
        in_specs=[pl.BlockSpec(memory_space=pltpu.SMEM)]
        + [pl.BlockSpec(memory_space=pltpu.VMEM)] * 3,
        out_specs=[pl.BlockSpec(memory_space=pltpu.VMEM)] * 4,
        out_shape=[
            pltpu.HBM((tokens, 2 * D), f32),
            pltpu.HBM((tokens, 1), f32),
            pltpu.HBM((tokens // 2, D), f32),
            pltpu.HBM((tokens // 2, D), f32),
        ],
        compiler_params=params(8),
        name="select",
    )(core, in_hbm(teacher_patches), in_hbm(student_patches), in_hbm(mask_order))


def lane_rows(row):
    parts = [row[:, j * LANES : (j + 1) * LANES] for j in range(row.shape[1] // LANES)]
    return jnp.concatenate(parts, axis=0)


def chunks(tokens):
    return [slice(c, c + LANES) for c in range(0, tokens, LANES)]


FETCHES = 8
WIDE = 256


def fetch(protos_ref, buffer_ref, sems, i):
    size = buffer_ref.shape[0] // FETCHES
    rows = pl.ds(pl.multiple_of(i * size, size), size)
    return pltpu.make_async_copy(protos_ref.at[rows, :], buffer_ref.at[rows, :], sems.at[i])


def fetch_all(units_ref, column, unit_ref, protos_ref, buffer_ref, sems):
    units = pltpu.make_async_copy(
        units_ref.at[:, pl.ds(column, D)], unit_ref, sems.at[FETCHES]
    )
    units.start()
    for i in range(FETCHES):
        fetch(protos_ref, buffer_ref, sems, i).start()
    units.wait()


def energy_body(
    place_ref, units_ref, *refs
):
    piece_refs, (protos_ref, energy_ref, sums_ref, cast_ref, weights_ref, total_ref) = refs[:12], refs[12:]
    own = units_ref.shape[0]
    tokens = cast_ref.shape[0]

    def rows_of(slot, start, size):
        return pl.ds(pl.multiple_of(place_ref[4 + slot] * own + start, size), size)

    cast_ref[rows_of(0, 0, own), :] = units_ref[...].astype(bf16)
    places = [(slot, start, own // 2) for slot in (1, 3, 2) for start in (0, own // 2)]
    for core in range(2):

        @pl.when(place_ref[3] == core)
        def _(core=core):
            for i, ref in enumerate(piece_refs):
                kind = core if i < len(places) else 1 - core
                rows = rows_of(*places[i % len(places)])
                cast_ref[rows, kind * D : (kind + 1) * D] = ref[...].astype(bf16)

    weights_ref[...] = directions(protos_ref[...])
    total_ref[...] = jnp.zeros_like(total_ref)
    size = 512
    parts = [slice(c, c + size) for c in range(0, weights_ref.shape[0], size)]

    def step(i, carry):
        chunk = cast_ref[pl.ds(pl.multiple_of(i * size, size), size), :][:, :D]
        logits = nt_dot(weights_ref[parts[0], :], chunk)
        for k, part in enumerate(parts):
            following = nt_dot(weights_ref[parts[k + 1], :], chunk) if k + 1 < len(parts) else None
            energy = jnp.exp2(logits * teacher_power)
            total = total_ref[part, :]
            for j in range(size // LANES):
                tile = energy[:, j * LANES : (j + 1) * LANES]
                energy_ref[i * (size // LANES) + j, part, :] = tile.astype(bf16)
                total = total + tile
            total_ref[part, :] = total
            logits = following
        return carry

    lax.fori_loop(0, tokens // size, step, 0)
    totals = lane_totals(total_ref[...])
    for copy in range(sums_ref.shape[0]):
        sums_ref[copy] = totals


def fixed(*shape):
    return pl.BlockSpec(shape, lambda i: (0,) * len(shape))


def left(tokens):
    return pl.BlockSpec((tokens, D), lambda *i: (0, 0))


def right(tokens):
    return pl.BlockSpec((tokens, D), lambda *i: (0, 1))


def energy_of(place, units, pieces, protos, share, copies):
    own = units.shape[0]
    tokens = own * 4
    direct = pl.BlockSpec(memory_space=pltpu.VMEM)
    return pl.pallas_call(
        energy_body,
        grid_spec=pltpu.PrefetchScalarGridSpec(
            num_scalar_prefetch=1,
            grid=(1,),
            in_specs=[pl.BlockSpec(units.shape, lambda i, p: (0, 0))]
            + [direct] * len(pieces)
            + [pl.BlockSpec((share, D), lambda i, p: (p[0], 0))],
            out_specs=[
                direct,
                pl.BlockSpec((copies, share // LANES, LANES), lambda i, p: (0, 0, 0)),
                direct,
            ],
            scratch_shapes=[pltpu.VMEM((share, D), bf16), pltpu.VMEM((share, LANES), f32)],
        ),
        out_shape=[
            pltpu.VMEM((tokens // LANES, share, LANES), bf16),
            jax.ShapeDtypeStruct((copies, share // LANES, LANES), f32),
            pltpu.VMEM((tokens, 2 * D), bf16),
        ],
        compiler_params=params(24),
        cost_estimate=work(4 * tokens * share * D, 8 * 2**20, tokens * share),
        name="energy",
    )(place, in_hbm(units), *pieces, in_hbm(protos))


def student_body(units_ref, protos_ref, sums_ref, unit_ref, cast_ref, total_ref, buffer_ref, sems):
    size = buffer_ref.shape[0] // FETCHES
    fetch_all(units_ref, D, unit_ref, protos_ref, buffer_ref, sems)
    cast_ref[...] = unit_ref[...].astype(bf16)
    total_ref[...] = jnp.zeros_like(total_ref)

    def step(i, carry):
        fetch(protos_ref, buffer_ref, sems, i).wait()
        total = total_ref[...]

        def logits_of(part):
            rows = pl.ds(pl.multiple_of(i * size + part * WIDE, WIDE), WIDE)
            return nt_dot(cast_ref[...], directions(buffer_ref[rows, :]))

        parts = size // WIDE
        logits = logits_of(0)
        for part in range(parts):
            following = logits_of(part + 1) if part + 1 < parts else None
            values = jnp.exp2(logits * student_power)
            logits = following
            for j in range(WIDE // LANES):
                total = total + values[:, j * LANES : (j + 1) * LANES]
        total_ref[...] = total
        return carry

    lax.fori_loop(0, FETCHES, step, 0)
    sums_ref[...] = lane_totals(total_ref[...])


def student_sums(units, protos):
    tokens, count = units.shape[0], protos.shape[0]
    return pl.pallas_call(
        student_body,
        in_specs=[pl.BlockSpec(memory_space=pl.ANY)] * 2,
        out_specs=pl.BlockSpec(memory_space=pltpu.VMEM),
        out_shape=jax.ShapeDtypeStruct((tokens // LANES, LANES), f32),
        scratch_shapes=[
            pltpu.VMEM((tokens, D), f32),
            pltpu.VMEM((tokens, D), bf16),
            pltpu.VMEM((tokens, LANES), f32),
            pltpu.VMEM((count, D), bf16),
            pltpu.SemaphoreType.DMA((FETCHES + 1,)),
        ],
        compiler_params=params(16),
        cost_estimate=work(4 * tokens * count * D, 8 * 2**20, tokens * count),
        name="student",
    )(in_hbm(units), in_hbm(protos))


def right(tokens):
    return pl.BlockSpec((tokens, D), lambda *i: (0, 1))


def row_body(energy_ref, pieces_ref, *refs):
    norm_refs, (scale_ref, sums_ref, tile_ref) = refs[:-3], refs[-3:]
    scale_ref[...] = 1.0 / jnp.sum(pieces_ref[...], axis=0)
    fill_columns(scale_ref[...], tile_ref)
    tiles, protos, _ = energy_ref.shape
    size = 512
    totals = []
    for j in range(tiles):
        total = jnp.zeros((1, LANES), f32)
        for start in range(0, protos, size):
            part = slice(start, start + size)
            energy = energy_ref[j, part, :].astype(f32)
            total = total + jnp.sum(energy * tile_ref[part, :], axis=0, keepdims=True)
        totals.append(total)
    for ref in norm_refs:
        totals += [ref[...], jnp.zeros_like(ref)]
    totals = jnp.concatenate(totals, axis=0)
    for copy in range(sums_ref.shape[0]):
        sums_ref[copy] = totals


def row_sums(energy, pieces, copies, norm_part=()):
    tiles, protos, _ = energy.shape
    whole = pl.BlockSpec(memory_space=pltpu.VMEM)
    rows = tiles + 2 * sum(part.shape[0] for part in norm_part)
    return pl.pallas_call(
        row_body,
        in_specs=[whole] * (2 + len(norm_part)),
        out_specs=[whole] * 2,
        out_shape=[
            jax.ShapeDtypeStruct((protos // LANES, LANES), f32),
            jax.ShapeDtypeStruct((copies, rows, LANES), f32),
        ],
        scratch_shapes=[pltpu.VMEM((protos, LANES), f32)],
        compiler_params=params(12),
        cost_estimate=work(2 * energy.size, 0),
        name="row_sums",
    )(energy, pieces, *norm_part)


def column_body(energy_ref, pieces_ref, sums_ref, scale_ref):
    tiles, protos, _ = energy_ref.shape
    scale_ref[...] = 1.0 / jnp.sum(pieces_ref[...], axis=0)

    def step(k, carry):
        rows = pl.ds(pl.multiple_of(k * LANES, LANES), LANES)
        total = jnp.zeros((LANES, LANES), f32)
        for j in range(tiles):
            total = total + energy_ref[j, rows, :].astype(f32) * scale_ref[j : j + 1, :]
        sums_ref[0, pl.ds(k, 1), :] = lane_totals(total)
        return carry

    lax.fori_loop(0, protos // LANES, step, 0, unroll=4)
    for copy in range(1, sums_ref.shape[0]):
        sums_ref[copy] = sums_ref[0]


def column_sums(energy, pieces, copies):
    tiles, protos, _ = energy.shape
    whole = pl.BlockSpec(memory_space=pltpu.VMEM)
    return pl.pallas_call(
        column_body,
        in_specs=[whole] * 2,
        out_specs=whole,
        out_shape=jax.ShapeDtypeStruct((copies, protos // LANES, LANES), f32),
        scratch_shapes=[pltpu.VMEM((tiles, LANES), f32)],
        compiler_params=params(12),
        cost_estimate=work(2 * energy.size, 0),
        name="column_sums",
    )(energy, pieces)


LEFT_PLACE = [4, 5, 6, 7, 3, 2, 1, 0]
RIGHT_PLACE = [4, 0, 1, 2, 3, 7, 6, 5]


def collect(send, keep, offset):
    n = lax.axis_size("z")
    way = [1 if (z + offset) % 2 else -1 for z in range(n)]
    got = lax.ppermute(send, "z", [(z, (z - way[z]) % n) for z in range(n)])
    return keep[0] + got[0], keep[1] + got[1], keep[2:] + got[2:]


def pass_on(sums, offset, after):
    n = lax.axis_size("z")
    way = [1 if (z + offset) % 2 else -1 for z in range(n)]
    own, following, far = sums
    got = lax.ppermute(far, "z", [(z, (z + 2 * way[z]) % n) for z in range(n)])
    following, _ = lax.optimization_barrier((following, after))
    return [own, got], following + got[1]


def deliver(sums, offset):
    n = lax.axis_size("z")
    way = [1 if (z + offset) % 2 else -1 for z in range(n)]
    own, following = sums
    return own + [lax.ppermute(following, "z", [(z, (z + way[z]) % n) for z in range(n)])]


def gradient_body(
    table_ref,
    units_ref,
    energy_ref,
    pieces_ref,
    sw_first_ref,
    sw_second_ref,
    scale_ref,
    send_left_ref,
    send_right_ref,
    keep_left_ref,
    keep_right_ref,
    feature_send_ref,
    feature_keep_ref,
    r_ref,
    n_ref,
    total_ref,
    feature_ref,
    stage_ref,
    sems,
):
    step = pl.program_id(0)
    tiles = energy_ref.shape[0]
    groups = pieces_ref.shape[0]
    own = tiles // groups

    @pl.when(step == 0)
    def _():
        scale = (1.0 / student_temp) / jnp.sum(pieces_ref[:, :, :tiles, :], axis=(0, 1))
        for k in range(tiles):
            r_ref[:, k * LANES : (k + 1) * LANES] = scale[k : k + 1, :]
        for group in range(groups):
            total = jnp.sum(pieces_ref[group, :, tiles : tiles + own, :], axis=0)
            inverse = (1.0 / student_temp) / total
            for k in range(own):
                lanes = slice((group * own + k) * LANES, (group * own + k + 1) * LANES)
                n_ref[:, lanes] = inverse[k : k + 1, :]
        feature_ref[...] = jnp.zeros_like(feature_ref)

    both = lambda first, second: jnp.concatenate([first, second], axis=0)
    block = sw_first_ref.shape[0]
    sw = both(directions(sw_first_ref[...]), directions(sw_second_ref[...]))
    local = [table_ref[3, 2 * step], table_ref[3, 2 * step + 1]]
    here = [pl.ds(pl.multiple_of(place * block, block), block) for place in local]
    columns = []
    for place in local:
        for k in range(block // LANES):
            row = scale_ref[pl.ds(place * (block // LANES) + k, 1), :]
            columns.append(to_column(row))
    col_scale = jnp.concatenate(columns, axis=0)

    def logits_of(part):
        return nt_dot(sw, units_ref[part, D:])

    parts = [slice(c, c + WIDE) for c in range(0, units_ref.shape[0], WIDE)]

    logits = logits_of(parts[0])
    for i, part in enumerate(parts):
        following = logits_of(parts[i + 1]) if i + 1 < len(parts) else None
        grads = []
        for j in range(WIDE // LANES):
            tile = i * (WIDE // LANES) + j
            lanes = slice(tile * LANES, (tile + 1) * LANES)
            energy = both(energy_ref[tile, here[0], :], energy_ref[tile, here[1], :]).astype(f32)
            probs = jnp.exp2(logits[:, j * LANES : (j + 1) * LANES] * student_power) * n_ref[:, lanes]
            grads.append((probs - energy * r_ref[:, lanes] * col_scale).astype(bf16))
        logit_grad = jnp.concatenate(grads, axis=1)
        if i % 2 == 0:
            before = logit_grad
        else:
            pair = jnp.concatenate([before, logit_grad], axis=1)
            rows = slice(part.start - WIDE, part.stop)
            added = jnp.dot(pair, units_ref[rows, D:], preferred_element_type=f32)
            total_ref[...] = added if i == 1 else total_ref[...] + added
        feature_ref[part, :] += lax.dot_general(
            logit_grad, sw, (((0,), (0,)), ((), ())), preferred_element_type=f32
        )
        logits = following

    def copies(which, at):
        found = []
        for half, (sent_ref, kept_ref) in enumerate(
            ((send_left_ref, keep_left_ref), (send_right_ref, keep_right_ref))
        ):
            block_at = 2 * at + which
            place = table_ref[1 + half, block_at]
            source, sem = stage_ref.at[half, block_at], sems.at[half, block_at]
            sent = pltpu.make_async_copy(source, sent_ref.at[jnp.minimum(place, 3)], sem)
            kept = pltpu.make_async_copy(source, kept_ref.at[jnp.maximum(place - 4, 0)], sem)
            found += [(place < 4, sent), (place >= 4, kept)]
        return found

    for which in range(2):
        rows_here = slice(which * block, (which + 1) * block)
        for half in range(2):
            columns_here = slice(half * (D // 2), (half + 1) * (D // 2))
            stage_ref[half, 2 * step + which] = total_ref[rows_here, columns_here]
        for wanted, copy in copies(which, step):
            pl.when(wanted)(copy.start)

    @pl.when(step == pl.num_programs(0) - 1)
    def _():
        size = feature_send_ref.shape[1]
        for core in range(2):

            @pl.when(table_ref[4, 0] == core)
            def _(core=core):
                for at in range(feature_ref.shape[0] // size):
                    out_ref = feature_keep_ref if at % 2 == core else feature_send_ref
                    out_ref[at // 2] = feature_ref[at * size : (at + 1) * size, :]

        for at in range(stage_ref.shape[1] // 2):
            for which in range(2):
                for wanted, copy in copies(which, at):
                    pl.when(wanted)(copy.wait)


def block_table(y, z, core):
    blocks = len(LEFT_PLACE)
    way = jnp.where(z % 2 == 1, 1, -1)
    local = (z + way * jnp.arange(blocks) + blocks) % blocks
    cores = jnp.full((blocks,), core)
    table = [y * blocks + local, jnp.array(LEFT_PLACE), jnp.array(RIGHT_PLACE), local, cores]
    return jnp.stack(table).astype(jnp.int32)


def gradients(table, units_all, energy, pieces, student_protos, scale, shares):
    tiles, share, _ = energy.shape
    tokens = units_all.shape[0]
    block = 256
    blocks = share // block
    whole = lambda *shape: pl.BlockSpec(shape, lambda i, p: (0,) * len(shape))
    first = pl.BlockSpec((block, D), lambda i, p: (p[0, 2 * i], 0))
    second = pl.BlockSpec((block, D), lambda i, p: (p[0, 2 * i + 1], 0))
    direct = pl.BlockSpec(memory_space=pltpu.VMEM)
    half = pltpu.HBM((blocks // 2, block, D // 2), f32)
    return pl.pallas_call(
        gradient_body,
        grid_spec=pltpu.PrefetchScalarGridSpec(
            num_scalar_prefetch=1,
            grid=(blocks // 2,),
            in_specs=[
                direct,
                direct,
                whole(*pieces.shape),
                first,
                second,
                whole(*scale.shape),
            ],
            out_specs=[pl.BlockSpec(memory_space=pl.ANY)] * 4 + [direct] * 2,
            scratch_shapes=[
                pltpu.VMEM((1, tokens), f32),
                pltpu.VMEM((1, tokens), f32),
                pltpu.VMEM((2 * block, D), f32),
                pltpu.VMEM((tokens, D), f32),
                pltpu.VMEM((2, blocks, block, D // 2), f32),
                pltpu.SemaphoreType.DMA((2, blocks)),
            ],
        ),
        out_shape=[half] * 4 + [pltpu.VMEM((shares // 2, tokens // shares, D), f32)] * 2,
        compiler_params=params(24),
        cost_estimate=work(8 * tokens * share * D, 8 * 2**20, tokens * share),
        name="gradients",
    )(
        table,
        units_all,
        energy,
        pieces,
        in_hbm(student_protos),
        in_hbm(student_protos),
        scale,
    )


def project(total, unit, length):
    return (total - unit * jnp.sum(unit * total, axis=-1, keepdims=True)) / length


def student_end_body(place_ref, pieces_ref, unit_ref, length_ref, out_ref):
    result = project(jnp.sum(pieces_ref[...], axis=0), unit_ref[...], length_ref[...])
    for copy in range(out_ref.shape[0]):
        out_ref[copy] = result


def student_end(place, pieces, units, length, copies):
    _, rows, _ = pieces.shape
    return pl.pallas_call(
        student_end_body,
        grid_spec=pltpu.PrefetchScalarGridSpec(
            num_scalar_prefetch=1,
            grid=(1,),
            in_specs=[
                pl.BlockSpec(memory_space=pltpu.VMEM),
                pl.BlockSpec((rows, D), lambda i, p: (p[2], 1)),
                pl.BlockSpec((rows, 1), lambda i, p: (p[2], 0)),
            ],
            out_specs=pl.BlockSpec((copies, rows, D), lambda i, p: (0, 0, 0)),
        ),
        out_shape=jax.ShapeDtypeStruct((copies, rows, D), f32),
        compiler_params=params(8),
        name="student_end",
    )(place, pieces, in_hbm(units), in_hbm(length))


def proto_end_body(place_ref, *refs):
    piece_refs, (protos_ref, out_ref) = refs[:-2], refs[-2:]
    unit, length = unit_rows(protos_ref[...].astype(f32))
    half = len(piece_refs) // 2
    sums = []
    for group in (piece_refs[:half], piece_refs[half:]):
        total = group[0][...]
        for ref in group[1:]:
            total = total + (ref[0] if len(ref.shape) == 3 else ref[...])
        sums.append(total)
    out_ref[...] = project(jnp.concatenate(sums, axis=1), unit, length)


def proto_end(place, pieces, protos):
    rows, width = pieces[0].shape
    return pl.pallas_call(
        proto_end_body,
        grid_spec=pltpu.PrefetchScalarGridSpec(
            num_scalar_prefetch=1,
            grid=(1,),
            in_specs=[pl.BlockSpec(memory_space=pltpu.VMEM)] * len(pieces)
            + [pl.BlockSpec((rows, D), lambda i, p: (p[1], 0))],
            out_specs=pl.BlockSpec((rows, D), lambda i, p: (0, 0)),
        ),
        out_shape=jax.ShapeDtypeStruct((rows, D), f32),
        compiler_params=params(8),
        name="proto_end",
    )(place, *pieces, in_hbm(protos))


def on_device(teacher_patches, student_patches, mask_order, teacher_protos, student_protos):
    y_size, z_size = lax.axis_size("y"), lax.axis_size("z")
    proto_size = lax.axis_size("x") * lax.axis_size("core")
    y, z = lax.axis_index("y"), lax.axis_index("z")
    others = [(y - step + y_size) % y_size for step in range(y_size)]
    core = lax.axis_index("core")
    place = [y, y * z_size + z, lax.axis_index(PROTOS), core] + others
    place = jnp.stack(place).astype(jnp.int32)
    table = block_table(y, z, core)
    share = teacher_protos.shape[0] // y_size

    units, student_length, top, bottom = select_tokens(
        core.astype(jnp.int32)[None], teacher_patches, student_patches, mask_order
    )
    from_y = lambda value, step: lax.ppermute(
        value, "y", [(i, (i + step) % y_size) for i in range(y_size)]
    )
    from_core = lambda value: lax.ppermute(value, "core", [(0, 1), (1, 0)])
    first_top, third_bottom = from_y(top, 1), from_y(bottom, 3)
    first_bottom, third_top = from_y(bottom, 1), from_y(top, 3)
    units, first_top, third_bottom = lax.optimization_barrier((units, first_top, third_bottom))
    second_top, second_bottom = from_y(first_top, 1), from_y(third_bottom, 3)
    norm_part = student_sums(units, student_protos)
    got = [first_top, first_bottom, third_top, third_bottom, second_top, second_bottom]
    norm_part, got, place, table = lax.optimization_barrier((norm_part, got, place, table))
    got = got + [from_core(piece) for piece in got]

    energy, sums, units_all = energy_of(place, units, got, teacher_protos, share, z_size)
    peers = y_size * lax.axis_size("x")
    for sweep in range(ITERS):
        if sweep > 0:
            sums = column_sums(energy, pieces, z_size)
        norms = (norm_part,) if sweep == ITERS - 1 else ()
        col_scale, row_part = row_sums(energy, spread(sums, "z"), 1, norms)
        row_part = row_part + from_core(row_part)
        pieces = spread(jnp.broadcast_to(row_part, (peers,) + row_part.shape[1:]), ("y", "x"))
    pieces = pieces.reshape((y_size, peers // y_size) + pieces.shape[1:])

    send_left, send_right, keep_left, keep_right, feature_send, feature_keep = gradients(
        table, units_all, energy, pieces, student_protos, col_scale, y_size * proto_size
    )
    feature_part = feature_keep + from_core(feature_send)
    feature_part, keep_left, keep_right = lax.optimization_barrier(
        (feature_part, keep_left, keep_right)
    )
    left, right_half = collect(send_left, keep_left, 0), collect(send_right, keep_right, 1)
    feature_pieces = spread(feature_part, ("y", "x"))
    feature_pieces, _, _ = lax.optimization_barrier((feature_pieces, left, right_half))
    result = student_end(place, feature_pieces, units, student_length, proto_size)
    left, right_half = pass_on(left, 0, result), pass_on(right_half, 1, result)
    left, right_half = deliver(left, 0), deliver(right_half, 1)
    result = spread(result, PROTOS)
    grad_protos = proto_end(place, left + right_half, student_protos)
    return (result.reshape(-1, MASKED, D), grad_protos)


def solution(mesh):
    fine = Mesh(mesh.devices.reshape(4, 8, 4, 2), ("y", "z", "x", "core"))
    return jax.shard_map(
        on_device,
        mesh=fine,
        in_specs=(
            P(ROWS, None, None),
            P(ROWS, None, None),
            P(ROWS, None),
            P(PROTOS, None),
            P(PROTOS, None),
        ),
        out_specs=(P(ROWS, None, None), P(PROTOS + ROWS, None)),
        check_vma=False,
    )
```

```python
import math

import jax
import jax.numpy as jnp
from jax import lax
from jax.experimental import pallas as pl
from jax.experimental.pallas import tpu as pltpu
from jax.sharding import Mesh, PartitionSpec as P

D = 256
MASKED = 128
ITERS = 3
LANES = 128

teacher_temp = 0.07
student_temp = 0.1
epsilon = 1e-06

teacher_power = math.log2(math.e) / teacher_temp
student_power = math.log2(math.e) / student_temp

ROWS = ("y", "z")
PROTOS = ("x", "core")

f32 = jnp.float32
bf16 = jnp.bfloat16


def params(mib):
    return pltpu.CompilerParams(vmem_limit_bytes=mib * 2**20)


def spread(value, axes):
    return lax.all_to_all(value, axes, 0, 0, tiled=True)


def work(flops, moved, powers=0):
    return pl.CostEstimate(flops=int(flops), bytes_accessed=int(moved), transcendentals=int(powers))


def in_hbm(value):
    return pltpu.with_memory_space_constraint(value, pltpu.HBM)


def nt_dot(a, b):
    return lax.dot_general(a, b, (((1,), (1,)), ((), ())), preferred_element_type=f32)


def unit_rows(values):
    length = jnp.sqrt(jnp.sum(values * values, axis=-1, keepdims=True) + epsilon)
    return (values / length, length)


def directions(values):
    values = values.astype(f32)
    return (values * lax.rsqrt(jnp.sum(values * values, axis=-1, keepdims=True) + epsilon)).astype(bf16)


def to_column(row):
    return jnp.broadcast_to(row, (LANES, LANES)).T


def fill_columns(rows, tile_ref):
    for k in range(rows.shape[0]):
        tile_ref[k * LANES : (k + 1) * LANES, :] = to_column(rows[k : k + 1, :])


def lane_totals(tile):
    parts = [
        jnp.sum(tile[k * LANES : (k + 1) * LANES, :].T, axis=0, keepdims=True)
        for k in range(tile.shape[0] // LANES)
    ]
    return jnp.concatenate(parts, axis=0)


def select_body(core_ref, teacher_ref, student_ref, order_ref, units_ref, length_ref, top_ref, bottom_ref):
    images, patches, _ = teacher_ref.shape
    for image in range(images):
        chosen = order_ref[image : image + 1, :MASKED]
        place = lax.broadcasted_iota(jnp.int32, (patches, MASKED), 0)
        onehot = jnp.where(place == chosen, 1.0, 0.0).astype(bf16)

        def pick(ref):
            return lax.dot_general(
                onehot, ref[image], (((0,), (0,)), ((), ())), preferred_element_type=f32
            )

        rows = slice(image * MASKED, (image + 1) * MASKED)
        teacher = unit_rows(pick(teacher_ref))[0]
        student, length_ref[rows, :] = unit_rows(pick(student_ref))
        units_ref[rows, :D] = teacher
        units_ref[rows, D:] = student
        mine = jnp.where(core_ref[0] == 0, teacher, student)
        half = top_ref.shape[0]
        if image * MASKED < half:
            top_ref[rows, :] = mine
        else:
            bottom_ref[image * MASKED - half : (image + 1) * MASKED - half, :] = mine


def select_tokens(core, teacher_patches, student_patches, mask_order):
    tokens = teacher_patches.shape[0] * MASKED
    return pl.pallas_call(
        select_body,
        in_specs=[pl.BlockSpec(memory_space=pltpu.SMEM)]
        + [pl.BlockSpec(memory_space=pltpu.VMEM)] * 3,
        out_specs=[pl.BlockSpec(memory_space=pltpu.VMEM)] * 4,
        out_shape=[
            pltpu.HBM((tokens, 2 * D), f32),
            pltpu.HBM((tokens, 1), f32),
            pltpu.HBM((tokens // 2, D), f32),
            pltpu.HBM((tokens // 2, D), f32),
        ],
        compiler_params=params(8),
        name="select",
    )(core, in_hbm(teacher_patches), in_hbm(student_patches), in_hbm(mask_order))


def lane_rows(row):
    parts = [row[:, j * LANES : (j + 1) * LANES] for j in range(row.shape[1] // LANES)]
    return jnp.concatenate(parts, axis=0)


def chunks(tokens):
    return [slice(c, c + LANES) for c in range(0, tokens, LANES)]


FETCHES = 8
WIDE = 256


def fetch(protos_ref, buffer_ref, sems, i):
    size = buffer_ref.shape[0] // FETCHES
    rows = pl.ds(pl.multiple_of(i * size, size), size)
    return pltpu.make_async_copy(protos_ref.at[rows, :], buffer_ref.at[rows, :], sems.at[i])


def fetch_all(units_ref, column, unit_ref, protos_ref, buffer_ref, sems):
    units = pltpu.make_async_copy(
        units_ref.at[:, pl.ds(column, D)], unit_ref, sems.at[FETCHES]
    )
    units.start()
    for i in range(FETCHES):
        fetch(protos_ref, buffer_ref, sems, i).start()
    units.wait()


def energy_body(
    place_ref, units_ref, *refs
):
    piece_refs, (protos_ref, energy_ref, sums_ref, cast_ref, weights_ref, total_ref) = refs[:12], refs[12:]
    own = units_ref.shape[0]
    tokens = cast_ref.shape[0]

    def rows_of(slot, start, size):
        return pl.ds(pl.multiple_of(place_ref[4 + slot] * own + start, size), size)

    cast_ref[rows_of(0, 0, own), :] = units_ref[...].astype(bf16)
    places = [(slot, start, own // 2) for slot in (1, 3, 2) for start in (0, own // 2)]
    for core in range(2):

        @pl.when(place_ref[3] == core)
        def _(core=core):
            for i, ref in enumerate(piece_refs):
                kind = core if i < len(places) else 1 - core
                rows = rows_of(*places[i % len(places)])
                cast_ref[rows, kind * D : (kind + 1) * D] = ref[...].astype(bf16)

    weights_ref[...] = directions(protos_ref[...])
    total_ref[...] = jnp.zeros_like(total_ref)
    size = 512
    parts = [slice(c, c + size) for c in range(0, weights_ref.shape[0], size)]

    def step(i, carry):
        chunk = cast_ref[pl.ds(pl.multiple_of(i * size, size), size), :][:, :D]
        logits = nt_dot(weights_ref[parts[0], :], chunk)
        for k, part in enumerate(parts):
            following = nt_dot(weights_ref[parts[k + 1], :], chunk) if k + 1 < len(parts) else None
            energy = jnp.exp2(logits * teacher_power)
            total = total_ref[part, :]
            for j in range(size // LANES):
                tile = energy[:, j * LANES : (j + 1) * LANES]
                energy_ref[i * (size // LANES) + j, part, :] = tile.astype(bf16)
                total = total + tile
            total_ref[part, :] = total
            logits = following
        return carry

    lax.fori_loop(0, tokens // size, step, 0)
    totals = lane_totals(total_ref[...])
    for copy in range(sums_ref.shape[0]):
        sums_ref[copy] = totals


def fixed(*shape):
    return pl.BlockSpec(shape, lambda i: (0,) * len(shape))


def left(tokens):
    return pl.BlockSpec((tokens, D), lambda *i: (0, 0))


def right(tokens):
    return pl.BlockSpec((tokens, D), lambda *i: (0, 1))


def energy_of(place, units, pieces, protos, share, copies):
    own = units.shape[0]
    tokens = own * 4
    direct = pl.BlockSpec(memory_space=pltpu.VMEM)
    return pl.pallas_call(
        energy_body,
        grid_spec=pltpu.PrefetchScalarGridSpec(
            num_scalar_prefetch=1,
            grid=(1,),
            in_specs=[pl.BlockSpec(units.shape, lambda i, p: (0, 0))]
            + [direct] * len(pieces)
            + [pl.BlockSpec((share, D), lambda i, p: (p[0], 0))],
            out_specs=[
                direct,
                pl.BlockSpec((copies, share // LANES, LANES), lambda i, p: (0, 0, 0)),
                direct,
            ],
            scratch_shapes=[pltpu.VMEM((share, D), bf16), pltpu.VMEM((share, LANES), f32)],
        ),
        out_shape=[
            pltpu.VMEM((tokens // LANES, share, LANES), bf16),
            jax.ShapeDtypeStruct((copies, share // LANES, LANES), f32),
            pltpu.VMEM((tokens, 2 * D), bf16),
        ],
        compiler_params=params(24),
        cost_estimate=work(4 * tokens * share * D, 8 * 2**20, tokens * share),
        name="energy",
    )(place, in_hbm(units), *pieces, in_hbm(protos))


def student_body(units_ref, protos_ref, sums_ref, unit_ref, cast_ref, total_ref, buffer_ref, sems):
    size, wide = buffer_ref.shape[0] // FETCHES, 512
    fetch_all(units_ref, D, unit_ref, protos_ref, buffer_ref, sems)
    cast_ref[...] = unit_ref[...].astype(bf16)
    total_ref[...] = jnp.zeros_like(total_ref)

    def step(i, carry):
        fetch(protos_ref, buffer_ref, sems, i).wait()
        total = total_ref[...]

        def logits_of(part):
            rows = pl.ds(pl.multiple_of(i * size + part * wide, wide), wide)
            return nt_dot(cast_ref[...], directions(buffer_ref[rows, :]))

        parts = size // wide
        logits = logits_of(0)
        for part in range(parts):
            following = logits_of(part + 1) if part + 1 < parts else None
            values = jnp.exp2(logits * student_power)
            logits = following
            for j in range(wide // LANES):
                total = total + values[:, j * LANES : (j + 1) * LANES]
        total_ref[...] = total
        return carry

    lax.fori_loop(0, FETCHES, step, 0)
    sums_ref[...] = lane_totals(total_ref[...])


def student_sums(units, protos):
    tokens, count = units.shape[0], protos.shape[0]
    return pl.pallas_call(
        student_body,
        in_specs=[pl.BlockSpec(memory_space=pl.ANY)] * 2,
        out_specs=pl.BlockSpec(memory_space=pltpu.VMEM),
        out_shape=jax.ShapeDtypeStruct((tokens // LANES, LANES), f32),
        scratch_shapes=[
            pltpu.VMEM((tokens, D), f32),
            pltpu.VMEM((tokens, D), bf16),
            pltpu.VMEM((tokens, LANES), f32),
            pltpu.VMEM((count, D), bf16),
            pltpu.SemaphoreType.DMA((FETCHES + 1,)),
        ],
        compiler_params=params(16),
        cost_estimate=work(4 * tokens * count * D, 8 * 2**20, tokens * count),
        name="student",
    )(in_hbm(units), in_hbm(protos))


def right(tokens):
    return pl.BlockSpec((tokens, D), lambda *i: (0, 1))


def row_body(energy_ref, pieces_ref, *refs):
    norm_refs, (scale_ref, sums_ref, tile_ref) = refs[:-3], refs[-3:]
    scale_ref[...] = 1.0 / jnp.sum(pieces_ref[...], axis=0)
    fill_columns(scale_ref[...], tile_ref)
    tiles, protos, _ = energy_ref.shape
    size = 512
    totals = []
    for j in range(tiles):
        total = jnp.zeros((1, LANES), f32)
        for start in range(0, protos, size):
            part = slice(start, start + size)
            energy = energy_ref[j, part, :].astype(f32)
            total = total + jnp.sum(energy * tile_ref[part, :], axis=0, keepdims=True)
        totals.append(total)
    for ref in norm_refs:
        totals += [ref[...], jnp.zeros_like(ref)]
    totals = jnp.concatenate(totals, axis=0)
    for copy in range(sums_ref.shape[0]):
        sums_ref[copy] = totals


def row_sums(energy, pieces, copies, norm_part=()):
    tiles, protos, _ = energy.shape
    whole = pl.BlockSpec(memory_space=pltpu.VMEM)
    rows = tiles + 2 * sum(part.shape[0] for part in norm_part)
    return pl.pallas_call(
        row_body,
        in_specs=[whole] * (2 + len(norm_part)),
        out_specs=[whole] * 2,
        out_shape=[
            jax.ShapeDtypeStruct((protos // LANES, LANES), f32),
            jax.ShapeDtypeStruct((copies, rows, LANES), f32),
        ],
        scratch_shapes=[pltpu.VMEM((protos, LANES), f32)],
        compiler_params=params(12),
        cost_estimate=work(2 * energy.size, 0),
        name="row_sums",
    )(energy, pieces, *norm_part)


def column_body(energy_ref, pieces_ref, sums_ref, scale_ref):
    tiles, protos, _ = energy_ref.shape
    scale_ref[...] = 1.0 / jnp.sum(pieces_ref[...], axis=0)

    def step(k, carry):
        rows = pl.ds(pl.multiple_of(k * LANES, LANES), LANES)
        total = jnp.zeros((LANES, LANES), f32)
        for j in range(tiles):
            total = total + energy_ref[j, rows, :].astype(f32) * scale_ref[j : j + 1, :]
        sums_ref[0, pl.ds(k, 1), :] = lane_totals(total)
        return carry

    lax.fori_loop(0, protos // LANES, step, 0, unroll=4)
    for copy in range(1, sums_ref.shape[0]):
        sums_ref[copy] = sums_ref[0]


def column_sums(energy, pieces, copies):
    tiles, protos, _ = energy.shape
    whole = pl.BlockSpec(memory_space=pltpu.VMEM)
    return pl.pallas_call(
        column_body,
        in_specs=[whole] * 2,
        out_specs=whole,
        out_shape=jax.ShapeDtypeStruct((copies, protos // LANES, LANES), f32),
        scratch_shapes=[pltpu.VMEM((tiles, LANES), f32)],
        compiler_params=params(12),
        cost_estimate=work(2 * energy.size, 0),
        name="column_sums",
    )(energy, pieces)


LEFT_PLACE = [4, 5, 6, 7, 3, 2, 1, 0]
RIGHT_PLACE = [4, 0, 1, 2, 3, 7, 6, 5]


def collect(send, keep, offset):
    n = lax.axis_size("z")
    way = [1 if (z + offset) % 2 else -1 for z in range(n)]
    got = lax.ppermute(send, "z", [(z, (z - way[z]) % n) for z in range(n)])
    return keep[0] + got[0], keep[1] + got[1], keep[2:] + got[2:]


def pass_on(sums, offset, after):
    n = lax.axis_size("z")
    way = [1 if (z + offset) % 2 else -1 for z in range(n)]
    own, following, far = sums
    got = lax.ppermute(far, "z", [(z, (z + 2 * way[z]) % n) for z in range(n)])
    following, _ = lax.optimization_barrier((following, after))
    return [own, got], following + got[1]


def deliver(sums, offset):
    n = lax.axis_size("z")
    way = [1 if (z + offset) % 2 else -1 for z in range(n)]
    own, following = sums
    return own + [lax.ppermute(following, "z", [(z, (z + way[z]) % n) for z in range(n)])]


def gradient_body(
    table_ref,
    units_ref,
    energy_ref,
    pieces_ref,
    sw_first_ref,
    sw_second_ref,
    scale_ref,
    send_left_ref,
    send_right_ref,
    keep_left_ref,
    keep_right_ref,
    feature_send_ref,
    feature_keep_ref,
    r_ref,
    n_ref,
    total_ref,
    feature_ref,
    stage_ref,
    sems,
):
    step = pl.program_id(0)
    tiles = energy_ref.shape[0]
    groups = pieces_ref.shape[0]
    own = tiles // groups

    @pl.when(step == 0)
    def _():
        scale = (1.0 / student_temp) / jnp.sum(pieces_ref[:, :, :tiles, :], axis=(0, 1))
        for k in range(tiles):
            r_ref[:, k * LANES : (k + 1) * LANES] = scale[k : k + 1, :]
        for group in range(groups):
            total = jnp.sum(pieces_ref[group, :, tiles : tiles + own, :], axis=0)
            inverse = (1.0 / student_temp) / total
            for k in range(own):
                lanes = slice((group * own + k) * LANES, (group * own + k + 1) * LANES)
                n_ref[:, lanes] = inverse[k : k + 1, :]
        feature_ref[...] = jnp.zeros_like(feature_ref)

    both = lambda first, second: jnp.concatenate([first, second], axis=0)
    block = sw_first_ref.shape[0]
    sw = both(directions(sw_first_ref[...]), directions(sw_second_ref[...]))
    local = [table_ref[3, 2 * step], table_ref[3, 2 * step + 1]]
    here = [pl.ds(pl.multiple_of(place * block, block), block) for place in local]
    columns = []
    for place in local:
        for k in range(block // LANES):
            row = scale_ref[pl.ds(place * (block // LANES) + k, 1), :]
            columns.append(to_column(row))
    col_scale = jnp.concatenate(columns, axis=0)

    def logits_of(part):
        return nt_dot(sw, units_ref[part, D:])

    parts = [slice(c, c + WIDE) for c in range(0, units_ref.shape[0], WIDE)]

    logits = logits_of(parts[0])
    for i, part in enumerate(parts):
        following = logits_of(parts[i + 1]) if i + 1 < len(parts) else None
        grads = []
        for j in range(WIDE // LANES):
            tile = i * (WIDE // LANES) + j
            lanes = slice(tile * LANES, (tile + 1) * LANES)
            energy = both(energy_ref[tile, here[0], :], energy_ref[tile, here[1], :]).astype(f32)
            probs = jnp.exp2(logits[:, j * LANES : (j + 1) * LANES] * student_power) * n_ref[:, lanes]
            grads.append((probs - energy * r_ref[:, lanes] * col_scale).astype(bf16))
        logit_grad = jnp.concatenate(grads, axis=1)
        added = jnp.dot(logit_grad, units_ref[part, D:], preferred_element_type=f32)
        total_ref[...] = added if i == 0 else total_ref[...] + added
        feature_ref[part, :] += lax.dot_general(
            logit_grad, sw, (((0,), (0,)), ((), ())), preferred_element_type=f32
        )
        logits = following

    def copies(which, at):
        found = []
        for half, (sent_ref, kept_ref) in enumerate(
            ((send_left_ref, keep_left_ref), (send_right_ref, keep_right_ref))
        ):
            block_at = 2 * at + which
            place = table_ref[1 + half, block_at]
            source, sem = stage_ref.at[half, block_at], sems.at[half, block_at]
            sent = pltpu.make_async_copy(source, sent_ref.at[jnp.minimum(place, 3)], sem)
            kept = pltpu.make_async_copy(source, kept_ref.at[jnp.maximum(place - 4, 0)], sem)
            found += [(place < 4, sent), (place >= 4, kept)]
        return found

    for which in range(2):
        rows_here = slice(which * block, (which + 1) * block)
        for half in range(2):
            columns_here = slice(half * (D // 2), (half + 1) * (D // 2))
            stage_ref[half, 2 * step + which] = total_ref[rows_here, columns_here]
        for wanted, copy in copies(which, step):
            pl.when(wanted)(copy.start)

    @pl.when(step == pl.num_programs(0) - 1)
    def _():
        size = feature_send_ref.shape[1]
        for core in range(2):

            @pl.when(table_ref[4, 0] == core)
            def _(core=core):
                for at in range(feature_ref.shape[0] // size):
                    out_ref = feature_keep_ref if at % 2 == core else feature_send_ref
                    out_ref[at // 2] = feature_ref[at * size : (at + 1) * size, :]

        for at in range(stage_ref.shape[1] // 2):
            for which in range(2):
                for wanted, copy in copies(which, at):
                    pl.when(wanted)(copy.wait)


def block_table(y, z, core):
    blocks = len(LEFT_PLACE)
    way = jnp.where(z % 2 == 1, 1, -1)
    local = (z + way * jnp.arange(blocks) + blocks) % blocks
    cores = jnp.full((blocks,), core)
    table = [y * blocks + local, jnp.array(LEFT_PLACE), jnp.array(RIGHT_PLACE), local, cores]
    return jnp.stack(table).astype(jnp.int32)


def gradients(table, units_all, energy, pieces, student_protos, scale, shares):
    tiles, share, _ = energy.shape
    tokens = units_all.shape[0]
    block = 256
    blocks = share // block
    whole = lambda *shape: pl.BlockSpec(shape, lambda i, p: (0,) * len(shape))
    first = pl.BlockSpec((block, D), lambda i, p: (p[0, 2 * i], 0))
    second = pl.BlockSpec((block, D), lambda i, p: (p[0, 2 * i + 1], 0))
    direct = pl.BlockSpec(memory_space=pltpu.VMEM)
    half = pltpu.HBM((blocks // 2, block, D // 2), f32)
    return pl.pallas_call(
        gradient_body,
        grid_spec=pltpu.PrefetchScalarGridSpec(
            num_scalar_prefetch=1,
            grid=(blocks // 2,),
            in_specs=[
                direct,
                direct,
                whole(*pieces.shape),
                first,
                second,
                whole(*scale.shape),
            ],
            out_specs=[pl.BlockSpec(memory_space=pl.ANY)] * 4 + [direct] * 2,
            scratch_shapes=[
                pltpu.VMEM((1, tokens), f32),
                pltpu.VMEM((1, tokens), f32),
                pltpu.VMEM((2 * block, D), f32),
                pltpu.VMEM((tokens, D), f32),
                pltpu.VMEM((2, blocks, block, D // 2), f32),
                pltpu.SemaphoreType.DMA((2, blocks)),
            ],
        ),
        out_shape=[half] * 4 + [pltpu.VMEM((shares // 2, tokens // shares, D), f32)] * 2,
        compiler_params=params(24),
        cost_estimate=work(8 * tokens * share * D, 8 * 2**20, tokens * share),
        name="gradients",
    )(
        table,
        units_all,
        energy,
        pieces,
        in_hbm(student_protos),
        in_hbm(student_protos),
        scale,
    )


def project(total, unit, length):
    return (total - unit * jnp.sum(unit * total, axis=-1, keepdims=True)) / length


def student_end_body(place_ref, pieces_ref, unit_ref, length_ref, out_ref):
    result = project(jnp.sum(pieces_ref[...], axis=0), unit_ref[...], length_ref[...])
    for copy in range(out_ref.shape[0]):
        out_ref[copy] = result


def student_end(place, pieces, units, length, copies):
    _, rows, _ = pieces.shape
    return pl.pallas_call(
        student_end_body,
        grid_spec=pltpu.PrefetchScalarGridSpec(
            num_scalar_prefetch=1,
            grid=(1,),
            in_specs=[
                pl.BlockSpec(memory_space=pltpu.VMEM),
                pl.BlockSpec((rows, D), lambda i, p: (p[2], 1)),
                pl.BlockSpec((rows, 1), lambda i, p: (p[2], 0)),
            ],
            out_specs=pl.BlockSpec((copies, rows, D), lambda i, p: (0, 0, 0)),
        ),
        out_shape=jax.ShapeDtypeStruct((copies, rows, D), f32),
        compiler_params=params(8),
        name="student_end",
    )(place, pieces, in_hbm(units), in_hbm(length))


def proto_end_body(place_ref, *refs):
    piece_refs, (protos_ref, out_ref) = refs[:-2], refs[-2:]
    unit, length = unit_rows(protos_ref[...].astype(f32))
    half = len(piece_refs) // 2
    sums = []
    for group in (piece_refs[:half], piece_refs[half:]):
        total = group[0][...]
        for ref in group[1:]:
            total = total + (ref[0] if len(ref.shape) == 3 else ref[...])
        sums.append(total)
    out_ref[...] = project(jnp.concatenate(sums, axis=1), unit, length)


def proto_end(place, pieces, protos):
    rows, width = pieces[0].shape
    return pl.pallas_call(
        proto_end_body,
        grid_spec=pltpu.PrefetchScalarGridSpec(
            num_scalar_prefetch=1,
            grid=(1,),
            in_specs=[pl.BlockSpec(memory_space=pltpu.VMEM)] * len(pieces)
            + [pl.BlockSpec((rows, D), lambda i, p: (p[1], 0))],
            out_specs=pl.BlockSpec((rows, D), lambda i, p: (0, 0)),
        ),
        out_shape=jax.ShapeDtypeStruct((rows, D), f32),
        compiler_params=params(8),
        name="proto_end",
    )(place, *pieces, in_hbm(protos))


def on_device(teacher_patches, student_patches, mask_order, teacher_protos, student_protos):
    y_size, z_size = lax.axis_size("y"), lax.axis_size("z")
    proto_size = lax.axis_size("x") * lax.axis_size("core")
    y, z = lax.axis_index("y"), lax.axis_index("z")
    others = [(y - step + y_size) % y_size for step in range(y_size)]
    core = lax.axis_index("core")
    place = [y, y * z_size + z, lax.axis_index(PROTOS), core] + others
    place = jnp.stack(place).astype(jnp.int32)
    table = block_table(y, z, core)
    share = teacher_protos.shape[0] // y_size

    units, student_length, top, bottom = select_tokens(
        core.astype(jnp.int32)[None], teacher_patches, student_patches, mask_order
    )
    from_y = lambda value, step: lax.ppermute(
        value, "y", [(i, (i + step) % y_size) for i in range(y_size)]
    )
    from_core = lambda value: lax.ppermute(value, "core", [(0, 1), (1, 0)])
    first_top, third_bottom = from_y(top, 1), from_y(bottom, 3)
    first_bottom, third_top = from_y(bottom, 1), from_y(top, 3)
    units, first_top, third_bottom = lax.optimization_barrier((units, first_top, third_bottom))
    second_top, second_bottom = from_y(first_top, 1), from_y(third_bottom, 3)
    norm_part = student_sums(units, student_protos)
    got = [first_top, first_bottom, third_top, third_bottom, second_top, second_bottom]
    norm_part, got, place, table = lax.optimization_barrier((norm_part, got, place, table))
    got = got + [from_core(piece) for piece in got]

    energy, sums, units_all = energy_of(place, units, got, teacher_protos, share, z_size)
    peers = y_size * lax.axis_size("x")
    for sweep in range(ITERS):
        if sweep > 0:
            sums = column_sums(energy, pieces, z_size)
        norms = (norm_part,) if sweep == ITERS - 1 else ()
        col_scale, row_part = row_sums(energy, spread(sums, "z"), 1, norms)
        row_part = row_part + from_core(row_part)
        pieces = spread(jnp.broadcast_to(row_part, (peers,) + row_part.shape[1:]), ("y", "x"))
    pieces = pieces.reshape((y_size, peers // y_size) + pieces.shape[1:])

    send_left, send_right, keep_left, keep_right, feature_send, feature_keep = gradients(
        table, units_all, energy, pieces, student_protos, col_scale, y_size * proto_size
    )
    feature_part = feature_keep + from_core(feature_send)
    feature_part, keep_left, keep_right = lax.optimization_barrier(
        (feature_part, keep_left, keep_right)
    )
    left, right_half = collect(send_left, keep_left, 0), collect(send_right, keep_right, 1)
    feature_pieces = spread(feature_part, ("y", "x"))
    feature_pieces, _, _ = lax.optimization_barrier((feature_pieces, left, right_half))
    result = student_end(place, feature_pieces, units, student_length, proto_size)
    left, right_half = pass_on(left, 0, result), pass_on(right_half, 1, result)
    left, right_half = deliver(left, 0), deliver(right_half, 1)
    result = spread(result, PROTOS)
    grad_protos = proto_end(place, left + right_half, student_protos)
    return (result.reshape(-1, MASKED, D), grad_protos)


def solution(mesh):
    fine = Mesh(mesh.devices.reshape(4, 8, 4, 2), ("y", "z", "x", "core"))
    return jax.shard_map(
        on_device,
        mesh=fine,
        in_specs=(
            P(ROWS, None, None),
            P(ROWS, None, None),
            P(ROWS, None),
            P(PROTOS, None),
            P(PROTOS, None),
        ),
        out_specs=(P(ROWS, None, None), P(PROTOS + ROWS, None)),
        check_vma=False,
    )
```
